128 devices in a mesh: dp: 8 (over y, core), seq: 16 (over x, z).
Axes of the slice: x: 4, y: 4, z: 4, core: 2. Of those that a mesh axis runs over, the one named last changes fastest.
Arguments:
- tokens: bfloat16 [8, 4096, 768], P('dp', 'seq'), may hold values from -6 to 6
- starts: int32 [8, 16], P('dp', 'seq'), may hold values from 0 to 1, as said below
- g_in: float32 [768], replicated, may hold values from 0.5 to 1.5
- w_in: bfloat16 [768, 3328], P('dp'), may hold values from -0.21875 to 0.21875
- w_dt: bfloat16 [768, 48], P('dp'), may hold values from -0.21875 to 0.21875
- conv_w: float32 [4, 1792], replicated, may hold values from -3 to 3
- conv_b: float32 [1792], replicated, may hold values from -3 to 3
- dt_bias: float32 [48], replicated, may hold values from -4.5 to -2.5
- a_log: float32 [24], replicated, as said below
- dskip: float32 [24], replicated, may hold values from 0.5 to 1.5
- g_out: float32 [1536], replicated, may hold values from 0.5 to 1.5
- w_out: bfloat16 [1536, 768], P('dp'), may hold values from -0.15625 to 0.15625
- d_out: bfloat16 [8, 4096, 768], P('dp', 'seq'), may hold values from -6 to 6
Outputs:
- out: bfloat16 [8, 4096, 768], P('dp', 'seq')
- d_tokens: float32 [8, 4096, 768], P('dp', 'seq')
- d_g_in: float32 [768], replicated
- d_w_in: float32 [768, 3328], P('dp')
- d_w_dt: float32 [768, 48], P('dp')
- d_conv_w: float32 [4, 1792], replicated
- d_conv_b: float32 [1792], replicated
- d_dt_bias: float32 [48], replicated
- d_a_log: float32 [24], replicated
- d_dskip: float32 [24], replicated
- d_g_out: float32 [1536], replicated
- d_w_out: float32 [1536, 768], P('dp')
The draws below stay inside these ranges and needn't reach their ends.
Inputs may be any that keep to these rules, and one draw needn't show every extreme that they name: `starts`: the first block of every group is 1; a 1 stands only at block indices that are multiples of 4; in one group, drawn from the seed, only the first block is 1. `a_log`: each value lies between log(0.5 / (0.03 * 4096)) and 4 above it.
All inputs are finite; a program needn't handle non-finite values.
Results may differ from the reference program's by a relative error of at most 0.025.
Values may be sent and summed in bfloat16 or wider, within the bound.
No kernel may reach another device: no remote copies, remote signals or barrier semaphores. Data moves between devices by JAX's collectives and lax.ppermute only.
A program may use at most 192 MiB of HBM per device.

```python
import math
from functools import partial
import jax
import jax.numpy as jnp
from jax import lax

D = 768
H = 24
E = 1536
N = 64
K = 4
TOK_DEV = 256
MIN_BLOCKS = 4
GROUPS = 8
BLOCKS = 16
GROUP_TOKENS = 4096


def draw_starts(key, part):
    key = jax.random.fold_in(key, 11)
    bit_key, whole_key = jax.random.split(key)
    random_bits = jax.random.randint(bit_key, (GROUPS, BLOCKS), 0, 2)
    columns = jnp.arange(BLOCKS)[None, :]
    allowed = columns % MIN_BLOCKS == 0
    flags = jnp.where(allowed, random_bits, 0)
    flags = jnp.where(columns == 0, 1, flags)
    chosen = jax.random.randint(whole_key, (), 0, GROUPS)
    group_rows = jnp.arange(GROUPS)[:, None]
    flags = jnp.where(group_rows == chosen, (columns == 0).astype(jnp.int32), flags)
    return flags.astype(jnp.int32)


def draw_a_log(key, part):
    key = jax.random.fold_in(key, 5)
    slowest = math.log(0.5 / (0.03 * GROUP_TOKENS))
    upper_end = slowest + 4.0
    return jax.random.uniform(key, (H,), jnp.float32, slowest, upper_end)


def block_scale(stream_key, shape, cuts, smallest, top_value):
    factor_of, own = 1.0, jax.random.fold_in(stream_key, 6)
    for position, blocks in cuts:
        draws = jnp.exp(jax.random.uniform(jax.random.fold_in(own, position), (blocks,), jnp.float32, smallest / len(cuts), top_value / len(cuts)))
        factor_of = factor_of * jnp.repeat(draws, shape[position] // blocks).reshape([-1 if axis == position else 1 for axis in range(len(shape))])
    return factor_of


def gaussian(key, extent, deviation, limit, cuts=(), held_as=jnp.bfloat16):
    drawn = jax.random.normal(key, extent, jnp.float32) * deviation
    if len(cuts) > 0:
        drawn = block_scale(key, extent, cuts, -0.22, 0.18) * drawn
    return jnp.clip(drawn, min=-limit, max=limit).astype(held_as)


def setup_inputs(seed: int = 0) -> dict:
    key_of = jax.random.split(jax.random.key(seed), 14)
    tokens = gaussian(key_of[0], (GROUPS, GROUP_TOKENS, D), 1.0, 6.0, ((0, 8), (1, 16)))
    starts = draw_starts(jax.random.fold_in(key_of[13], 71), 0)
    g_in = jnp.clip(1.0 + 0.1 * jax.random.normal(key_of[2], (D,), jnp.float32), 0.5, 1.5)
    w_in = gaussian(key_of[3], (D, 2 * E + 4 * N), D ** -0.5, 0.21875, ((0, 8),))
    w_dt = gaussian(key_of[4], (D, 2 * H), D ** -0.5, 0.21875, ((0, 8),))
    conv_w = gaussian(key_of[5], (K, E + 4 * N), K ** -0.5, 3.0, (), jnp.float32)
    conv_b = gaussian(key_of[6], (E + 4 * N,), 0.5, 3.0, (), jnp.float32)
    dt_bias = jnp.clip(jax.random.uniform(key_of[7], (2 * H,), jnp.float32, -4.5, -2.5), -4.5, -2.5)
    a_log = draw_a_log(jax.random.fold_in(key_of[13], 71), 0)
    dskip = jnp.clip(jax.random.uniform(key_of[9], (H,), jnp.float32, 0.5, 1.5), 0.5, 1.5)
    g_out = jnp.clip(1.0 + 0.1 * jax.random.normal(key_of[10], (E,), jnp.float32), 0.5, 1.5)
    w_out = gaussian(key_of[11], (E, D), E ** -0.5, 0.15625, ((0, 8),))
    d_out = gaussian(key_of[12], (GROUPS, GROUP_TOKENS, D), 1.0, 6.0, ((0, 8), (1, 16)))
    return {"tokens": tokens, "starts": starts, "g_in": g_in, "w_in": w_in, "w_dt": w_dt, "conv_w": conv_w, "conv_b": conv_b, "dt_bias": dt_bias, "a_log": a_log, "dskip": dskip, "g_out": g_out, "w_out": w_out, "d_out": d_out}


@jax.custom_vjp
def low(v):
    return lax.optimization_barrier(v.astype(jnp.bfloat16)).astype(jnp.float32)

@jax.custom_vjp
def low_back(v):
    return v

def low_keep(v):
    return (low(v), None)

def low_pass(kept, grad):
    return (grad,)

def back_keep(v):
    return (v, None)

def back_low(kept, grad):
    return (low(grad),)
low.defvjp(low_keep, low_pass)
low_back.defvjp(back_keep, back_low)
EPSILON = 1e-05
EXACT = lax.Precision.HIGHEST

def rms_scale(values, scale_gain):
    return values * lax.rsqrt(lax.optimization_barrier(jnp.mean(values * values, axis=-1, keepdims=True)) + EPSILON) * scale_gain

def decay_matrix(gaps, mask):
    return jnp.where(mask, jnp.exp(jnp.where(mask, gaps, 0.0)), 0.0)

def block_mix(x_heads, b_mat, c_mat, dt_all, cum_all, mask):
    cum_heads = jnp.swapaxes(cum_all, 1, 2)
    decays = decay_matrix(cum_heads[:, :, :, None] - cum_heads[:, :, None, :], mask)
    c_dot_b = jnp.einsum('gtn,gsn->gts', c_mat, b_mat, precision=EXACT)
    weights = decays * c_dot_b[:, None] * jnp.swapaxes(dt_all, 1, 2)[:, :, None, :]
    return jnp.einsum('ghts,gshp->gthp', weights, x_heads, precision=EXACT)

def block_forward(carry, pieces):
    x_heads, b_mat, c_mat, dt_all, la_all, continued = pieces
    positions = jnp.arange(x_heads.shape[1])
    cum_fwd = jnp.cumsum(la_all, axis=1)
    incoming = carry * continued[:, None, None, None]
    mix_sum = block_mix(x_heads, b_mat, c_mat, dt_all, cum_fwd, positions[:, None] > positions[None, :])
    mix_sum = mix_sum + jnp.exp(cum_fwd)[..., None] * jnp.einsum('gtn,ghnp->gthp', c_mat, incoming, precision=EXACT)
    last_cum = cum_fwd[:, -1, :]
    tail_weights = jnp.exp(last_cum[:, None, :] - cum_fwd) * dt_all
    scaled_x = tail_weights[..., None] * x_heads
    state_out = jnp.einsum('gsn,gshp->ghnp', b_mat, scaled_x, precision=EXACT)
    state_out = state_out + jnp.exp(last_cum)[:, :, None, None] * incoming
    return (state_out, mix_sum)

def block_reverse(carry, pieces):
    x_heads, b_mat, c_mat, dt_all, la_all, continued = pieces
    positions = jnp.arange(x_heads.shape[1])
    cum_rev = jnp.flip(jnp.cumsum(jnp.flip(la_all, 1), axis=1), 1)
    mix_sum = block_mix(x_heads, b_mat, c_mat, dt_all, cum_rev, positions[:, None] < positions[None, :])
    mix_sum = mix_sum + jnp.exp(cum_rev)[..., None] * jnp.einsum('gtn,ghnp->gthp', c_mat, carry, precision=EXACT)
    first_cum = cum_rev[:, 0, :]
    tail_weights = jnp.exp(first_cum[:, None, :] - cum_rev) * dt_all
    scaled_x = tail_weights[..., None] * x_heads
    state_out = jnp.einsum('gsn,gshp->ghnp', b_mat, scaled_x, precision=EXACT)
    state_out = (state_out + jnp.exp(first_cum)[:, :, None, None] * carry) * continued[:, None, None, None]
    return (state_out, mix_sum)

def layer_forward(tokens, g_in, w_in, w_dt, conv_w, conv_b, dt_bias, a_log, dskip, g_out, w_out, starts):
    num_groups, seq_len, model_width = tokens.shape
    inner_width = g_out.shape[0]
    num_heads = a_log.shape[0]
    state_width = (conv_b.shape[0] - inner_width) // 4
    head_size = inner_width // num_heads
    conv_width = conv_w.shape[0]
    block_len = TOK_DEV
    num_blocks = seq_len // block_len
    normed_in = low(rms_scale(tokens, g_in))
    projected = low_back(jnp.einsum('gsd,dk->gsk', normed_in, w_in, precision=EXACT))
    step_raw = low_back(jnp.einsum('gsd,dk->gsk', normed_in, w_dt, precision=EXACT))
    gate_in = projected[..., :inner_width]
    conv_input = low(projected[..., inner_width:])
    seq_ids = jnp.repeat(jnp.cumsum(starts, axis=1), block_len, axis=1).astype(jnp.int32)
    conv_sum = conv_b + conv_w[conv_width - 1] * conv_input
    for offset in range(1, conv_width):
        shifted = jnp.pad(conv_input, ((0, 0), (offset, 0), (0, 0)))[:, :seq_len]
        earlier = jnp.pad(seq_ids, ((0, 0), (offset, 0)), constant_values=-1)[:, :seq_len]
        conv_sum = conv_sum + conv_w[conv_width - 1 - offset] * jnp.where((earlier == seq_ids)[..., None], shifted, 0.0)
    activated = jax.nn.silu(conv_sum)
    x_heads = activated[..., :inner_width].reshape(num_groups, seq_len, num_heads, head_size)
    col_start = inner_width
    b_fwd = activated[..., col_start:col_start + state_width]
    c_fwd = activated[..., col_start + state_width:col_start + 2 * state_width]
    b_rev = activated[..., col_start + 2 * state_width:col_start + 3 * state_width]
    c_rev = activated[..., col_start + 3 * state_width:col_start + 4 * state_width]
    dt_all = jax.nn.softplus(step_raw + dt_bias)
    rates = jnp.exp(a_log)
    dt_fwd = dt_all[..., :num_heads]
    dt_rev = dt_all[..., num_heads:]
    continued = (1 - starts).astype(jnp.float32)

    def to_blocks(values):
        return jnp.moveaxis(values.reshape((num_groups, num_blocks, block_len) + values.shape[2:]), 1, 0)
    zeros_state = jnp.zeros((num_groups, num_heads, state_width, head_size), jnp.float32)
    final_fwd, mix_fwd = lax.scan(jax.checkpoint(block_forward), zeros_state, (to_blocks(x_heads), to_blocks(b_fwd), to_blocks(c_fwd), to_blocks(dt_fwd), to_blocks(-dt_fwd * rates), continued.T))
    final_rev, mix_rev = lax.scan(jax.checkpoint(block_reverse), zeros_state, (to_blocks(x_heads), to_blocks(b_rev), to_blocks(c_rev), to_blocks(dt_rev), to_blocks(-dt_rev * rates), continued.T), reverse=True)
    mix_all = jnp.moveaxis(mix_fwd + mix_rev, 0, 1).reshape(num_groups, seq_len, inner_width)
    mix_all = mix_all + (x_heads * dskip[:, None]).reshape(num_groups, seq_len, inner_width)
    gated = mix_all * jax.nn.silu(gate_in)
    mixed_low = low(rms_scale(gated, g_out))
    return tokens + jnp.einsum('gse,ed->gsd', mixed_low, w_out, precision=EXACT)

def reference(tokens, starts, g_in, w_in, w_dt, conv_w, conv_b, dt_bias, a_log, dskip, g_out, w_out, d_out):
    forward_fn = partial(layer_forward, starts=starts)
    output, pull_back = jax.vjp(forward_fn, tokens.astype(jnp.float32), g_in, w_in.astype(jnp.float32), w_dt.astype(jnp.float32), conv_w, conv_b, dt_bias, a_log, dskip, g_out, w_out.astype(jnp.float32))
    grads = pull_back(d_out.astype(jnp.float32))
    return (output.astype(jnp.bfloat16), grads[0], grads[1], grads[2], grads[3], grads[4], grads[5], grads[6], grads[7], grads[8], grads[9], grads[10])
```

```python
import jax
import jax.numpy as jnp
from jax import lax
from jax.experimental import pallas as pl
from jax.experimental.pallas import tpu as pltpu
from jax.sharding import PartitionSpec as P

F32, BF = jnp.float32, jnp.bfloat16
EPS = 1e-05
LOG2E = 1.4426950408889634
D, H, E, N, T = 768, 24, 1536, 64, 256
C = E + 4 * N
CD = C + 128
HALO = 16
TILES = E // 128
DP, SEQ = 8, 16
VMEM = 56 * 1024 * 1024


def iota(shape, dim):
    return lax.broadcasted_iota(jnp.int32, shape, dim)


def mm(a, b):
    return jnp.dot(a, b, preferred_element_type=F32)


def mm_nt(a, b):
    return lax.dot_general(a, b, (((1,), (1,)), ((), ())), preferred_element_type=F32)


def flip(v):
    return v.astype(F32).T.astype(v.dtype)


def sigmoid(v):
    return 1.0 / (1.0 + jnp.exp(-v))


def silu(v):
    return v * sigmoid(v)


def split2(v):
    hi = v.astype(BF)
    return hi, (v - hi.astype(F32)).astype(BF)


def pair(v):
    return jnp.concatenate(split2(v), axis=1)


def onehot(cond):
    return jnp.where(cond, 1.0, 0.0).astype(BF)


def spread(v, tile, base):
    head = iota((256, 128), 0) & 127
    column = (iota((256, 128), 1) >> 6) + (2 * tile + base)
    return mm(v, onehot(head == column))


def head_sum(v, tile, base):
    head = (iota((128, 128), 0) >> 6) + (2 * tile + base)
    mark = onehot(head == iota((128, 128), 1))
    hi, lo = split2(v)
    return mm(hi, mark) + mm(lo, mark)


def head_sum1(v, tile, base):
    head = (iota((128, 128), 0) >> 6) + (2 * tile + base)
    return mm(v.astype(BF), onehot(head == iota((128, 128), 1)))


def tri_sum(mask, v):
    hi = v.astype(BF)
    rest = v - hi.astype(F32)
    mid = rest.astype(BF)
    low = (rest - mid.astype(F32)).astype(BF)
    return mm(mask, hi) + mm(mask, mid) + mm(mask, low)


def tri(cond):
    return onehot(cond(iota((T, T), 0), iota((T, T), 1)))


def lanes(rows=T):
    return iota((rows, 128), 1)


def tile_at(i):
    return pl.ds(pl.multiple_of(i * 128, 128), 128)


def bc_parts(cs, at):
    both = silu(cs[:, at : at + 128])
    return both[:, :N].astype(BF), both[:, N:].astype(BF)


def ends(cum):
    return jnp.where(lanes(1) < H, cum[T - 1 : T], cum[0:1])


def decay_rows(dec, i, first, second):
    a, b = spread(dec, i, first), spread(dec, i, second)
    ah, bh = a.astype(BF).astype(F32), b.astype(BF).astype(F32)
    row = iota((16, 128), 0)
    out = jnp.where(row == 0, ah, jnp.where(row == 1, a - ah, jnp.where(row == 2, bh, b - bh)))
    return jnp.where(row < 4, out, 0.0).astype(BF)


def put_slices(pay, i, first, second, dec):
    group, at = i // 3, tile_at(lax.rem(i, 3))
    for q in range(4):
        j = 4 * group + q
        pay[j, 0:16, at] = first[16 * q : 16 * q + 16].astype(BF)
        pay[j, 16:32, at] = second[16 * q : 16 * q + 16].astype(BF)
        pay[j, 32:48, at] = dec


def take_slices(recv, first, second, first_scale):
    for j in range(SEQ):
        rows, at = pl.ds(16 * (j % 4), 16), pl.ds(384 * (j // 4), 384)
        first[rows, at] = (recv[j, 0:16].astype(F32) * first_scale).astype(BF)
        second[rows, at] = recv[j, 16:32]


def front(ids, cont, tok, halo, gin, cw, cb, dtb, alog, *refs):
    parts, (u_out, ci_out, cs, sraw_out, dt_out, cum_out, pay), (w, cif, sem) = (
        refs[:8],
        refs[8:15],
        refs[15:],
    )
    copies = [
        pltpu.make_async_copy(
            parts[k], w.at[pl.ds(pl.multiple_of(ids[k] * 96, 16), 96)], sem.at[k]
        )
        for k in range(8)
    ]
    for copy in copies:
        copy.start()
    x = jnp.concatenate([halo[...], tok[...]], axis=0).astype(F32)
    u = x * lax.rsqrt(jnp.mean(x * x, axis=1, keepdims=True) + EPS) * gin[...]
    u_out[...] = u.astype(BF)
    for copy in copies:
        copy.wait()
    keep = cont[0]
    mask = jnp.where(iota((HALO + T, 1), 0) < HALO, keep, 1.0)
    for j in range(7):
        at = slice(256 * j, 256 * j + 256)
        ci = (mm(u_out[...], w[:, at]) * mask).astype(BF)
        ci_out[:, at] = ci
        cif[...] = ci.astype(F32)
        total = cb[:, at]
        for k in range(4):
            total = total + cw[k : k + 1, at] * cif[HALO - 3 + k : HALO - 3 + k + T, :]
        cs[:, at] = total
    sraw = mm(u_out[HALO:, :], w[:, C:]) + dtb[...]
    sraw_out[...] = sraw
    e = jnp.exp(-jnp.abs(sraw))
    dt = jnp.maximum(sraw, 0.0) + jnp.log1p(e)
    dt = jnp.where(lanes() < 2 * H, dt, 0.0)
    dt_out[...] = dt
    rate = jnp.where(lanes(1) < 2 * H, jnp.exp(alog[...]), 0.0)
    la = -dt * rate
    cum = jnp.where(
        lanes() < H,
        tri_sum(tri(lambda r, c: r >= c), la),
        tri_sum(tri(lambda r, c: r <= c), la),
    )
    cum_out[...] = cum
    last = ends(cum)
    tail = pair(jnp.exp(last - cum) * dt)
    dec = pair(jnp.broadcast_to(jnp.exp(last) * keep, (16, 128)))
    bf_t = flip(bc_parts(cs, E)[0])
    br_t = flip(bc_parts(cs, E + 128)[0])

    def tile(i, _):
        x_act = silu(cs[:, tile_at(i)])
        sf = mm(bf_t, (spread(tail, i, 0) * x_act).astype(BF))
        sr = mm(br_t, (spread(tail, i, H) * x_act).astype(BF)) * keep
        put_slices(pay, i, sf, sr, decay_rows(dec, i, 0, H))
        return 0

    lax.fori_loop(0, TILES, tile, 0)


def scan_blocks(recv, out):
    carry = jnp.zeros((16, 384), F32)
    back = jnp.zeros((16, 384), F32)
    for i in range(SEQ):
        k = SEQ - 1 - i
        out[i, 0:16] = carry.astype(BF)
        out[k, 16:32] = back.astype(BF)
        dec = recv[i, 32:48].astype(F32)
        carry = (dec[0:1] + dec[1:2]) * carry + recv[i, 0:16].astype(F32)
        dec = recv[k, 32:48].astype(F32)
        back = (dec[2:3] + dec[3:4]) * back + recv[k, 16:32].astype(F32)


def lower_blocks(e_left, e_right, g):
    left = e_left * g[:, :128]
    right = e_right * g[128:, 128:]
    return left, right


def columns_of(cum2, col):
    for h in range(2 * H):
        col[h] = jnp.broadcast_to(cum2[:, h : h + 1], (T, 128))


def halves(v):
    first = lanes() < 64
    return jnp.where(first, v, 0.0).astype(BF), jnp.where(first, 0.0, v).astype(BF)


def low_full(left, right):
    right = jnp.concatenate([jnp.zeros((128, 128), right.dtype), right], axis=0)
    return jnp.concatenate([left, right], axis=1)


def up_full(left, right):
    left = jnp.concatenate([left, jnp.zeros((128, 128), left.dtype)], axis=0)
    return jnp.concatenate([left, right], axis=1)


def local_mix(cs, dt, cum, yf, yr, col, row, gf, gr):
    cum2 = cum[...] * LOG2E
    row[...] = cum2.T
    columns_of(cum2, col)
    r, c = iota((T, T), 0), iota((T, T), 1)
    b, cc = bc_parts(cs, E)
    gf[...] = jnp.where(r > c, mm_nt(cc, b), 0.0)
    b, cc = bc_parts(cs, E + 128)
    gr[...] = jnp.where(r < c, mm_nt(cc, b), 0.0)
    dt2 = pair(dt[...])

    def weights(h, forward):
        at, along = col[h], row[pl.ds(h, 1), :]
        if forward:
            left = jnp.exp2(jnp.minimum(at - along[:, :128], 0.0)) * gf[:, :128]
            right = jnp.exp2(jnp.minimum(at[128:] - along[:, 128:], 0.0)) * gf[128:, 128:]
            return low_full(left.astype(BF), right.astype(BF))
        left = jnp.exp2(jnp.minimum(at[:128] - along[:, :128], 0.0)) * gr[:128, :128]
        right = jnp.exp2(jnp.minimum(at - along[:, 128:], 0.0)) * gr[:, 128:]
        return up_full(left.astype(BF), right.astype(BF))

    def tile(i, _):
        at = tile_at(i)
        x = silu(cs[:, at])
        x0, x1 = halves(x * spread(dt2, i, 0))
        yf[:, at] = mm(weights(2 * i, True), x0) + mm(weights(2 * i + 1, True), x1)
        x0, x1 = halves(x * spread(dt2, i, H))
        yr[:, at] = mm(weights(H + 2 * i, False), x0) + mm(weights(H + 2 * i + 1, False), x1)
        return 0

    lax.fori_loop(0, TILES, tile, 0)


def load_rest(rest, wg, wo, sem):
    copies = []
    for p in range(DP):
        at = 384 * p
        if wg is not None:
            copies.append((rest.at[pl.ds(at, 96)], wg.at[0, pl.ds(96 * p, 96)]))
            copies.append((rest.at[pl.ds(at + 96, 96)], wg.at[1, pl.ds(96 * p, 96)]))
        if wo is not None:
            copies.append((rest.at[pl.ds(at + 192, 192)], wo.at[pl.ds(192 * p, 192)]))
    copies = [pltpu.make_async_copy(a, b, sem.at[k]) for k, (a, b) in enumerate(copies)]
    for copy in copies:
        copy.start()
    return copies


def gate_products(u, dout, rest, gate, dn, wg, wo, sem):
    copies = load_rest(rest, wg, wo, sem)
    for copy in copies:
        copy.wait()
    gate[:, :D] = mm(u[HALO:, :], wg[0])
    gate[:, D:] = mm(u[HALO:, :], wg[1])
    dn[...] = mm_nt(dout[...], wo[...])


def gated_norm(cont, cs, cum, ylf, ylr, recv, gate, dn, gout, dsk, *refs):
    (n16, dg16, dm16, row, dgout, ddsk, pay), (sf, sr, yfs, yrs, mix, xdm) = refs[:7], refs[7:]
    keep = cont[0]
    take_slices(recv, sf, sr, keep)
    cumv = cum[...]
    ef2 = pair(jnp.exp(cumv))
    dec = pair(jnp.broadcast_to(jnp.exp(ends(cumv)) * keep, (16, 128)))
    _, cf = bc_parts(cs, E)
    _, cr = bc_parts(cs, E + 128)
    zero = jnp.zeros((T, 128), F32)

    def first(i, sums):
        at = tile_at(i)
        yf = ylf[:, at] + spread(ef2, i, 0) * mm(cf, sf[:, at])
        yr = ylr[:, at] + spread(ef2, i, H) * mm(cr, sr[:, at])
        yfs[:, at] = yf
        yrs[:, at] = yr
        m = yf + yr + dsk[:, at] * silu(cs[:, at])
        mix[:, at] = m
        gd = m * silu(gate[:, at])
        return sums[0] + gd * gd, sums[1] + dn[:, at] * gout[:, at] * gd

    squares, crossed = lax.fori_loop(0, TILES, first, (zero, zero))
    rs = lax.rsqrt(jnp.sum(squares, axis=1, keepdims=True) / E + EPS)
    pull = jnp.sum(crossed, axis=1, keepdims=True) / E * (rs * rs * rs)
    cf_t, cr_t = flip(cf), flip(cr)

    def second(i, rows):
        at = tile_at(i)
        g, m = gate[:, at], mix[:, at]
        sg = sigmoid(g)
        sl = g * sg
        gd = m * sl
        gdr = gd * rs
        n16[:, at] = (gdr * gout[:, at]).astype(BF)
        dgout[:, at] = jnp.sum(dn[:, at] * gdr, axis=0, keepdims=True)
        dgd = rs * (dn[:, at] * gout[:, at]) - gd * pull
        dg16[:, at] = (dgd * m * sg * (1.0 + g * (1.0 - sg))).astype(BF)
        dm = dgd * sl
        low = dm.astype(BF)
        dm16[:, at] = low
        dmr = low.astype(F32)
        xdm[:, at] = jnp.sum(dm * silu(cs[:, at]), axis=0, keepdims=True)
        lf = mm(cf_t, (spread(ef2, i, 0) * dm).astype(BF)) * keep
        lr = mm(cr_t, (spread(ef2, i, H) * dm).astype(BF))
        put_slices(pay, i, lr, lf, decay_rows(dec, i, H, 0))
        return (
            rows + head_sum(dmr * yfs[:, at], i, 0) + head_sum(dmr * yrs[:, at], i, H)
        )

    row[...] = lax.fori_loop(0, TILES, second, zero)
    total = jnp.zeros((8, 128), F32)
    for i in range(TILES):
        total = total + head_sum(
            jnp.broadcast_to(xdm[:, 128 * i : 128 * i + 128], (8, 128)), i, 0
        )
    ddsk[...] = total[0:1]


def out_and_grads(ids, tok, u, n16, dg16, dout, rest, out, keep, send, wo, n_t, u_t, sem):
    copies = load_rest(rest, None, wo, sem)
    n_t[...] = flip(n16[...])
    u_t[...] = flip(u[HALO:, :])
    for ref, base in ((send, 4), (keep, 0)):
        for k in range(4):
            d = ids[base + k]
            ref[k, 192:384] = mm(
                n_t[pl.ds(pl.multiple_of(d * 192, 64), 192), :], dout[...]
            ).astype(BF)
            rows = u_t[pl.ds(pl.multiple_of(d * 96, 32), 96), :]
            ref[k, 0:96] = mm(rows, dg16[:, :D]).astype(BF)
            ref[k, 96:192] = mm(rows, dg16[:, D:]).astype(BF)
    for copy in copies:
        copy.wait()
    out[...] = (tok[...].astype(F32) + mm(n16[...], wo[...])).astype(BF)


def local_back(cs, dt, cum, dm16, zf, zr, dgf, dgr, col, row, gf, gr, dm_t):
    cum2 = cum[...] * LOG2E
    row[...] = cum2.T
    columns_of(cum2, col)
    dm_t[...] = flip(dm16[...])
    s, t = iota((T, T), 0), iota((T, T), 1)
    b, cc = bc_parts(cs, E)
    gf[...] = jnp.where(t > s, mm_nt(b, cc), 0.0)
    b, cc = bc_parts(cs, E + 128)
    gr[...] = jnp.where(t < s, mm_nt(b, cc), 0.0)
    dgf[...] = jnp.zeros((T, T), F32)
    dgr[...] = jnp.zeros((T, T), F32)
    dt2 = pair(dt[...])

    def tile(i, _):
        at = tile_at(i)
        x = silu(cs[:, at])
        d0, d1 = halves(dm16[:, at].astype(F32))
        dms = dm_t[at, :]
        for forward in (True, False):
            base = 0 if forward else H
            xs = halves(x * spread(dt2, i, base))
            total = jnp.zeros((T, 128), F32)
            small = jnp.zeros((128, 128), F32)
            large = jnp.zeros((T, 128), F32)
            for e in range(2):
                h = base + 2 * i + e
                at_s, along = col[h], row[pl.ds(h, 1), :]
                if forward:
                    ea = jnp.exp2(jnp.minimum(along[:, :128] - at_s[:128], 0.0))
                    eb = jnp.exp2(jnp.minimum(along[:, 128:] - at_s, 0.0))
                    w = up_full((ea * gf[:128, :128]).astype(BF), (eb * gf[:, 128:]).astype(BF))
                    small = small + ea * mm(xs[e][:128], dms[:, :128])
                    large = large + eb * mm(xs[e], dms[:, 128:])
                else:
                    ea = jnp.exp2(jnp.minimum(along[:, :128] - at_s, 0.0))
                    eb = jnp.exp2(jnp.minimum(along[:, 128:] - at_s[128:], 0.0))
                    w = low_full((ea * gr[:, :128]).astype(BF), (eb * gr[128:, 128:]).astype(BF))
                    large = large + ea * mm(xs[e], dms[:, :128])
                    small = small + eb * mm(xs[e][128:], dms[:, 128:])
                total = total + mm(w, (d0, d1)[e])
            if forward:
                zf[:, at] = total
                dgf[:128, :128] += small
                dgf[:, 128:] += large
            else:
                zr[:, at] = total
                dgr[:, :128] += large
                dgr[128:, 128:] += small
        return 0

    lax.fori_loop(0, TILES, tile, 0)
    dgf[...] = jnp.where(t > s, dgf[...], 0.0)
    dgr[...] = jnp.where(t < s, dgr[...], 0.0)


def last_back(
    ids, cont, tok, halo, gin, cw, alog, dsk, cs, sraw, dt, cum, ci, u, dout, dm16, dg16, zf, zr,
    dgf, dgr, back, fore, row, dgout, ddsk, rest, *refs
):
    parts, (dtok, dhalo, keep_out, send_out), scratch = refs[:8], refs[8:12], refs[12:]
    w, wg, sf, sr, kf, kr, dcs, cif, dall, u_t, small, srow, sem, sem2 = scratch
    copies = [
        pltpu.make_async_copy(
            parts[k], w.at[pl.ds(pl.multiple_of(ids[k] * 96, 16), 96)], sem2.at[k]
        )
        for k in range(8)
    ]
    for copy in copies:
        copy.start()
    copies += load_rest(rest, wg, None, sem)
    keep = cont[0]
    take_slices(back, kr, kf, keep)
    take_slices(fore, sf, sr, keep)
    u_t[...] = flip(u[...])
    cumv, dtv = cum[...], dt[...]
    last = ends(cumv)
    te2, ef2, dt2 = pair(jnp.exp(last - cumv)), pair(jnp.exp(cumv)), pair(dtv)
    bf, cf = bc_parts(cs, E)
    br, cr = bc_parts(cs, E + 128)
    dcs[0:HALO] = jnp.zeros((HALO, C), F32)
    dcs[HALO + T :] = jnp.zeros((16, C), F32)
    zero = jnp.zeros((T, 128), F32)

    def silu_slope(v):
        sg = sigmoid(v)
        return sg * (1.0 + v * (1.0 - sg))

    def tile(i, sums):
        inner, tails, direct, dbf, dcf, dbr, dcr, dots = sums
        at = tile_at(i)
        x = silu(cs[:, at])
        dm = dm16[:, at].astype(F32)
        dx = dsk[:, at] * dm
        new = []
        for base, z, k, s, b in ((0, zf, kf, sf, bf), (H, zr, kr, sr, br)):
            dts, te, ef = spread(dt2, i, base), spread(te2, i, base), spread(ef2, i, base)
            xd = (x * dts).astype(BF).astype(F32)
            zi, zt = z[:, at], te * mm(b, k[:, at])
            zs = zi + zt
            dx = dx + dts * zs
            inner = inner + head_sum(xd * zi, i, base)
            tails = tails + head_sum1(xd * zt, i, base)
            direct = direct + head_sum1(x * zs, i, base)
            new.append(mm_nt((te * xd).astype(BF), k[:, at]))
            new.append(mm_nt((ef * dm).astype(BF), s[:, at]))
            both = jnp.sum(s[:, at].astype(F32) * k[:, at].astype(F32), axis=0, keepdims=True)
            dots = dots + head_sum(jnp.broadcast_to(both, (8, 128)), i, base)
        dcs[HALO : HALO + T, at] = dx * silu_slope(cs[:, at])
        return (inner, tails, direct, dbf + new[0], dcf + new[1], dbr + new[2], dcr + new[3], dots)

    zn = jnp.zeros((T, N), F32)
    inner, tails, direct, dbf, dcf, dbr, dcr, dots = lax.fori_loop(
        0, TILES, tile, (zero, zero, zero, zn, zn, zn, zn, jnp.zeros((8, 128), F32))
    )
    gf16, gr16 = dgf[...].astype(BF), dgr[...].astype(BF)
    dbf = dbf + mm(gf16, cf)
    dcf = dcf + mm(flip(gf16), bf)
    dbr = dbr + mm(gr16, cr)
    dcr = dcr + mm(flip(gr16), br)
    for at, b, c in ((E, dbf, dcf), (E + 128, dbr, dcr)):
        dcs[HALO : HALO + T, at : at + 128] = jnp.concatenate([b, c], axis=1) * silu_slope(
            cs[:, at : at + 128]
        )
    rate = jnp.where(lanes(1) < 2 * H, jnp.exp(alog[...]), 0.0)
    v = row[...] - inner
    forward = lanes() < H
    dla = jnp.where(
        forward,
        tri_sum(tri(lambda r, c: r <= c), v) + tri_sum(tri(lambda r, c: r > c), tails),
        tri_sum(tri(lambda r, c: r >= c), v) + tri_sum(tri(lambda r, c: r < c), tails),
    ) + jnp.exp(last) * dots[0:1]
    dstep = (direct - dla * rate) * sigmoid(sraw[...])
    dstep = jnp.where(lanes() < 2 * H, dstep, 0.0)
    dall[0:HALO, C:] = jnp.zeros((HALO, 128), BF)
    dall[HALO:, C:] = dstep.astype(BF)
    dal = jnp.sum(dla * (-dtv * rate), axis=0, keepdims=True)
    small[...] = jnp.zeros((96, 128), F32)
    small[88:89] = jnp.sum(dstep, axis=0, keepdims=True)
    srow[...] = jnp.broadcast_to(dal, (8, 128))
    small[89:90, 0:H] = srow[0:1, 0:H] + srow[0:1, H : 2 * H]
    small[90:91] = ddsk[...]
    mask = jnp.where(iota((HALO + T, 1), 0) < HALO, keep, 1.0)
    for j in range(7):
        at = slice(256 * j, 256 * j + 256)
        g = dcs[HALO : HALO + T, at]
        cif[...] = ci[:, at].astype(F32)
        grads = [jnp.sum(g, axis=0, keepdims=True)]
        total = jnp.zeros((HALO + T, 256), F32)
        for k in range(4):
            grads.append(
                jnp.sum(g * cif[HALO - 3 + k : HALO - 3 + k + T, :], axis=0, keepdims=True)
            )
            total = total + cw[k : k + 1, at] * dcs[3 - k : 3 - k + HALO + T, at]
        dall[:, at] = (total * mask).astype(BF)
        for half in range(2):
            tile_no, cut = 2 * j + half, slice(128 * half, 128 * half + 128)
            small[56 + tile_no : 57 + tile_no] = grads[0][:, cut]
            for k in range(4):
                at_row = 14 * k + tile_no
                small[at_row : at_row + 1] = grads[k + 1][:, cut]
    for j in range(TILES):
        small[70 + j : 71 + j] = dgout[:, 128 * j : 128 * j + 128]
    for copy in copies:
        copy.wait()
    du = mm_nt(dall[...], w[...])
    dg = mm_nt(dg16[:, :D], wg[0]) + mm_nt(dg16[:, D:], wg[1])
    du = du + jnp.concatenate([jnp.zeros((HALO, D), F32), dg], axis=0)
    x = jnp.concatenate([halo[...], tok[...]], axis=0).astype(F32)
    r = lax.rsqrt(jnp.mean(x * x, axis=1, keepdims=True) + EPS)
    duxr = du * x * r
    for j in range(6):
        small[82 + j : 83 + j] = jnp.sum(duxr[:, 128 * j : 128 * j + 128], axis=0, keepdims=True)
    dxh = du * gin[...]
    dx = r * dxh - x * (r * r * r * jnp.mean(dxh * x, axis=1, keepdims=True))
    dhalo[...] = dx[:HALO]
    dtok[...] = dout[...].astype(F32) + dx[HALO:]
    low = small[...].astype(BF)
    for ref, base in ((send_out, 12), (keep_out, 8)):
        for k in range(4):
            rows = u_t[pl.ds(pl.multiple_of(ids[base + k] * 96, 32), 96), :]
            ref[k, :, :CD] = mm(rows, dall[...]).astype(BF)
            ref[k, :, CD:] = low


def add_pairs(a, b, *outs):
    for k in range(4):
        outs[k][...] = (a[k].astype(F32) + b[k].astype(F32)).astype(BF)


def add_four(a, b, c, d, out):
    total = a[...].astype(F32) + b[...].astype(F32) + c[...].astype(F32) + d[...].astype(F32)
    for j in range(total.shape[1] // 128):
        out[j] = total[:, 128 * j : 128 * j + 128].astype(BF)


def add_blocks(recv, out):
    total = recv[0].astype(F32)
    for i in range(1, SEQ):
        total = total + recv[i].astype(F32)
    low = total.astype(BF)
    for i in range(SEQ):
        out[i] = low


def finish(rest, tail, dwin, dwdt, dwout, dcw, dcb, dgout, dgin, ddtb, dal, ddsk):
    for j in range(6):
        at = slice(128 * j, 128 * j + 128)
        dwin[:, at] = rest[j, 0:96].astype(F32)
        dwin[:, D + 128 * j : D + 128 * j + 128] = rest[j, 96:192].astype(F32)
        dwout[:, at] = rest[j, 192:384].astype(F32)
    for j in range(14):
        dwin[:, E + 128 * j : E + 128 * j + 128] = tail[j].astype(F32)
    dwdt[...] = tail[14, :, 0 : 2 * H].astype(F32)
    small = tail[15].astype(F32)
    for j in range(14):
        at = slice(128 * j, 128 * j + 128)
        for k in range(4):
            dcw[k : k + 1, at] = small[14 * k + j : 14 * k + j + 1]
        dcb[:, at] = small[56 + j : 57 + j]
    for j in range(TILES):
        dgout[:, 128 * j : 128 * j + 128] = small[70 + j : 71 + j]
    for j in range(6):
        dgin[:, 128 * j : 128 * j + 128] = small[82 + j : 83 + j]
    ddtb[...] = small[88:89, 0 : 2 * H]
    dal[...] = small[89:90, 0:H]
    ddsk[...] = small[90:91, 0:H]


V = pl.BlockSpec(memory_space=pltpu.VMEM)
S = pl.BlockSpec(memory_space=pltpu.SMEM)
ANY = pl.BlockSpec(memory_space=pl.ANY)


def shape(*dims, dtype=F32):
    return jax.ShapeDtypeStruct(dims, dtype)


def call(kernel, name, ins, outs, scratch=(), flops=0, **more):
    specs, args = zip(*ins)
    moved = sum(a.size * a.dtype.itemsize for a in args)
    moved += sum(o.size * o.dtype.itemsize for o in outs)
    return pl.pallas_call(
        kernel,
        name=name,
        out_shape=tuple(outs),
        in_specs=list(specs),
        out_specs=tuple(V for _ in outs),
        scratch_shapes=list(scratch),
        cost_estimate=pl.CostEstimate(flops=flops, bytes_accessed=moved, transcendentals=0),
        compiler_params=pltpu.CompilerParams(vmem_limit_bytes=VMEM),
        **more,
    )(*args)


def vm(*dims, dtype=F32):
    return pltpu.VMEM(dims, dtype)


def shift_y(k):
    return [(2 * y + c, 2 * ((y + k) % 4) + c) for y in range(4) for c in range(2)]


SWAP = [(i, i ^ 1) for i in range(DP)]


def exchange(value):
    return lax.all_to_all(value, "seq", 0, 0, tiled=True)


def add_swapped(keep, send, name):
    recv = lax.ppermute(send, "dp", SWAP)
    rows, cols = keep.shape[1:]
    step = rows // 3
    return pl.pallas_call(
        add_pairs,
        name=name,
        grid=(3,),
        out_shape=tuple(shape(rows, cols, dtype=BF) for _ in range(4)),
        in_specs=[pl.BlockSpec((4, step, cols), lambda i: (0, i, 0))] * 2,
        out_specs=tuple(pl.BlockSpec((step, cols), lambda i: (i, 0)) for _ in range(4)),
        compiler_params=pltpu.CompilerParams(vmem_limit_bytes=VMEM),
    )(keep, recv)


def over_y(parts, name):
    got = [lax.ppermute(parts[k], "dp", shift_y(k)) for k in (1, 2, 3)]
    rows, cols = parts[0].shape
    return call(
        add_four,
        name,
        [(V, parts[0])] + [(V, g) for g in got],
        [shape(cols // 128, rows, 128, dtype=BF)],
    )[0]


def over_seq(tiles, rows, name):
    got = exchange(tiles.reshape(SEQ, rows, 128))
    total = call(add_blocks, name, [(V, got)], [shape(SEQ, rows, 128, dtype=BF)])[0]
    return exchange(total)


def local(
    tokens, starts, g_in, w_in, w_dt, conv_w, conv_b, dt_bias, a_log, dskip, g_out, w_out, d_out
):
    dp = lax.axis_index("dp")
    y, core = dp // 2, dp % 2
    tok, dout = tokens[0], d_out[0]
    cont = (1 - starts[0]).astype(F32)

    own = jnp.concatenate([w_in[:, E:], jnp.pad(w_dt, ((0, 0), (0, 128 - 2 * H)))], axis=1)
    halo = lax.ppermute(tok[-HALO:], "seq", [(i, i + 1) for i in range(SEQ - 1)])
    column = [own] + [lax.ppermute(own, "dp", shift_y(k)) for k in (1, 2, 3)]
    parts = column + [lax.ppermute(part, "dp", SWAP) for part in column]
    from_y = [2 * ((y - k) % 4) + core for k in range(4)]
    to_y = [(y + k) % 4 for k in range(4)]
    mine = [2 * t + core for t in to_y]
    other = [2 * t + 1 - core for t in to_y]
    ids = jnp.stack(from_y + [2 * ((y - k) % 4) + 1 - core for k in range(4)] + mine + other)
    rest_own = jnp.concatenate([w_in[:, :D], w_in[:, D:E], w_out], axis=0)
    rest_own = lax.optimization_barrier([rest_own] + column[1:])[0]
    rest = lax.all_gather(rest_own, "dp", axis=0, tiled=True)

    row = lambda v: v.reshape(1, -1)
    pad = lambda v: jnp.pad(v, (0, 128 - v.shape[0])).reshape(1, 128)
    alog = pad(jnp.concatenate([a_log, a_log]))
    dsk = row(jnp.repeat(dskip, N))
    gin, gout = row(g_in), row(g_out)
    part_ins = [(ANY, part) for part in parts]
    w_scratch = vm(D, CD, dtype=BF)
    dma = pltpu.SemaphoreType.DMA

    u, ci, cs, sraw, dt, cum, pay = call(
        front,
        "front",
        [(S, ids), (S, cont), (V, tok), (V, halo), (V, gin), (V, conv_w), (V, row(conv_b))]
        + [(V, pad(dt_bias)), (V, alog)]
        + part_ins,
        [shape(HALO + T, D, dtype=BF), shape(HALO + T, C, dtype=BF), shape(T, C)]
        + [shape(T, 128)] * 3
        + [shape(SEQ, 48, 384, dtype=BF)],
        [w_scratch, vm(HALO + T, 256), dma((8,))],
        flops=2 * T * D * CD,
    )

    def across(payload, name):
        got = exchange(payload)
        out = call(scan_blocks, name, [(V, got)], [shape(SEQ, 32, 384, dtype=BF)])[0]
        return exchange(out)

    mix_scratch = [vm(2 * H, T, 128), vm(128, T), vm(T, T), vm(T, T)]
    fore = across(pay, "scan_states")
    ylf, ylr = call(
        local_mix,
        "local_mix",
        [(V, cs), (V, dt), (V, cum)],
        [shape(T, E)] * 2,
        mix_scratch,
        flops=2 * 48 * T * T * 256,
    )
    rest_scratch = [vm(2, D, D, dtype=BF), vm(E, D, dtype=BF), dma((24,))]
    gate, dn = call(
        gate_products,
        "gate_products",
        [(V, u), (V, dout), (ANY, rest)],
        [shape(T, E)] * 2,
        rest_scratch,
        flops=4 * T * D * E,
    )
    n16, dg16, dm16, rows, dgout, ddsk, pay_back = call(
        gated_norm,
        "gated_norm",
        [(S, cont), (V, cs), (V, cum), (V, ylf), (V, ylr), (V, fore), (V, gate), (V, dn)]
        + [(V, gout), (V, dsk)],
        [shape(T, E, dtype=BF)] * 3
        + [shape(T, 128), shape(1, E), shape(1, 128), shape(SEQ, 48, 384, dtype=BF)],
        [vm(N, E, dtype=BF)] * 2 + [vm(T, E)] * 3 + [vm(1, E)],
        flops=12 * T * N * E,
    )
    back = across(pay_back, "scan_adjoints")
    out, rest_keep, rest_send = call(
        out_and_grads,
        "out_and_grads",
        [(S, ids[8:]), (V, tok), (V, u), (V, n16), (V, dg16), (V, dout), (ANY, rest)],
        [shape(T, D, dtype=BF)] + [shape(4, 384, D, dtype=BF)] * 2,
        [vm(E, D, dtype=BF), vm(E, T, dtype=BF), vm(D, T, dtype=BF), dma((8,))],
        flops=6 * T * D * E,
    )
    zf, zr, dgf, dgr = call(
        local_back,
        "local_back",
        [(V, cs), (V, dt), (V, cum), (V, dm16)],
        [shape(T, E)] * 2 + [shape(T, T)] * 2,
        mix_scratch + [vm(E, T, dtype=BF)],
        flops=4 * 48 * T * T * 256,
    )
    rest_tiles = over_y(add_swapped(rest_keep, rest_send, "add_rest_cores"), "add_rest_y")

    dtok, dhalo, keep, send = call(
        last_back,
        "last_back",
        [(S, ids), (S, cont), (V, tok), (V, halo), (V, gin), (V, conv_w), (V, alog), (V, dsk)]
        + [(V, a) for a in (cs, sraw, dt, cum, ci, u, dout, dm16, dg16, zf, zr, dgf, dgr)]
        + [(V, back), (V, fore), (V, rows), (V, dgout), (V, ddsk), (ANY, rest)]
        + part_ins,
        [shape(T, D), shape(HALO, D)] + [shape(4, 96, 2048, dtype=BF)] * 2,
        [w_scratch, vm(2, D, D, dtype=BF)]
        + [vm(N, E, dtype=BF)] * 4
        + [vm(HALO + T + 16, C), vm(HALO + T, 256), vm(HALO + T, CD, dtype=BF)]
        + [vm(D, HALO + T, dtype=BF), vm(96, 128), vm(8, 128), dma((16,)), dma((8,))],
        flops=2 * T * D * (2 * CD + E),
    )
    dback = lax.ppermute(dhalo, "seq", [(i + 1, i) for i in range(SEQ - 1)])
    dtok = dtok.at[-HALO:].add(dback)
    tail_tiles = over_y(add_swapped(keep, send, "add_tail_cores"), "add_tail_y")
    rest_sum = over_seq(rest_tiles, 144, "add_rest_seq").reshape(6, 384, 128)
    tail_sum = over_seq(tail_tiles, 96, "add_tail_seq")
    dwin, dwdt, dwout, dcw, dcb, dgo, dgi, ddtb, dal, dds = call(
        finish,
        "finish",
        [(V, rest_sum), (V, tail_sum)],
        [shape(96, E + C), shape(96, 2 * H), shape(192, D), shape(4, C), shape(1, C)]
        + [shape(1, E), shape(1, D), shape(1, 2 * H), shape(1, H), shape(1, H)],
    )
    flat = lambda v: v.reshape(-1)
    return (
        out[None], dtok[None], flat(dgi), dwin, dwdt, dcw, flat(dcb), flat(ddtb), flat(dal),
        flat(dds), flat(dgo), dwout,
    )


def solution(mesh):
    split = P("dp", "seq", None)
    rows = P("dp", None)
    return jax.shard_map(
        local,
        mesh=mesh,
        in_specs=(split, P("dp", "seq"), P(), rows, rows, P(), P(), P(), P(), P(), P(), rows, split),
        out_specs=(split, split, P(), rows, rows, P(), P(), P(), P(), P(), P(), rows),
        check_vma=False,
    )
```

```python
from functools import partial

import jax
import jax.numpy as jnp
from jax import lax
from jax.experimental import pallas as pl
from jax.experimental.pallas import tpu as pltpu
from jax.sharding import PartitionSpec as P

F32, BF = jnp.float32, jnp.bfloat16
EPS = 1e-05
LOG2E = 1.4426950408889634
D, H, E, N, T = 768, 24, 1536, 64, 256
C = E + 4 * N
CD = C + 128
HALO = 16
WIDE = E // 256
DP, SEQ = 8, 16
VMEM = 56 * 1024 * 1024
SMALL = 12 * 1024 * 1024


def iota(shape, dim):
    return lax.broadcasted_iota(jnp.int32, shape, dim)


def mm(a, b):
    return jnp.dot(a, b, preferred_element_type=F32)


def mm_nt(a, b):
    return lax.dot_general(a, b, (((1,), (1,)), ((), ())), preferred_element_type=F32)


def flip(v):
    return v.astype(F32).T.astype(v.dtype)


def sigmoid(v):
    return 1.0 / (1.0 + jnp.exp(-v))


def silu(v):
    return v * sigmoid(v)


def split2(v):
    hi = v.astype(BF)
    return hi, (v - hi.astype(F32)).astype(BF)


def pair(v):
    return jnp.concatenate(split2(v), axis=1)


def onehot(cond):
    return jnp.where(cond, 1.0, 0.0).astype(BF)


def marks():
    columns = onehot((iota((256, E), 0) & 127) == (iota((256, E), 1) >> 6))
    return columns, onehot((iota((E, 128), 0) >> 6) == iota((E, 128), 1))


def to_front(v):
    return pltpu.roll(v, 128 - H, 1)


def to_back(v):
    return pltpu.roll(v, H, 1)


def pairs_of(v):
    return pair(v), pair(to_front(v))


def tri_sum(mask, v):
    hi = v.astype(BF)
    rest = v - hi.astype(F32)
    mid = rest.astype(BF)
    low = (rest - mid.astype(F32)).astype(BF)
    return mm(mask, hi) + mm(mask, mid) + mm(mask, low)


def tri(cond):
    return onehot(cond(iota((T, T), 0), iota((T, T), 1)))


def lanes(rows=T):
    return iota((rows, 128), 1)


def wide(i):
    return pl.ds(pl.multiple_of(i * 256, 256), 256)


def fetch(sources, sems, tiles=WIDE):
    def copies(i):
        return [
            pltpu.make_async_copy(src.at[:, wide(i)], dst.at[:, wide(i)], sems.at[k, i])
            for k, (src, dst) in enumerate(sources)
        ]

    for i in range(tiles):
        for copy in copies(i):
            copy.start()

    def wait(i):
        for copy in copies(i):
            copy.wait()

    return wait


def parts_of_bc(act):
    return [act[:, N * k : N * k + N].astype(BF) for k in range(4)]


def ends(cum):
    return jnp.where(lanes(1) < H, cum[T - 1 : T], cum[0:1])


def put_slices(pay, i, first, second, dec_first, dec_second):
    row = iota((16, 128), 0)
    for e in range(2):
        at = slice(128 * e, 128 * e + 128)
        tile = 2 * i + e
        group = lax.div(tile, 3)
        into = pl.ds(pl.multiple_of(lax.rem(tile, 3) * 128, 128), 128)
        a, b = dec_first[:, at], dec_second[:, at]
        ah, bh = a.astype(BF).astype(F32), b.astype(BF).astype(F32)
        dec = jnp.where(
            row == 0, ah, jnp.where(row == 1, a - ah, jnp.where(row == 2, bh, b - bh))
        )
        dec = jnp.where(row < 4, dec, 0.0).astype(BF)
        for q in range(4):
            j = 4 * group + q
            pay[j, 0:16, into] = first[16 * q : 16 * q + 16, at].astype(BF)
            pay[j, 16:32, into] = second[16 * q : 16 * q + 16, at].astype(BF)
            pay[j, 32:48, into] = dec


def take_slices(recv, first, second, first_scale):
    for j in range(SEQ):
        rows, at = pl.ds(16 * (j % 4), 16), pl.ds(384 * (j // 4), 384)
        first[rows, at] = (recv[j, 0:16].astype(F32) * first_scale).astype(BF)
        second[rows, at] = recv[j, 16:32]


def load_weights(ids, parts, w, sem):
    copies = [
        pltpu.make_async_copy(
            parts[k], w.at[pl.ds(pl.multiple_of(ids[k] * 96, 32), 96)], sem.at[k]
        )
        for k in range(8)
    ]
    for copy in copies:
        copy.start()
    return copies


def load_rest(rest, wg, wo, sem):
    gates, outs = [], []
    for p in range(DP):
        at = 384 * p
        if wg is not None:
            gates.append((rest.at[pl.ds(at, 96)], wg.at[0, pl.ds(96 * p, 96)]))
            gates.append((rest.at[pl.ds(at + 96, 96)], wg.at[1, pl.ds(96 * p, 96)]))
        if wo is not None:
            outs.append((rest.at[pl.ds(at + 192, 192)], wo.at[pl.ds(192 * p, 192)]))
    copies = [pltpu.make_async_copy(a, b, sem.at[k]) for k, (a, b) in enumerate(gates + outs)]
    for copy in copies:
        copy.start()
    return copies[: len(gates)], copies[len(gates) :]


def finish_all(copies):
    for copy in copies:
        copy.wait()


def front(ids, cont, tok, halo, gin, cw, cb, dtb, alog, hc, *refs):
    parts, outs, (w, cif, csv, civ, sem, osem) = refs[:8], refs[8:15], refs[15:]
    u_out, ci_out, cs_out, sraw_out, dt_out, cum_out, pay = outs
    copies = load_weights(ids, parts, w, sem)
    x = jnp.concatenate([halo[...], tok[...]], axis=0).astype(F32)
    u = x * lax.rsqrt(jnp.mean(x * x, axis=1, keepdims=True) + EPS) * gin[...]
    u_out[...] = u.astype(BF)
    keep = cont[0]
    mask = jnp.where(iota((HALO + T, 1), 0) < HALO, keep, 1.0)
    finish_all(copies)
    sraw = mm(u_out[HALO:, :], w[:, C:]) + dtb[...]
    sraw_out[...] = sraw
    dt = jnp.maximum(sraw, 0.0) + jnp.log1p(jnp.exp(-jnp.abs(sraw)))
    dt = jnp.where(lanes() < 2 * H, dt, 0.0)
    dt_out[...] = dt
    rate = jnp.where(lanes(1) < 2 * H, jnp.exp(alog[...]), 0.0)
    la = -dt * rate
    cum = jnp.where(
        lanes() < H,
        tri_sum(tri(lambda r, c: r >= c), la),
        tri_sum(tri(lambda r, c: r <= c), la),
    )
    cum_out[...] = cum
    last = ends(cum)
    tail_f, tail_r = pairs_of(jnp.exp(last - cum) * dt)
    dec_f, dec_r = pairs_of(jnp.broadcast_to(jnp.exp(last) * keep, (16, 128)))

    def outward(i):
        at = wide(i)
        return [
            pltpu.make_async_copy(csv.at[:, at], cs_out.at[:, at], osem.at[0, i]),
            pltpu.make_async_copy(civ.at[:, at], ci_out.at[:, at], osem.at[1, i]),
        ]

    def convolve(i):
        at = wide(i)
        ci = (mm(u_out[...], w[:, at]) * mask).astype(BF)
        civ[:, at] = ci
        for e in range(2):
            here = pl.ds(pl.multiple_of(i * 256 + 128 * e, 128), 128)
            cif[e] = ci[:, 128 * e : 128 * e + 128].astype(F32)
            total = cb[:, here]
            for k in range(4):
                total = total + cw[k : k + 1, here] * cif[e, HALO - 3 + k : HALO - 3 + k + T]
            csv[:, here] = total
        for copy in outward(i):
            copy.start()
        return silu(csv[:, at])

    bf, _, br, _ = parts_of_bc(convolve(WIDE))
    bf_t, br_t = flip(bf), flip(br)

    def tile(i, _):
        at = wide(i)
        x_act = convolve(i)
        sf = mm(bf_t, (mm(tail_f, hc[:, at]) * x_act).astype(BF))
        sr = mm(br_t, (mm(tail_r, hc[:, at]) * x_act).astype(BF)) * keep
        put_slices(pay, i, sf, sr, mm(dec_f, hc[:, at]), mm(dec_r, hc[:, at]))
        return 0

    lax.fori_loop(0, WIDE, tile, 0)
    for i in range(WIDE + 1):
        finish_all(outward(i))


def scan_blocks(recv, out):
    carry = jnp.zeros((16, 384), F32)
    back = jnp.zeros((16, 384), F32)
    for i in range(SEQ):
        k = SEQ - 1 - i
        out[i, 0:16] = carry.astype(BF)
        out[k, 16:32] = back.astype(BF)
        dec = recv[i, 32:48].astype(F32)
        carry = (dec[0:1] + dec[1:2]) * carry + recv[i, 0:16].astype(F32)
        dec = recv[k, 32:48].astype(F32)
        back = (dec[2:3] + dec[3:4]) * back + recv[k, 16:32].astype(F32)


def columns_of(cum2, col, base=0):
    for h in range(col.shape[0]):
        col[h] = jnp.broadcast_to(cum2[:, base + h : base + h + 1], (T, 128))


def by_head(v):
    head = iota((T, 256), 1) >> 6
    return [jnp.where(head == e, v, 0.0).astype(BF) for e in range(4)]


def low_full(left, right):
    right = jnp.concatenate([jnp.zeros((128, 128), right.dtype), right], axis=0)
    return jnp.concatenate([left, right], axis=1)


def up_full(left, right):
    left = jnp.concatenate([left, jnp.zeros((128, 128), left.dtype)], axis=0)
    return jnp.concatenate([left, right], axis=1)


def local_mix(forward, cs, dt, cum, hc, *refs):
    if forward:
        y, csv, ysv, hcv, col, row, g, sem, osem = refs
    else:
        ylf, dsk, y, base_out, csv, ysv, yfv, bsv, hcv, col, row, g, sem, osem = refs
    hc_copy = pltpu.make_async_copy(hc, hcv, sem.at[2, 1])
    hc_copy.start()
    first = 0 if forward else H
    bc = pltpu.make_async_copy(cs.at[:, E:], csv.at[:, E:], sem.at[2, 0])
    bc.start()
    wait = fetch([(cs, csv)] if forward else [(cs, csv), (ylf, yfv)], sem)
    cum2 = cum[...] * LOG2E
    row[...] = cum2.T
    columns_of(cum2, col, first)
    dt2 = pairs_of(dt[...])[0 if forward else 1]
    bc.wait()
    parts = parts_of_bc(silu(csv[:, E:]))
    b, cc = parts[:2] if forward else parts[2:]
    r, c = iota((T, T), 0), iota((T, T), 1)
    g[...] = jnp.where(r > c if forward else r < c, mm_nt(cc, b), 0.0)
    hc_copy.wait()

    def weights(h):
        at, along = col[h], row[pl.ds(first + h, 1), :]
        if forward:
            left = jnp.exp2(jnp.minimum(at - along[:, :128], 0.0)) * g[:, :128]
            right = jnp.exp2(jnp.minimum(at[128:] - along[:, 128:], 0.0)) * g[128:, 128:]
            return low_full(left.astype(BF), right.astype(BF))
        left = jnp.exp2(jnp.minimum(at[:128] - along[:, :128], 0.0)) * g[:128, :128]
        right = jnp.exp2(jnp.minimum(at - along[:, 128:], 0.0)) * g[:, 128:]
        return up_full(left.astype(BF), right.astype(BF))

    def outward(i):
        pairs = [(ysv, y)] if forward else [(ysv, y), (bsv, base_out)]
        return [
            pltpu.make_async_copy(a.at[:, wide(i)], b.at[:, wide(i)], osem.at[k, i])
            for k, (a, b) in enumerate(pairs)
        ]

    def tile(i, _):
        at = wide(i)
        wait(i)
        x = silu(csv[:, at])
        xs = by_head(x * mm(dt2, hcv[:, at]))
        left = jnp.concatenate([weights(4 * i + e) for e in range(4)], axis=1)
        own = mm(left, jnp.concatenate(xs, axis=0))
        ysv[:, at] = own.astype(BF)
        if not forward:
            bsv[:, at] = own + yfv[:, at].astype(F32) + dsk[:, at] * x
        for copy in outward(i):
            copy.start()
        return 0

    lax.fori_loop(0, WIDE, tile, 0)
    for i in range(WIDE):
        finish_all(outward(i))


def gate_products(u, dout, rest, gate, dn, wg, wo, sem):
    gates, outs = load_rest(rest, wg, wo, sem)
    finish_all(gates)
    gate[:, :D] = mm(u[HALO:, :], wg[0])
    gate[:, D:] = mm(u[HALO:, :], wg[1])
    finish_all(outs)
    dn[...] = mm_nt(dout[...], wo[...])


def gated_norm(cont, cum, recv, gout, hc, cs, base, gate, dn, *refs):
    (n16, dg16, dm16, dgout, pay), scratch = refs[:5], refs[5:]
    bcv, yv, gv, dv, gds, eff, efr, nv, dgv, dmv, sf, sr, bsem, sem, osem = scratch
    bc = pltpu.make_async_copy(cs.at[:, E:], bcv, bsem)
    bc.start()
    wait = fetch([(base, yv), (gate, gv), (dn, dv)], sem)
    keep = cont[0]
    take_slices(recv, sf, sr, keep)
    cumv = cum[...]
    ef_f, ef_r = pairs_of(jnp.exp(cumv))
    dec_f, dec_r = pairs_of(jnp.broadcast_to(jnp.exp(ends(cumv)) * keep, (16, 128)))
    bc.wait()
    _, cf, _, cr = parts_of_bc(silu(bcv[...]))
    zero = jnp.zeros((T, 128), F32)

    def first(i, sums):
        at = wide(i)
        wait(i)
        ef, er = mm(ef_f, hc[:, at]), mm(ef_r, hc[:, at])
        eff[:, at] = ef
        efr[:, at] = er
        m = yv[:, at] + ef * mm(cf, sf[:, at]) + er * mm(cr, sr[:, at])
        g = gv[:, at]
        sg = sigmoid(g)
        sl = g * sg
        gd = m * sl
        gds[:, at] = gd
        gv[:, at] = sl
        yv[:, at] = m * sg * (1.0 + g * (1.0 - sg))
        squares, crossed = gd * gd, dv[:, at] * gout[:, at] * gd
        return (
            sums[0] + squares[:, :128] + squares[:, 128:],
            sums[1] + crossed[:, :128] + crossed[:, 128:],
        )

    squares, crossed = lax.fori_loop(0, WIDE, first, (zero, zero))
    rs = lax.rsqrt(jnp.sum(squares, axis=1, keepdims=True) / E + EPS)
    pull = jnp.sum(crossed, axis=1, keepdims=True) / E * (rs * rs * rs)
    cf_t, cr_t = flip(cf), flip(cr)

    def outward(i):
        return [
            pltpu.make_async_copy(a.at[:, wide(i)], b.at[:, wide(i)], osem.at[k, i])
            for k, (a, b) in enumerate([(nv, n16), (dgv, dg16), (dmv, dm16)])
        ]

    def second(i, _):
        at = wide(i)
        gd = gds[:, at]
        gdr = gd * rs
        go = gout[:, at]
        nv[:, at] = (gdr * go).astype(BF)
        d = dv[:, at]
        dgout[:, at] = jnp.sum(d * gdr, axis=0, keepdims=True)
        dgd = rs * (d * go) - gd * pull
        dgv[:, at] = (dgd * yv[:, at]).astype(BF)
        dm = dgd * gv[:, at]
        dmv[:, at] = dm.astype(BF)
        for copy in outward(i):
            copy.start()
        lf = mm(cf_t, (eff[:, at] * dm).astype(BF)) * keep
        lr = mm(cr_t, (efr[:, at] * dm).astype(BF))
        put_slices(pay, i, lr, lf, mm(dec_r, hc[:, at]), mm(dec_f, hc[:, at]))
        return 0

    lax.fori_loop(0, WIDE, second, 0)
    for i in range(WIDE):
        finish_all(outward(i))


def pieces_out(ids, sources, keep, send, sem):
    copies = []
    for ref, base in ((send, 12), (keep, 8)):
        for k in range(4):
            for src, rows, put in sources:
                start = pl.multiple_of(ids[base + k] * rows, 32)
                copies.append((src.at[pl.ds(start, rows)], put(ref, k)))
    return [pltpu.make_async_copy(a, b, sem.at[k]) for k, (a, b) in enumerate(copies)]


def out_and_rows(
    ids, cont, tok, u, dout, n16, dg16, dm16, cum, recv, hc, hr, rest, cs, ylf, ylr, *refs
):
    (out, rows, dc, keep, send), scratch = refs[:5], refs[5:]
    wo, n_t, u_t, dwo, dwg, bcv, yfv, yrv, sf, sr, bsem, sem, wsem, osem = scratch
    bc = pltpu.make_async_copy(cs.at[:, E:], bcv, bsem)
    bc.start()
    wait = fetch([(ylf, yfv), (ylr, yrv)], sem)
    _, copies = load_rest(rest, None, wo, wsem)
    n_t[...] = flip(n16[...])
    u_t[...] = flip(u[HALO:, :])

    def rows_out(i, _):
        at = pl.ds(pl.multiple_of(i * 256, 256), 256)
        dwo[at, :] = mm(n_t[at, :], dout[...]).astype(BF)
        return 0

    def rows_gate(i, _):
        at = pl.ds(pl.multiple_of(i * 256, 256), 256)
        dwg[at, :] = mm(u_t[at, :], dg16[...]).astype(BF)
        return 0

    lax.fori_loop(0, E // 256, rows_out, 0)
    lax.fori_loop(0, D // 256, rows_gate, 0)
    outward = pieces_out(
        ids,
        [
            (dwg.at[:, :D], 96, lambda ref, k: ref.at[k, 0:96]),
            (dwg.at[:, D:], 96, lambda ref, k: ref.at[k, 96:192]),
            (dwo, 192, lambda ref, k: ref.at[k, 192:384]),
        ],
        keep,
        send,
        osem,
    )
    for copy in outward:
        copy.start()
    take_slices(recv, sf, sr, cont[0])
    ef_f, ef_r = pairs_of(jnp.exp(cum[...]))
    bc.wait()
    _, cf, _, cr = parts_of_bc(silu(bcv[...]))

    def tile(i, sums):
        at = wide(i)
        wait(i)
        dm = dm16[:, at].astype(F32)
        new = []
        for ef2, c, s, yl in ((ef_f, cf, sf, yfv), (ef_r, cr, sr, yrv)):
            ef = mm(ef2, hc[:, at])
            y = yl[:, at].astype(F32) + ef * mm(c, s[:, at])
            new.append(mm((dm * y).astype(BF), hr[at, :]))
            new.append(mm_nt((ef * dm).astype(BF), s[:, at]))
        return tuple(a + b for a, b in zip(sums, new))

    zero, zn = jnp.zeros((T, 128), F32), jnp.zeros((T, N), F32)
    rf, dcf, rr, dcr = lax.fori_loop(0, WIDE, tile, (zero, zn, zero, zn))
    rows[...] = rf + to_back(rr)
    dc[...] = jnp.concatenate([dcf, dcr], axis=1)
    finish_all(copies)
    out[...] = (tok[...].astype(F32) + mm(n16[...], wo[...])).astype(BF)
    finish_all(outward)


def local_back(dt, cum, dm16, hc, cs, zf, zr, dgf, dgr, *scratch):
    csv, zfv, zrv, col, row, gf, gr, dm_t, sem, osem = scratch
    bc = pltpu.make_async_copy(cs.at[:, E:], csv.at[:, E:], sem.at[0, WIDE])
    bc.start()
    wait = fetch([(cs, csv)], sem)
    cum2 = cum[...] * LOG2E
    row[...] = cum2.T
    columns_of(cum2, col)
    dm_t[...] = flip(dm16[...])
    dt_f, dt_r = pairs_of(dt[...])
    bc.wait()
    bf, cf, br, cr = parts_of_bc(silu(csv[:, E:]))
    s, t = iota((T, T), 0), iota((T, T), 1)
    gf[...] = jnp.where(t > s, mm_nt(bf, cf), 0.0)
    gr[...] = jnp.where(t < s, mm_nt(br, cr), 0.0)
    dgf[...] = jnp.zeros((T, T), F32)
    dgr[...] = jnp.zeros((T, T), F32)

    def outward(i):
        return [
            pltpu.make_async_copy(a.at[:, wide(i)], b.at[:, wide(i)], osem.at[k, i])
            for k, (a, b) in enumerate([(zfv, zf), (zrv, zr)])
        ]

    def tile(i, _):
        at = wide(i)
        wait(i)
        x = silu(csv[:, at])
        ds = jnp.concatenate(by_head(dm16[:, at].astype(F32)), axis=0)
        dms = dm_t[at, :]
        for forward in (True, False):
            first = 0 if forward else H
            xs = by_head(x * mm(dt_f if forward else dt_r, hc[:, at]))
            ws = []
            small = jnp.zeros((128, 128), F32)
            large = jnp.zeros((T, 128), F32)
            for e in range(4):
                h = first + 4 * i + e
                at_s, along = col[h], row[pl.ds(h, 1), :]
                dw = mm(xs[e], dms)
                if forward:
                    ea = jnp.exp2(jnp.minimum(along[:, :128] - at_s[:128], 0.0))
                    eb = jnp.exp2(jnp.minimum(along[:, 128:] - at_s, 0.0))
                    ws.append(
                        up_full((ea * gf[:128, :128]).astype(BF), (eb * gf[:, 128:]).astype(BF))
                    )
                    small = small + ea * dw[:128, :128]
                    large = large + eb * dw[:, 128:]
                else:
                    ea = jnp.exp2(jnp.minimum(along[:, :128] - at_s, 0.0))
                    eb = jnp.exp2(jnp.minimum(along[:, 128:] - at_s[128:], 0.0))
                    ws.append(
                        low_full((ea * gr[:, :128]).astype(BF), (eb * gr[128:, 128:]).astype(BF))
                    )
                    large = large + ea * dw[:, :128]
                    small = small + eb * dw[128:, 128:]
            total = mm(jnp.concatenate(ws, axis=1), ds)
            if forward:
                zfv[:, at] = total.astype(BF)
                dgf[:128, :128] += small
                dgf[:, 128:] += large
            else:
                zrv[:, at] = total.astype(BF)
                dgr[:, :128] += large
                dgr[128:, 128:] += small
        for copy in outward(i):
            copy.start()
        return 0

    lax.fori_loop(0, WIDE, tile, 0)
    dgf[...] = jnp.where(t > s, dgf[...], 0.0)
    dgr[...] = jnp.where(t < s, dgr[...], 0.0)
    for i in range(WIDE):
        finish_all(outward(i))


def inner_back(
    ids, cont, tok, halo, gin, cw, alog, dsk, sraw, dt, cum, u, dout, dgf, dgr, back, fore, rows,
    dc, dgout, hc, hr, cs, zf, zr, dm16, ci, dg16, rest, *refs
):
    parts, (dtok, dhalo, dall, small_out), scratch = refs[:8], refs[8:12], refs[12:]
    csv, zfv, zrv, dmv, civ, dgv, w, wg, sf, sr, kf, kr, dcs, cif, du, small = scratch[:16]
    line, sem, csem, wsem, gsem, dsem = scratch[16:]
    bcc = pltpu.make_async_copy(cs.at[:, E:], csv.at[:, E:], csem.at[1])
    bcc.start()
    wait = fetch([(cs, csv), (zf, zfv), (zr, zrv), (dm16, dmv)], sem)
    cic = pltpu.make_async_copy(ci, civ, csem.at[0])
    cic.start()
    loads = load_weights(ids, parts, w, wsem) + load_rest(rest, wg, None, gsem)[0]
    loads.append(pltpu.make_async_copy(dg16, dgv, dsem))
    loads[-1].start()
    keep = cont[0]
    take_slices(back, kr, kf, keep)
    take_slices(fore, sf, sr, keep)
    cumv, dtv = cum[...], dt[...]
    last = ends(cumv)
    te_f, te_r = pairs_of(jnp.exp(last - cumv))
    dt_f, dt_r = pairs_of(dtv)
    line[...] = jnp.zeros((8, E), F32)
    dcs[:, 0:HALO] = jnp.zeros((C // 128, HALO, 128), F32)
    dcs[:, HALO + T :] = jnp.zeros((C // 128, 16, 128), F32)
    bcc.wait()
    bc = csv[:, E:]
    bf, cf, br, cr = parts_of_bc(silu(bc))

    def slope(v, sg):
        return sg * (1.0 + v * (1.0 - sg))

    def tile(i, sums):
        at = wide(i)
        wait(i)
        v = csv[:, at]
        sg = sigmoid(v)
        x = v * sg
        dm = dmv[:, at].astype(F32)
        line[2:3, at] = jnp.sum(dm * x, axis=0, keepdims=True)
        dx = dsk[:, at] * dm
        new = []
        for d, dt2, te2, z, k, s, b in (
            (0, dt_f, te_f, zfv, kf, sf, bf),
            (1, dt_r, te_r, zrv, kr, sr, br),
        ):
            dts, te = mm(dt2, hc[:, at]), mm(te2, hc[:, at])
            xd = (x * dts).astype(BF).astype(F32)
            zi, zt = z[:, at].astype(F32), te * mm(b, k[:, at])
            dx = dx + dts * (zi + zt)
            new.append(mm((xd * zi).astype(BF), hr[at, :]))
            new.append(mm((xd * zt).astype(BF), hr[at, :]))
            new.append(mm_nt((te * xd).astype(BF), k[:, at]))
            both = s[:, at].astype(F32) * k[:, at].astype(F32)
            line[d : d + 1, at] = jnp.sum(both, axis=0, keepdims=True)
        dx = dx * slope(v, sg)
        for e in range(2):
            dcs[2 * i + e, HALO : HALO + T] = dx[:, 128 * e : 128 * e + 128]
        return tuple(a + b for a, b in zip(sums, new))

    zero, zn = jnp.zeros((T, 128), F32), jnp.zeros((T, N), F32)
    sums = lax.fori_loop(0, WIDE, tile, (zero, zero, zn, zero, zero, zn))
    inner, tails = sums[0] + to_back(sums[3]), sums[1] + to_back(sums[4])
    gf16, gr16 = dgf[...].astype(BF), dgr[...].astype(BF)
    dbf = sums[2] + mm(gf16, cf)
    dbr = sums[5] + mm(gr16, cr)
    dcf = dc[:, :N] + mm(flip(gf16), bf)
    dcr = dc[:, N:] + mm(flip(gr16), br)
    dbc = jnp.concatenate([dbf, dcf, dbr, dcr], axis=1) * slope(bc, sigmoid(bc))
    for e in range(2):
        dcs[2 * WIDE + e, HALO : HALO + T] = dbc[:, 128 * e : 128 * e + 128]
    hi, lo = split2(line[...])
    heads = mm(hi, hr[...]) + mm(lo, hr[...])
    dots = heads[0:1] + to_back(heads)[1:2]
    rate = jnp.where(lanes(1) < 2 * H, jnp.exp(alog[...]), 0.0)
    v = rows[...] - inner
    dla = jnp.where(
        lanes() < H,
        tri_sum(tri(lambda r, c: r <= c), v) + tri_sum(tri(lambda r, c: r > c), tails),
        tri_sum(tri(lambda r, c: r >= c), v) + tri_sum(tri(lambda r, c: r < c), tails),
    ) + jnp.exp(last) * dots
    sg = sigmoid(sraw[...])
    ratio = jnp.where(dtv > 1e-20, sg / jnp.maximum(dtv, 1e-20), 1.0)
    dstep = (inner + tails) * ratio - dla * rate * sg
    dstep = jnp.where(lanes() < 2 * H, dstep, 0.0)
    dall[0:HALO, C:] = jnp.zeros((HALO, 128), BF)
    dall[HALO:, C:] = dstep.astype(BF)
    dal = jnp.broadcast_to(jnp.sum(dla * (-dtv * rate), axis=0, keepdims=True), (8, 128))
    small[...] = jnp.zeros((96, 128), F32)
    small[88:89] = jnp.sum(dstep, axis=0, keepdims=True)
    small[89:90] = jnp.where(lanes(1) < H, dal[0:1] + to_front(dal)[0:1], 0.0)
    small[90:91] = jnp.where(lanes(1) < H, heads[2:3], 0.0)
    mask = jnp.where(iota((HALO + T, 1), 0) < HALO, keep, 1.0)

    cic.wait()

    def convolution(i, _):
        at = pl.ds(pl.multiple_of(i * 128, 128), 128)
        g = dcs[i, HALO : HALO + T]
        cif[...] = civ[:, at].astype(F32)
        small[pl.ds(56 + i, 1)] = jnp.sum(g, axis=0, keepdims=True)
        total = jnp.zeros((HALO + T, 128), F32)
        for k in range(4):
            shifted = cif[HALO - 3 + k : HALO - 3 + k + T]
            small[pl.ds(14 * k + i, 1)] = jnp.sum(g * shifted, axis=0, keepdims=True)
            total = total + cw[k : k + 1, at] * dcs[i, 3 - k : 3 - k + HALO + T]
        dall[:, at] = (total * mask).astype(BF)
        return 0

    lax.fori_loop(0, C // 128, convolution, 0)
    for j in range(E // 128):
        small[70 + j : 71 + j] = dgout[:, 128 * j : 128 * j + 128]
    finish_all(loads)

    def input_grad(i, _):
        at = wide(i)
        du[:, at] = mm_nt(dall[...], w[at, :])
        du[HALO:, at] += mm_nt(dgv[:, :D], wg[0, at, :]) + mm_nt(dgv[:, D:], wg[1, at, :])
        return 0

    lax.fori_loop(0, D // 256, input_grad, 0)
    x = jnp.concatenate([halo[...], tok[...]], axis=0).astype(F32)
    r = lax.rsqrt(jnp.mean(x * x, axis=1, keepdims=True) + EPS)
    duxr = jnp.sum(du[...] * x * r, axis=0, keepdims=True)
    for j in range(6):
        small[82 + j : 83 + j] = duxr[:, 128 * j : 128 * j + 128]
    small_out[...] = small[...].astype(BF)
    dxh = du[...] * gin[...]
    dx = r * dxh - x * (r * r * r * jnp.mean(dxh * x, axis=1, keepdims=True))
    dhalo[...] = dx[:HALO]
    dtok[...] = dout[...].astype(F32) + dx[HALO:]


def weight_back(ids, u, dall, small, keep, send, u_t, dw, osem, ssem):
    u_t[...] = flip(u[...])
    extra = []
    for ref, base in ((send, 0), (keep, 4)):
        for k in range(4):
            extra.append(
                pltpu.make_async_copy(small, ref.at[k, :, pl.ds(CD, 128)], ssem.at[base + k])
            )
            extra[-1].start()

    def rows(i, _):
        at = pl.ds(pl.multiple_of(i * 256, 256), 256)
        dw[at, :] = mm(u_t[at, :], dall[...]).astype(BF)
        return 0

    lax.fori_loop(0, D // 256, rows, 0)
    copies = pieces_out(
        ids, [(dw, 96, lambda ref, k: ref.at[k, :, pl.ds(0, CD)])], keep, send, osem
    )
    for copy in copies:
        copy.start()
    finish_all(extra)
    finish_all(copies)


def add_pairs(a, b, *outs):
    for k in range(4):

        def rows(i, _, k=k):
            at = pl.ds(pl.multiple_of(i * 48, 16), 48)
            outs[k][at] = (a[k, at].astype(F32) + b[k, at].astype(F32)).astype(BF)
            return 0

        lax.fori_loop(0, a.shape[1] // 48, rows, 0)


def add_middle(one, up, three, down, out_one, out_three):
    half = one.shape[0] // 2
    for ref, part, out, at in ((one, up, out_one, 0), (three, down, out_three, half)):
        for r in range(0, 2 * half, 48):
            rows = slice(r, r + 48)
            total = ref[rows].astype(F32)
            if at <= r < at + half:
                total = total + part[r - at : r - at + 48].astype(F32)
            out[rows] = total.astype(BF)


def add_y(*refs):
    rest, tail, out = refs[:3], refs[3:7], refs[7]

    def total(parts, rows, at):
        return sum(part[rows, at].astype(F32) for part in parts).astype(BF)

    for j in range(6):
        for r in range(0, 384, 48):
            row = 384 * j + r
            out[row // 144, row % 144 : row % 144 + 48] = total(
                rest, slice(r, r + 48), slice(128 * j, 128 * j + 128)
            )
    for j in range(SEQ):
        out[j, 144:] = total(tail, slice(0, 96), slice(128 * j, 128 * j + 128))


def add_blocks(recv, out):
    total = recv[0].astype(F32)
    for i in range(1, SEQ):
        total = total + recv[i].astype(F32)
    low = total.astype(BF)
    for i in range(SEQ):
        out[i] = low


def finish(sums, dwin, dwdt, dwout, dcw, dcb, dgout, dgin, ddtb, dal, ddsk):
    def put(ref, at, start, rows):
        for r in range(0, rows, 48):
            j, k = (start + r) // 144, (start + r) % 144
            ref[r : r + 48, at] = sums[j, k : k + 48].astype(F32)

    for j in range(6):
        at = slice(128 * j, 128 * j + 128)
        put(dwin, at, 384 * j, 96)
        put(dwin, slice(D + 128 * j, D + 128 * j + 128), 384 * j + 96, 96)
        put(dwout, at, 384 * j + 192, 192)
    for j in range(14):
        dwin[:, E + 128 * j : E + 128 * j + 128] = sums[j, 144:].astype(F32)
    dwdt[...] = sums[14, 144:, 0 : 2 * H].astype(F32)
    small = sums[15, 144:].astype(F32)
    for j in range(14):
        at = slice(128 * j, 128 * j + 128)
        for k in range(4):
            dcw[k : k + 1, at] = small[14 * k + j : 14 * k + j + 1]
        dcb[at] = small[56 + j]
    for j in range(E // 128):
        dgout[128 * j : 128 * j + 128] = small[70 + j]
    for j in range(6):
        dgin[128 * j : 128 * j + 128] = small[82 + j]
    ddtb[...] = small[88, 0 : 2 * H]
    dal[...] = small[89, 0:H]
    ddsk[...] = small[90, 0:H]


V = pl.BlockSpec(memory_space=pltpu.VMEM)
S = pl.BlockSpec(memory_space=pltpu.SMEM)
ANY = pl.BlockSpec(memory_space=pl.ANY)


def shape(*dims, dtype=F32):
    return jax.ShapeDtypeStruct(dims, dtype)


def call(kernel, name, ins, outs, scratch=(), flops=0, apart=(), limit=VMEM, light=False):
    specs, args = zip(*ins)
    moved = sum(a.size * a.dtype.itemsize for a in args)
    moved += sum(o.size * o.dtype.itemsize for o in outs)
    return pl.pallas_call(
        kernel,
        name=name,
        out_shape=tuple(outs),
        in_specs=list(specs),
        out_specs=tuple(ANY if i in apart else V for i in range(len(outs))),
        scratch_shapes=list(scratch),
        cost_estimate=pl.CostEstimate(
            flops=flops, bytes_accessed=0 if light else moved, transcendentals=0
        ),
        compiler_params=pltpu.CompilerParams(vmem_limit_bytes=limit),
    )(*args)


def vm(*dims, dtype=F32):
    return pltpu.VMEM(dims, dtype)


def shift_y(k):
    return [(2 * y + c, 2 * ((y + k) % 4) + c) for y in range(4) for c in range(2)]


SWAP = [(i, i ^ 1) for i in range(DP)]


def exchange(value):
    return lax.all_to_all(value, "seq", 0, 0, tiled=True)


def add_swapped(keep, send, name, after=None):
    recv = lax.ppermute(send, "dp", SWAP)
    if after is not None:
        recv = together(recv, after)[0]
    rows, cols = keep.shape[1:]
    outs = [shape(rows, cols, dtype=BF)] * 4
    return call(add_pairs, name, [(V, keep), (V, recv)], outs, limit=SMALL)


def over_y(parts):
    return [parts[0]] + [lax.ppermute(parts[k], "dp", shift_y(k)) for k in (1, 2, 3)]


def together(*values):
    return lax.optimization_barrier(values)


def local(
    tokens, starts, g_in, w_in, w_dt, conv_w, conv_b, dt_bias, a_log, dskip, g_out, w_out, d_out
):
    dp = lax.axis_index("dp")
    y, core = dp // 2, dp % 2
    tok, dout = tokens[0], d_out[0]
    cont = (1 - starts[0]).astype(F32)

    row = lambda v: v.reshape(1, -1)
    pad = lambda v: jnp.pad(v, (0, 128 - v.shape[0])).reshape(1, 128)
    alog = pad(jnp.concatenate([a_log, a_log]))
    dsk = row(jnp.repeat(dskip, N))
    gin, gout, cb, dtb = row(g_in), row(g_out), row(conv_b), pad(dt_bias)
    to_y = [(y + k) % 4 for k in range(4)]
    from_y = [(y - k) % 4 for k in range(4)]
    ids = [2 * t + core for t in from_y] + [2 * t + 1 - core for t in from_y]
    ids = jnp.stack(ids + [2 * t + core for t in to_y] + [2 * t + 1 - core for t in to_y])

    own = jnp.concatenate([w_in[:, E:], jnp.pad(w_dt, ((0, 0), (0, 128 - 2 * H)))], axis=1)
    column = [lax.ppermute(own, "dp", shift_y(k)) for k in (1, 2, 3)]
    halo = lax.ppermute(tok[-HALO:], "seq", [(i, i + 1) for i in range(SEQ - 1)])
    beside = lax.ppermute(own, "dp", SWAP)
    rest_own = jnp.concatenate([w_in[:, :D], w_in[:, D:E], w_out], axis=0)
    hc, hr = marks()
    *column, halo, beside, rest_own, alog, dsk, gin, gout, cb, dtb, ids, hc, hr = together(
        *column, halo, beside, rest_own, alog, dsk, gin, gout, cb, dtb, ids, hc, hr
    )
    parts = [own, *column, beside] + [lax.ppermute(part, "dp", SWAP) for part in column]
    rest = lax.all_gather(rest_own, "dp", axis=0, tiled=True)

    part_ins = [(ANY, part) for part in parts]
    w_scratch = vm(D, CD, dtype=BF)
    dma = pltpu.SemaphoreType.DMA
    full, half, state = vm(T, E), vm(T, E, dtype=BF), vm(N, E, dtype=BF)

    u, ci, cs, sraw, dt, cum, pay = call(
        front,
        "front",
        [(S, ids), (S, cont), (V, tok), (V, halo), (V, gin), (V, conv_w), (V, cb)]
        + [(V, dtb), (V, alog), (V, hc)]
        + part_ins,
        [shape(HALO + T, D, dtype=BF), shape(HALO + T, C, dtype=BF), shape(T, C)]
        + [shape(T, 128)] * 3
        + [shape(SEQ, 48, 384, dtype=BF)],
        [w_scratch, vm(2, HALO + T, 128), vm(T, C), vm(HALO + T, C, dtype=BF)]
        + [dma((8,)), dma((2, WIDE + 1))],
        flops=2 * T * D * CD,
        apart=(1, 2),
    )

    def scan(got, name):
        out = shape(SEQ, 32, 384, dtype=BF)
        return call(scan_blocks, name, [(V, got)], [out], limit=SMALL)[0]

    mix_scratch = [vm(256, E, dtype=BF), vm(H, T, 128), vm(128, T), vm(T, T)]
    mix_scratch += [dma((3, WIDE)), dma((2, WIDE))]
    mix_cost = 2 * 24 * T * T * 256
    got = exchange(pay)
    ylf = call(
        partial(local_mix, True),
        "mix_forward",
        [(ANY, cs), (V, dt), (V, cum), (ANY, hc)],
        [shape(T, E, dtype=BF)],
        [vm(T, C), half] + mix_scratch,
        flops=mix_cost,
        apart=(0,),
    )[0]
    ylr, base = call(
        partial(local_mix, False),
        "mix_reverse",
        [(ANY, cs), (V, dt), (V, cum), (ANY, hc), (ANY, ylf), (V, dsk)],
        [shape(T, E, dtype=BF), shape(T, E)],
        [vm(T, C), half, half, full] + mix_scratch,
        flops=mix_cost,
        apart=(0, 1),
    )
    got, ylr, base = together(got, ylr, base)
    fore = exchange(scan(got, "scan_states"))
    gate, dn = call(
        gate_products,
        "gate_products",
        [(V, u), (V, dout), (ANY, rest)],
        [shape(T, E)] * 2,
        [vm(2, D, D, dtype=BF), vm(E, D, dtype=BF), dma((24,))],
        flops=4 * T * D * E,
    )
    n16, dg16, dm16, dgout, pay_back = call(
        gated_norm,
        "gated_norm",
        [(S, cont), (V, cum), (V, fore), (V, gout), (V, hc)]
        + [(ANY, a) for a in (cs, base, gate, dn)],
        [shape(T, E, dtype=BF)] * 3 + [shape(1, E), shape(SEQ, 48, 384, dtype=BF)],
        [vm(T, 256)] + [full] * 6 + [half] * 3 + [state] * 2
        + [dma(()), dma((3, WIDE)), dma((3, WIDE))],
        flops=12 * T * N * E,
        apart=(0, 1, 2),
    )
    got = exchange(pay_back)
    out, rows, dc, rest_keep, rest_send = call(
        out_and_rows,
        "out_and_rows",
        [(S, ids), (S, cont)]
        + [(V, a) for a in (tok, u, dout, n16, dg16, dm16, cum, fore, hc, hr)]
        + [(ANY, a) for a in (rest, cs, ylf, ylr)],
        [shape(T, D, dtype=BF), shape(T, 128), shape(T, 128)] + [shape(4, 384, D, dtype=BF)] * 2,
        [vm(E, D, dtype=BF), vm(E, T, dtype=BF), vm(D, T, dtype=BF), vm(E, D, dtype=BF)]
        + [vm(D, E, dtype=BF), vm(T, 256), half, half, state, state]
        + [dma(()), dma((2, WIDE)), dma((8,)), dma((24,))],
        flops=8 * T * D * E,
        apart=(3, 4),
    )
    got, out, rows, rest_keep, rest_send = together(got, out, rows, rest_keep, rest_send)
    scanned = scan(got, "scan_adjoints")
    back = exchange(scanned)
    rest_parts = add_swapped(rest_keep, rest_send, "add_rest_cores", scanned)
    dm16, *rest_parts = together(dm16, *rest_parts)
    half_up = lax.ppermute(rest_parts[2][:192], "dp", shift_y(1))
    half_down = lax.ppermute(rest_parts[2][192:], "dp", shift_y(3))
    zf, zr, dgf, dgr = call(
        local_back,
        "local_back",
        [(V, dt), (V, cum), (V, dm16), (V, hc), (ANY, cs)],
        [shape(T, E, dtype=BF)] * 2 + [shape(T, T)] * 2,
        [vm(T, C), half, half, vm(2 * H, T, 128), vm(128, T), vm(T, T), vm(T, T)]
        + [vm(E, T, dtype=BF), dma((1, WIDE + 1)), dma((2, WIDE))],
        flops=4 * 48 * T * T * 256,
        apart=(0, 1),
    )
    back, zf, half_up, half_down = together(back, zf, half_up, half_down)
    up, down = call(
        add_middle,
        "add_rest_middle",
        [(V, rest_parts[1]), (V, half_up), (V, rest_parts[3]), (V, half_down)],
        [shape(384, D, dtype=BF)] * 2,
        limit=SMALL,
    )
    zf, up, down = together(zf, up, down)
    rest_parts = [
        rest_parts[0], lax.ppermute(up, "dp", shift_y(1)), lax.ppermute(down, "dp", shift_y(3))
    ]
    dtok, dhalo, dall, small = call(
        inner_back,
        "inner_back",
        [(S, ids), (S, cont)]
        + [(V, a) for a in (tok, halo, gin, conv_w, alog, dsk, sraw, dt, cum, u, dout, dgf, dgr)]
        + [(V, a) for a in (back, fore, rows, dc, dgout, hc, hr)]
        + [(ANY, a) for a in (cs, zf, zr, dm16, ci, dg16, rest)]
        + part_ins,
        [shape(T, D), shape(HALO, D), shape(HALO + T, CD, dtype=BF), shape(96, 128, dtype=BF)],
        [vm(T, C), half, half, half, vm(HALO + T, C, dtype=BF), half, w_scratch]
        + [vm(2, D, D, dtype=BF)]
        + [state] * 4
        + [vm(C // 128, HALO + T + 16, 128), vm(HALO + T, 128), vm(HALO + T, D), vm(96, 128)]
        + [vm(8, E), dma((4, WIDE)), dma((2,)), dma((8,)), dma((16,)), dma(())],
        flops=2 * T * D * (CD + E),
    )
    dall, *rest_parts = together(dall, *rest_parts)
    keep, send = call(
        weight_back,
        "weight_back",
        [(S, ids), (V, u), (V, dall), (V, small)],
        [shape(4, 96, 2048, dtype=BF)] * 2,
        [vm(D, HALO + T, dtype=BF), w_scratch, dma((8,)), dma((8,))],
        flops=2 * T * D * CD,
        apart=(0, 1),
    )
    tail_parts = over_y(add_swapped(keep, send, "add_tail_cores"))
    dback = lax.ppermute(dhalo, "seq", [(i + 1, i) for i in range(SEQ - 1)])
    dtok = dtok.at[-HALO:].add(dback)
    *tail_parts, dtok = together(*tail_parts, dtok)
    slices = shape(SEQ, 240, 128, dtype=BF)
    sums = [(V, part) for part in (*rest_parts, *tail_parts)]
    sums = call(add_y, "add_y", sums, [slices], limit=SMALL)[0]
    sums = call(add_blocks, "add_seq", [(V, exchange(sums))], [slices], limit=SMALL)[0]
    dwin, dwdt, dwout, dcw, dcb, dgo, dgi, ddtb, dal, dds = call(
        finish,
        "finish",
        [(V, exchange(sums))],
        [shape(96, E + C), shape(96, 2 * H), shape(192, D), shape(4, C), shape(C)]
        + [shape(E), shape(D), shape(2 * H), shape(H), shape(H)],
        limit=SMALL,
    )
    return (
        out[None], dtok[None], dgi, dwin, dwdt, dcw, dcb, ddtb, dal, dds, dgo, dwout,
    )


def solution(mesh):
    split = P("dp", "seq", None)
    rows = P("dp", None)
    return jax.shard_map(
        local,
        mesh=mesh,
        in_specs=(split, P("dp", "seq"), P(), rows, rows, P(), P(), P(), P(), P(), P(), rows, split),
        out_specs=(split, split, P(), rows, rows, P(), P(), P(), P(), P(), P(), rows),
        check_vma=False,
    )
```

```python
from functools import partial

import jax
import jax.numpy as jnp
from jax import lax
from jax.experimental import pallas as pl
from jax.experimental.pallas import tpu as pltpu
from jax.sharding import PartitionSpec as P

F32, BF = jnp.float32, jnp.bfloat16
EPS = 1e-05
LOG2E = 1.4426950408889634
D, H, E, N, T = 768, 24, 1536, 64, 256
C = E + 4 * N
CD = C + 128
HALO = 16
WIDE = E // 256
DP, SEQ = 8, 16
HALF = 21
VMEM = 56 * 1024 * 1024
SMALL = 12 * 1024 * 1024


def iota(shape, dim):
    return lax.broadcasted_iota(jnp.int32, shape, dim)


def mm(a, b):
    return jnp.dot(a, b, preferred_element_type=F32)


def mm_nt(a, b):
    return lax.dot_general(a, b, (((1,), (1,)), ((), ())), preferred_element_type=F32)


def flip(v):
    return v.astype(F32).T.astype(v.dtype)


def sigmoid(v):
    return 1.0 / (1.0 + jnp.exp(-v))


def silu(v):
    return v * sigmoid(v)


def split2(v):
    hi = v.astype(BF)
    return hi, (v - hi.astype(F32)).astype(BF)


def onehot(cond):
    return jnp.where(cond, 1.0, 0.0).astype(BF)


def marks():
    row, head = iota((64, E), 0), iota((64, E), 1) >> 6
    columns = onehot((row == head) | (row == head + H))
    return columns, onehot((iota((E, 128), 0) >> 6) == iota((E, 128), 1))


def to_front(v):
    return pltpu.roll(v, 128 - H, 1)


def to_back(v):
    return pltpu.roll(v, H, 1)


def pairs_of(v):
    def terms(v):
        hi = v.astype(BF).astype(F32)
        lane = lanes(v.shape[0])
        both = jnp.where(lane < H, hi, jnp.where(lane < 2 * H, to_back(v - hi), 0.0))
        return both[:, :64].astype(BF)

    return terms(v), terms(to_front(v))


def head_sum(v, marks):
    hi, lo = split2(v)
    return mm(hi, marks) + mm(lo, marks)


def tri_sum(mask, v):
    hi = v.astype(BF)
    rest = v - hi.astype(F32)
    mid = rest.astype(BF)
    low = (rest - mid.astype(F32)).astype(BF)
    return mm(mask, hi) + mm(mask, mid) + mm(mask, low)


def tri(cond):
    return onehot(cond(iota((T, T), 0), iota((T, T), 1)))


def lanes(rows=T):
    return iota((rows, 128), 1)


def wide(i):
    return pl.ds(pl.multiple_of(i * 256, 256), 256)


def fetch(sources, sems, tiles=WIDE):
    def copies(i):
        return [
            pltpu.make_async_copy(src.at[:, wide(i)], dst.at[:, wide(i)], sems.at[k, i])
            for k, (src, dst) in enumerate(sources)
        ]

    for i in range(tiles):
        for copy in copies(i):
            copy.start()

    def wait(i):
        for copy in copies(i):
            copy.wait()

    return wait


def parts_of_bc(act):
    return [act[:, N * k : N * k + N].astype(BF) for k in range(4)]


def ends(cum):
    return jnp.where(lanes(1) < H, cum[T - 1 : T], cum[0:1])


def put_slices(pay, i, first, second, dec_first, dec_second):
    row = iota((16, 128), 0)
    for e in range(2):
        at = slice(128 * e, 128 * e + 128)
        tile = 2 * i + e
        group = lax.div(tile, 3)
        into = pl.ds(pl.multiple_of(lax.rem(tile, 3) * 128, 128), 128)
        a, b = dec_first[:, at], dec_second[:, at]
        ah, bh = a.astype(BF).astype(F32), b.astype(BF).astype(F32)
        dec = jnp.where(
            row == 0, ah, jnp.where(row == 1, a - ah, jnp.where(row == 2, bh, b - bh))
        )
        dec = jnp.where(row < 4, dec, 0.0).astype(BF)
        for q in range(4):
            j = 4 * group + q
            pay[j, 0:16, into] = first[16 * q : 16 * q + 16, at].astype(BF)
            pay[j, 16:32, into] = second[16 * q : 16 * q + 16, at].astype(BF)
            pay[j, 32:48, into] = dec


def take_slices(recv, first, second, first_scale):
    for j in range(SEQ):
        rows, at = pl.ds(16 * (j % 4), 16), pl.ds(384 * (j // 4), 384)
        first[rows, at] = (recv[j, 0:16].astype(F32) * first_scale).astype(BF)
        second[rows, at] = recv[j, 16:32]


def load_weights(ids, parts, w, sem, start=True):
    copies = [
        pltpu.make_async_copy(
            parts[k], w.at[pl.ds(pl.multiple_of(ids[k] * 96, 32), 96)], sem.at[k]
        )
        for k in range(8)
    ]
    if start:
        for copy in copies:
            copy.start()
    return copies


def load_rest(rest, wg, wo, sem, start=True):
    gates, outs = [], []
    for p in range(DP):
        at = 384 * p
        if wg is not None:
            gates.append((rest.at[pl.ds(at, 96)], wg.at[0, pl.ds(96 * p, 96)]))
            gates.append((rest.at[pl.ds(at + 96, 96)], wg.at[1, pl.ds(96 * p, 96)]))
        if wo is not None:
            outs.append((rest.at[pl.ds(at + 192, 192)], wo.at[pl.ds(192 * p, 192)]))
    copies = [pltpu.make_async_copy(a, b, sem.at[k]) for k, (a, b) in enumerate(gates + outs)]
    if start:
        for copy in copies:
            copy.start()
    return copies[: len(gates)], copies[len(gates) :]


def finish_all(copies):
    for copy in copies:
        copy.wait()


def front(ids, cont, tok, halo, gin, cw, cb, dtb, alog, hc, *refs):
    parts, outs, (w, cif, csv, civ, uv, sem, osem, usem) = refs[:8], refs[8:15], refs[15:]
    u_out, ci_out, cs_out, sraw_out, dt_out, cum_out, pay = outs
    copies = load_weights(ids, parts, w, sem)
    x = jnp.concatenate([halo[...], tok[...]], axis=0).astype(F32)
    u = x * lax.rsqrt(jnp.mean(x * x, axis=1, keepdims=True) + EPS) * gin[...]
    uv[...] = u.astype(BF)
    u_copy = pltpu.make_async_copy(uv, u_out, usem)
    u_copy.start()
    keep = cont[0]
    mask = jnp.where(iota((HALO + T, 1), 0) < HALO, keep, 1.0)
    finish_all(copies)
    sraw = mm(uv[HALO:, :], w[:, C:]) + dtb[...]
    sraw_out[...] = sraw
    dt = jnp.maximum(sraw, 0.0) + jnp.log1p(jnp.exp(-jnp.abs(sraw)))
    dt = jnp.where(lanes() < 2 * H, dt, 0.0)
    dt_out[...] = dt
    rate = jnp.where(lanes(1) < 2 * H, jnp.exp(alog[...]), 0.0)
    la = -dt * rate
    cum = jnp.where(
        lanes() < H,
        tri_sum(tri(lambda r, c: r >= c), la),
        tri_sum(tri(lambda r, c: r <= c), la),
    )
    cum_out[...] = cum
    last = ends(cum)
    tail_f, tail_r = pairs_of(jnp.exp(last - cum) * dt)
    dec_f, dec_r = pairs_of(jnp.broadcast_to(jnp.exp(last) * keep, (16, 128)))

    def outward(i):
        at = wide(i)
        return [
            pltpu.make_async_copy(csv.at[:, at], cs_out.at[:, at], osem.at[0, i]),
            pltpu.make_async_copy(civ.at[:, at], ci_out.at[:, at], osem.at[1, i]),
        ]

    def convolve(i):
        at = wide(i)
        ci = (mm(uv[...], w[:, at]) * mask).astype(BF)
        civ[:, at] = ci
        for e in range(2):
            here = pl.ds(pl.multiple_of(i * 256 + 128 * e, 128), 128)
            cif[e] = ci[:, 128 * e : 128 * e + 128].astype(F32)
            total = cb[:, here]
            for k in range(4):
                total = total + cw[k : k + 1, here] * cif[e, HALO - 3 + k : HALO - 3 + k + T]
            csv[:, here] = total
        for copy in outward(i):
            copy.start()
        return silu(csv[:, at])

    bf, _, br, _ = parts_of_bc(convolve(WIDE))
    bf_t, br_t = flip(bf), flip(br)

    def tile(i, _):
        at = wide(i)
        x_act = convolve(i)
        sf = mm(bf_t, (mm(tail_f, hc[:, at]) * x_act).astype(BF))
        sr = mm(br_t, (mm(tail_r, hc[:, at]) * x_act).astype(BF)) * keep
        put_slices(pay, i, sf, sr, mm(dec_f, hc[:, at]), mm(dec_r, hc[:, at]))
        return 0

    lax.fori_loop(0, WIDE, tile, 0)
    u_copy.wait()
    for i in range(WIDE + 1):
        finish_all(outward(i))


def scan_blocks(recv, out):
    carry = jnp.zeros((16, 384), F32)
    back = jnp.zeros((16, 384), F32)
    for i in range(SEQ):
        k = SEQ - 1 - i
        out[i, 0:16] = carry.astype(BF)
        out[k, 16:32] = back.astype(BF)
        dec = recv[i, 32:48].astype(F32)
        carry = (dec[0:1] + dec[1:2]) * carry + recv[i, 0:16].astype(F32)
        dec = recv[k, 32:48].astype(F32)
        back = (dec[2:3] + dec[3:4]) * back + recv[k, 16:32].astype(F32)


def columns_of(cum2, col, base=0):
    for h in range(col.shape[0]):
        col[h] = jnp.broadcast_to(cum2[:, base + h : base + h + 1], (T, 128))


def by_head(v):
    head = iota((T, 256), 1) >> 6
    return [jnp.where(head == e, v, 0.0).astype(BF) for e in range(4)]


def low_full(left, right):
    right = jnp.concatenate([jnp.zeros((128, 128), right.dtype), right], axis=0)
    return jnp.concatenate([left, right], axis=1)


def up_full(left, right):
    left = jnp.concatenate([left, jnp.zeros((128, 128), left.dtype)], axis=0)
    return jnp.concatenate([left, right], axis=1)


def local_mix(dt, cum, dsk, hc, cs, ylf, ylr, base, *scratch):
    csv, yfv, yrv, bsv, col, row, gf, gr, bsem, sem, osem = scratch
    bc = pltpu.make_async_copy(cs.at[:, E:], csv.at[:, E:], bsem)
    bc.start()
    wait = fetch([(cs, csv)], sem)
    cum2 = cum[...] * LOG2E
    row[...] = cum2.T
    columns_of(cum2, col)
    dt_f, dt_r = pairs_of(dt[...])
    bc.wait()
    bf, cf, br, cr = parts_of_bc(silu(csv[:, E:]))
    r, c = iota((T, T), 0), iota((T, T), 1)
    gf[...] = jnp.where(r > c, mm_nt(cf, bf), 0.0)
    gr[...] = jnp.where(r < c, mm_nt(cr, br), 0.0)

    def weights(h, forward):
        at, along = col[h], row[pl.ds(h, 1), :]
        if forward:
            left = jnp.exp2(jnp.minimum(at - along[:, :128], 0.0)) * gf[:, :128]
            right = jnp.exp2(jnp.minimum(at[128:] - along[:, 128:], 0.0)) * gf[128:, 128:]
            return low_full(left.astype(BF), right.astype(BF))
        left = jnp.exp2(jnp.minimum(at[:128] - along[:, :128], 0.0)) * gr[:128, :128]
        right = jnp.exp2(jnp.minimum(at - along[:, 128:], 0.0)) * gr[:, 128:]
        return up_full(left.astype(BF), right.astype(BF))

    def outward(i):
        return [
            pltpu.make_async_copy(a.at[:, wide(i)], b.at[:, wide(i)], osem.at[k, i])
            for k, (a, b) in enumerate([(yfv, ylf), (yrv, ylr), (bsv, base)])
        ]

    def tile(i, _):
        at = wide(i)
        wait(i)
        x = silu(csv[:, at])
        total = dsk[:, at] * x
        for forward, first, dt2, y in ((True, 0, dt_f, yfv), (False, H, dt_r, yrv)):
            xs = by_head(x * mm(dt2, hc[:, at]))
            left = jnp.concatenate([weights(first + 4 * i + e, forward) for e in range(4)], axis=1)
            own = mm(left, jnp.concatenate(xs, axis=0))
            y[:, at] = own
            total = total + own
        bsv[:, at] = total
        for copy in outward(i):
            copy.start()
        return 0

    lax.fori_loop(0, WIDE, tile, 0)
    for i in range(WIDE):
        finish_all(outward(i))


def gate_products(u, dout, rest, gate, dn, wg, wo, gv, dv, sem, osem):
    gates, outs = load_rest(rest, wg, wo, sem)
    copies = []

    def put(k, value, src, dst, at):
        src[:, at] = value.astype(BF)
        copies.append(pltpu.make_async_copy(src.at[:, at], dst.at[:, at], osem.at[k]))
        copies[-1].start()

    finish_all(gates)
    put(0, mm(u[HALO:, :], wg[0]), gv, gate, slice(0, D))
    put(1, mm(u[HALO:, :], wg[1]), gv, gate, slice(D, E))
    finish_all(outs)
    put(2, mm_nt(dout[...], wo[:D]), dv, dn, slice(0, D))
    put(3, mm_nt(dout[...], wo[D:]), dv, dn, slice(D, E))
    finish_all(copies)


def gated_norm(cont, cum, recv, gout, hc, cs, base, gate, dn, *refs):
    (n16, dg16, dm16, dgout, pay), scratch = refs[:5], refs[5:]
    bcv, yv, gv, dv, gds, sls, eff, efr, nv, dgv, dmv, sf, sr, bsem, sem, osem = scratch
    bc = pltpu.make_async_copy(cs.at[:, E:], bcv, bsem)
    bc.start()
    wait = fetch([(base, yv), (gate, gv), (dn, dv)], sem)
    keep = cont[0]
    take_slices(recv, sf, sr, keep)
    cumv = cum[...]
    ef_f, ef_r = pairs_of(jnp.exp(cumv))
    dec_f, dec_r = pairs_of(jnp.broadcast_to(jnp.exp(ends(cumv)) * keep, (16, 128)))
    bc.wait()
    _, cf, _, cr = parts_of_bc(silu(bcv[...]))
    zero = jnp.zeros((T, 128), F32)

    def first(i, sums):
        at = wide(i)
        wait(i)
        ef, er = mm(ef_f, hc[:, at]), mm(ef_r, hc[:, at])
        eff[:, at] = ef
        efr[:, at] = er
        m = yv[:, at] + ef * mm(cf, sf[:, at]) + er * mm(cr, sr[:, at])
        g = gv[:, at].astype(F32)
        sg = sigmoid(g)
        sl = g * sg
        gd = m * sl
        gds[:, at] = gd
        sls[:, at] = sl
        yv[:, at] = m * sg * (1.0 + g * (1.0 - sg))
        squares, crossed = gd * gd, dv[:, at].astype(F32) * gout[:, at] * gd
        return (
            sums[0] + squares[:, :128] + squares[:, 128:],
            sums[1] + crossed[:, :128] + crossed[:, 128:],
        )

    squares, crossed = lax.fori_loop(0, WIDE, first, (zero, zero))
    rs = lax.rsqrt(jnp.sum(squares, axis=1, keepdims=True) / E + EPS)
    pull = jnp.sum(crossed, axis=1, keepdims=True) / E * (rs * rs * rs)
    cf_t, cr_t = flip(cf), flip(cr)

    def outward(i):
        return [
            pltpu.make_async_copy(a.at[:, wide(i)], b.at[:, wide(i)], osem.at[k, i])
            for k, (a, b) in enumerate([(nv, n16), (dgv, dg16), (dmv, dm16)])
        ]

    def second(i, _):
        at = wide(i)
        gd = gds[:, at]
        gdr = gd * rs
        go = gout[:, at]
        nv[:, at] = (gdr * go).astype(BF)
        d = dv[:, at].astype(F32)
        dgout[:, at] = jnp.sum(d * gdr, axis=0, keepdims=True)
        dgd = rs * (d * go) - gd * pull
        dgv[:, at] = (dgd * yv[:, at]).astype(BF)
        dm = dgd * sls[:, at]
        dmv[:, at] = dm.astype(BF)
        for copy in outward(i):
            copy.start()
        lf = mm(cf_t, (eff[:, at] * dm).astype(BF)) * keep
        lr = mm(cr_t, (efr[:, at] * dm).astype(BF))
        put_slices(pay, i, lr, lf, mm(dec_r, hc[:, at]), mm(dec_f, hc[:, at]))
        return 0

    lax.fori_loop(0, WIDE, second, 0)
    for i in range(WIDE):
        finish_all(outward(i))


def grads_and_rows(
    cont, cum, recv, hc, hr, dout, n16, u, dg16, dm16, cs, ylf, ylr, rows, dc, grads, *scratch
):
    n_t, u_t, dwo, dwg, bcv, yfv, yrv, sf, sr, doutv, nv, uv, dgv, dmv = scratch[:14]
    lsem, sem, osem = scratch[14:]
    loads = [(dout, doutv), (n16, nv), (u, uv), (dg16, dgv), (cs.at[:, E:], bcv)]
    loads = [pltpu.make_async_copy(a, b, lsem.at[k]) for k, (a, b) in enumerate(loads)]
    for copy in loads:
        copy.start()
    finish_all(loads[:2])
    wait = fetch([(ylf, yfv), (ylr, yrv), (dm16, dmv)], sem)
    n_t[...] = flip(nv[...])

    def rows_out(i, _):
        at = pl.ds(pl.multiple_of(i * 256, 256), 256)
        dwo[at, :] = mm(n_t[at, :], doutv[...]).astype(BF)
        return 0

    def rows_gate(i, _):
        at = pl.ds(pl.multiple_of(i * 256, 256), 256)
        dwg[at, :] = mm(u_t[at, :], dgv[...]).astype(BF)
        return 0

    lax.fori_loop(0, E // 256, rows_out, 0)
    finish_all(loads[2:4])
    u_t[...] = flip(uv[HALO:, :])
    lax.fori_loop(0, D // 256, rows_gate, 0)
    outward = []
    for d in range(DP):
        for src, rows_at, into in (
            (dwg.at[:, :D], 96, slice(384 * d, 384 * d + 96)),
            (dwg.at[:, D:], 96, slice(384 * d + 96, 384 * d + 192)),
            (dwo, 192, slice(384 * d + 192, 384 * d + 384)),
        ):
            src = src.at[pl.ds(rows_at * d, rows_at)]
            outward.append(pltpu.make_async_copy(src, grads.at[into], osem.at[len(outward)]))
            outward[-1].start()
    take_slices(recv, sf, sr, cont[0])
    ef_f, ef_r = pairs_of(jnp.exp(cum[...]))
    finish_all(loads[4:])
    _, cf, _, cr = parts_of_bc(silu(bcv[...]))

    def tile(i, sums):
        at = wide(i)
        wait(i)
        dm = dmv[:, at].astype(F32)
        new = []
        for ef2, c, s, yl in ((ef_f, cf, sf, yfv), (ef_r, cr, sr, yrv)):
            ef = mm(ef2, hc[:, at])
            y = yl[:, at] + ef * mm(c, s[:, at])
            new.append(head_sum(dm * y, hr[at, :]))
            new.append(mm_nt((ef * dm).astype(BF), s[:, at]))
        return tuple(a + b for a, b in zip(sums, new))

    zero, zn = jnp.zeros((T, 128), F32), jnp.zeros((T, N), F32)
    rf, dcf, rr, dcr = lax.fori_loop(0, WIDE, tile, (zero, zn, zero, zn))
    rows[...] = rf + to_back(rr)
    dc[...] = jnp.concatenate([dcf, dcr], axis=1)
    finish_all(outward)


def project_out(tok, n16, rest, out, wo, sem):
    finish_all(load_rest(rest, None, wo, sem)[1])
    out[...] = (tok[...].astype(F32) + mm(n16[...], wo[...])).astype(BF)


def local_back(dt, cum, dm16, hc, hr, cs, zf, zr, dgf, dgr, inner, *scratch):
    csv, zfv, zrv, col, row, gf, gr, dm_t, sem, osem = scratch
    bc = pltpu.make_async_copy(cs.at[:, E:], csv.at[:, E:], sem.at[0, WIDE])
    bc.start()
    wait = fetch([(cs, csv)], sem)
    cum2 = cum[...] * LOG2E
    row[...] = cum2.T
    columns_of(cum2, col)
    dm_t[...] = flip(dm16[...])
    dt_f, dt_r = pairs_of(dt[...])
    bc.wait()
    bf, cf, br, cr = parts_of_bc(silu(csv[:, E:]))
    s, t = iota((T, T), 0), iota((T, T), 1)
    gf[...] = jnp.where(t > s, mm_nt(bf, cf), 0.0)
    gr[...] = jnp.where(t < s, mm_nt(br, cr), 0.0)
    dgf[...] = jnp.zeros((T, T), F32)
    dgr[...] = jnp.zeros((T, T), F32)

    def outward(i):
        return [
            pltpu.make_async_copy(a.at[:, wide(i)], b.at[:, wide(i)], osem.at[k, i])
            for k, (a, b) in enumerate([(zfv, zf), (zrv, zr)])
        ]

    def tile(i, sums):
        at = wide(i)
        wait(i)
        x = silu(csv[:, at])
        new = []
        ds = jnp.concatenate(by_head(dm16[:, at].astype(F32)), axis=0)
        dms = dm_t[at, :]
        for forward in (True, False):
            first = 0 if forward else H
            xd = x * mm(dt_f if forward else dt_r, hc[:, at])
            xs = by_head(xd)
            ws = []
            small = jnp.zeros((128, 128), F32)
            large = jnp.zeros((T, 128), F32)
            for e in range(4):
                h = first + 4 * i + e
                at_s, along = col[h], row[pl.ds(h, 1), :]
                dw = mm(xs[e], dms)
                if forward:
                    ea = jnp.exp2(jnp.minimum(along[:, :128] - at_s[:128], 0.0))
                    eb = jnp.exp2(jnp.minimum(along[:, 128:] - at_s, 0.0))
                    ws.append(
                        up_full((ea * gf[:128, :128]).astype(BF), (eb * gf[:, 128:]).astype(BF))
                    )
                    small = small + ea * dw[:128, :128]
                    large = large + eb * dw[:, 128:]
                else:
                    ea = jnp.exp2(jnp.minimum(along[:, :128] - at_s, 0.0))
                    eb = jnp.exp2(jnp.minimum(along[:, 128:] - at_s[128:], 0.0))
                    ws.append(
                        low_full((ea * gr[:, :128]).astype(BF), (eb * gr[128:, 128:]).astype(BF))
                    )
                    large = large + ea * dw[:, :128]
                    small = small + eb * dw[128:, 128:]
            total = mm(jnp.concatenate(ws, axis=1), ds)
            new.append(head_sum(xd.astype(BF).astype(F32) * total, hr[at, :]))
            if forward:
                zfv[:, at] = total.astype(BF)
                dgf[:128, :128] += small
                dgf[:, 128:] += large
            else:
                zrv[:, at] = total.astype(BF)
                dgr[:, :128] += large
                dgr[128:, 128:] += small
        for copy in outward(i):
            copy.start()
        return sums[0] + new[0], sums[1] + new[1]

    zero = jnp.zeros((T, 128), F32)
    sums = lax.fori_loop(0, WIDE, tile, (zero, zero))
    inner[...] = sums[0] + to_back(sums[1])
    dgf[...] = jnp.where(t > s, dgf[...], 0.0)
    dgr[...] = jnp.where(t < s, dgr[...], 0.0)
    for i in range(WIDE):
        finish_all(outward(i))


def inner_back(
    ids, cont, halo, gin, cw, alog, dsk, sraw, dt, cum, back, fore, rows, inner, dc, dgout, hc, hr,
    dgf, dgr, tok, dout, cs, zf, zr, dm16, ci, dg16, rest, *refs
):
    parts, (dtok, dhalo, dall_out, small_out), scratch = refs[:8], refs[8:12], refs[12:]
    csv, zfv, zrv, dmv, civ, dgv, w, wg, sf, sr, kf, kr, dcs, cif, du, small = scratch[:16]
    line, dall, gfv, grv, tokv, doutv, sem, csem, wsem, gsem, osem = scratch[16:]
    first = [(cs.at[:, E:], csv.at[:, E:])]
    bcc = pltpu.make_async_copy(*first[0], csem.at[0])
    bcc.start()
    wait = fetch([(cs, csv), (zf, zfv), (zr, zrv), (dm16, dmv)], sem)
    later = [(dgf, gfv), (dgr, grv), (ci, civ), (dg16, dgv), (tok, tokv), (dout, doutv)]
    later = [pltpu.make_async_copy(a, b, csem.at[1 + k]) for k, (a, b) in enumerate(later)]
    keep = cont[0]
    take_slices(back, kr, kf, keep)
    take_slices(fore, sf, sr, keep)
    cumv, dtv = cum[...], dt[...]
    last = ends(cumv)
    te_f, te_r = pairs_of(jnp.exp(last - cumv))
    dt_f, dt_r = pairs_of(dtv)
    line[...] = jnp.zeros((8, E), F32)
    dcs[:, 0:HALO] = jnp.zeros((C // 128, HALO, 128), F32)
    dcs[:, HALO + T :] = jnp.zeros((C // 128, 16, 128), F32)
    bcc.wait()
    bc = csv[:, E:]
    bf, cf, br, cr = parts_of_bc(silu(bc))

    def weights():
        gates = load_rest(rest, wg, None, gsem, False)[0]
        return load_weights(ids, parts, w, wsem, False) + gates

    def slope(v, sg):
        return sg * (1.0 + v * (1.0 - sg))

    def tile(i, sums):
        at = wide(i)

        @pl.when(i == 1)
        def _():
            for copy in later:
                copy.start()

        @pl.when(i == 3)
        def _():
            for copy in weights():
                copy.start()

        wait(i)
        v = csv[:, at]
        sg = sigmoid(v)
        x = v * sg
        dm = dmv[:, at].astype(F32)
        line[2:3, at] = jnp.sum(dm * x, axis=0, keepdims=True)
        dx = dsk[:, at] * dm
        new = []
        for d, dt2, te2, z, k, s, b in (
            (0, dt_f, te_f, zfv, kf, sf, bf),
            (1, dt_r, te_r, zrv, kr, sr, br),
        ):
            dts, te = mm(dt2, hc[:, at]), mm(te2, hc[:, at])
            xd = (x * dts).astype(BF).astype(F32)
            zt = te * mm(b, k[:, at])
            dx = dx + dts * (z[:, at].astype(F32) + zt)
            new.append(mm((xd * zt).astype(BF), hr[at, :]))
            new.append(mm_nt((te * xd).astype(BF), k[:, at]))
            both = s[:, at].astype(F32) * k[:, at].astype(F32)
            line[d : d + 1, at] = jnp.sum(both, axis=0, keepdims=True)
        dx = dx * slope(v, sg)
        for e in range(2):
            dcs[2 * i + e, HALO : HALO + T] = dx[:, 128 * e : 128 * e + 128]
        return tuple(a + b for a, b in zip(sums, new))

    zero, zn = jnp.zeros((T, 128), F32), jnp.zeros((T, N), F32)
    sums = lax.fori_loop(0, WIDE, tile, (zero, zn, zero, zn))
    tails = sums[0] + to_back(sums[2])
    finish_all(later)
    gf16, gr16 = gfv[...].astype(BF), grv[...].astype(BF)
    dbf = sums[1] + mm(gf16, cf)
    dbr = sums[3] + mm(gr16, cr)
    dcf = dc[:, :N] + mm(flip(gf16), bf)
    dcr = dc[:, N:] + mm(flip(gr16), br)
    dbc = jnp.concatenate([dbf, dcf, dbr, dcr], axis=1) * slope(bc, sigmoid(bc))
    for e in range(2):
        dcs[2 * WIDE + e, HALO : HALO + T] = dbc[:, 128 * e : 128 * e + 128]
    hi, lo = split2(line[...])
    heads = mm(hi, hr[...]) + mm(lo, hr[...])
    dots = heads[0:1] + to_back(heads)[1:2]
    rate = jnp.where(lanes(1) < 2 * H, jnp.exp(alog[...]), 0.0)
    v = rows[...] - inner[...]
    dla = jnp.where(
        lanes() < H,
        tri_sum(tri(lambda r, c: r <= c), v) + tri_sum(tri(lambda r, c: r > c), tails),
        tri_sum(tri(lambda r, c: r >= c), v) + tri_sum(tri(lambda r, c: r < c), tails),
    ) + jnp.exp(last) * dots
    sg = sigmoid(sraw[...])
    ratio = jnp.where(dtv > 1e-20, sg / jnp.maximum(dtv, 1e-20), 1.0)
    dstep = (inner[...] + tails) * ratio - dla * rate * sg
    dstep = jnp.where(lanes() < 2 * H, dstep, 0.0)
    dall[0:HALO, C:] = jnp.zeros((HALO, 128), BF)
    dall[HALO:, C:] = dstep.astype(BF)
    dal = jnp.broadcast_to(jnp.sum(dla * (-dtv * rate), axis=0, keepdims=True), (8, 128))
    small[...] = jnp.zeros((96, 128), F32)
    small[88:89] = jnp.sum(dstep, axis=0, keepdims=True)
    small[89:90] = jnp.where(lanes(1) < H, dal[0:1] + to_front(dal)[0:1], 0.0)
    small[90:91] = jnp.where(lanes(1) < H, heads[2:3], 0.0)
    mask = jnp.where(iota((HALO + T, 1), 0) < HALO, keep, 1.0)

    def outward(i):
        at = pl.ds(pl.multiple_of(i * 128, 128), 128)
        return pltpu.make_async_copy(dall.at[:, at], dall_out.at[:, at], osem.at[i])

    outward(C // 128).start()

    def convolution(i, _):
        at = pl.ds(pl.multiple_of(i * 128, 128), 128)
        g = dcs[i, HALO : HALO + T]
        cif[...] = civ[:, at].astype(F32)
        small[pl.ds(56 + i, 1)] = jnp.sum(g, axis=0, keepdims=True)
        total = jnp.zeros((HALO + T, 128), F32)
        for k in range(4):
            shifted = cif[HALO - 3 + k : HALO - 3 + k + T]
            small[pl.ds(14 * k + i, 1)] = jnp.sum(g * shifted, axis=0, keepdims=True)
            total = total + cw[k : k + 1, at] * dcs[i, 3 - k : 3 - k + HALO + T]
        dall[:, at] = (total * mask).astype(BF)
        outward(i).start()
        return 0

    lax.fori_loop(0, C // 128, convolution, 0)
    for j in range(E // 128):
        small[70 + j : 71 + j] = dgout[:, 128 * j : 128 * j + 128]
    finish_all(weights())

    def input_grad(i, _):
        at = wide(i)
        du[:, at] = mm_nt(dall[...], w[at, :])
        du[HALO:, at] += mm_nt(dgv[:, :D], wg[0, at, :]) + mm_nt(dgv[:, D:], wg[1, at, :])
        return 0

    lax.fori_loop(0, D // 256, input_grad, 0)
    x = jnp.concatenate([halo[...], tokv[...]], axis=0).astype(F32)
    r = lax.rsqrt(jnp.mean(x * x, axis=1, keepdims=True) + EPS)
    duxr = jnp.sum(du[...] * x * r, axis=0, keepdims=True)
    for j in range(6):
        small[82 + j : 83 + j] = duxr[:, 128 * j : 128 * j + 128]
    small_out[...] = small[...].astype(BF)
    dxh = du[...] * gin[...]
    dx = r * dxh - x * (r * r * r * jnp.mean(dxh * x, axis=1, keepdims=True))
    dhalo[...] = dx[:HALO]
    dtok[...] = doutv[...].astype(F32) + dx[HALO:]
    for i in range(CD // 128):
        outward(i).wait()


def weight_back(ids, u, dall, small, keep, send, u_t, dw, osem, ssem):
    extra = []
    for ref, base in ((send, 0), (keep, 4)):
        for k in range(4):
            extra.append(
                pltpu.make_async_copy(small, ref.at[k, :, pl.ds(CD, 128)], ssem.at[base + k])
            )
            extra[-1].start()
    u_t[...] = flip(u[...])

    def piece(d, ref):
        where = ids[16 + d // 2]
        src = dw.at[pl.ds(96 * d, 96)]
        return pltpu.make_async_copy(src, ref.at[where, :, pl.ds(0, CD)], osem.at[d])

    def each(d, act):
        mine = ids[20] == d % 2

        @pl.when(mine)
        def _():
            act(piece(d, keep))

        @pl.when(jnp.logical_not(mine))
        def _():
            act(piece(d, send))

    done = 0
    for c in range(D // 256):
        at = slice(256 * c, 256 * c + 256)
        dw[at, :] = mm(u_t[at, :], dall[...]).astype(BF)
        while 96 * (done + 1) <= 256 * (c + 1):
            each(done, lambda copy: copy.start())
            done += 1
    finish_all(extra)
    for d in range(DP):
        each(d, lambda copy: copy.wait())


def add_pairs(ids, a, b, whole, one, three, mine, other):
    for k, out in ((0, whole), (1, one), (3, three)):

        def rows(i, _, k=k, out=out):
            at = pl.ds(pl.multiple_of(i * 48, 16), 48)
            out[at] = (a[k, at].astype(F32) + b[k, at].astype(F32)).astype(BF)
            return 0

        lax.fori_loop(0, 2, rows, 0)
    for out, half in ((mine, ids[HALF]), (other, 1 - ids[HALF])):
        at = pl.ds(pl.multiple_of(half * 1024, 1024), 1024)
        out[...] = (a[2, :, at].astype(F32) + b[2, :, at].astype(F32)).astype(BF)


def add_two(a, b, out):
    out[...] = (a[...].astype(F32) + b[...].astype(F32)).astype(BF)


def add_y(ids, rest, whole, one, three, half, out):
    for j in range(6):
        for r in range(0, 384, 48):
            row = 384 * j + r
            out[row // 144, row % 144 : row % 144 + 48] = rest[
                r : r + 48, 128 * j : 128 * j + 128
            ]
    for j in range(SEQ):
        at, in_half = slice(128 * j, 128 * j + 128), slice(128 * (j % 8), 128 * (j % 8) + 128)
        mine = jnp.where(ids[HALF] == j // 8, 1.0, 0.0)
        total = sum(part[:, at].astype(F32) for part in (whole, one, three))
        out[j, 144:] = (total + half[:, in_half].astype(F32) * mine).astype(BF)


def add_blocks(recv, out):
    total = recv[0].astype(F32)
    for i in range(1, SEQ):
        total = total + recv[i].astype(F32)
    low = total.astype(BF)
    for i in range(SEQ):
        out[i] = low


def finish(sums, dwin, dwdt, dwout, dcw, dcb, dgout, dgin, ddtb, dal, ddsk):
    def put(ref, at, start, rows):
        for r in range(0, rows, 48):
            j, k = (start + r) // 144, (start + r) % 144
            ref[r : r + 48, at] = sums[j, k : k + 48].astype(F32)

    for j in range(6):
        at = slice(128 * j, 128 * j + 128)
        put(dwin, at, 384 * j, 96)
        put(dwin, slice(D + 128 * j, D + 128 * j + 128), 384 * j + 96, 96)
        put(dwout, at, 384 * j + 192, 192)
    for j in range(14):
        dwin[:, E + 128 * j : E + 128 * j + 128] = sums[j, 144:].astype(F32)
    dwdt[...] = sums[14, 144:].astype(F32).T[: 2 * H]
    small = sums[15, 144:].astype(F32)
    for j in range(14):
        at = slice(128 * j, 128 * j + 128)
        for k in range(4):
            dcw[k : k + 1, at] = small[14 * k + j : 14 * k + j + 1]
        dcb[at] = small[56 + j]
    for j in range(E // 128):
        dgout[128 * j : 128 * j + 128] = small[70 + j]
    for j in range(6):
        dgin[128 * j : 128 * j + 128] = small[82 + j]
    ddtb[...] = small[88, 0 : 2 * H]
    dal[...] = small[89, 0:H]
    ddsk[...] = small[90, 0:H]


V = pl.BlockSpec(memory_space=pltpu.VMEM)
S = pl.BlockSpec(memory_space=pltpu.SMEM)
ANY = pl.BlockSpec(memory_space=pl.ANY)


def shape(*dims, dtype=F32):
    return jax.ShapeDtypeStruct(dims, dtype)


def call(kernel, name, ins, outs, scratch=(), flops=0, apart=(), limit=VMEM, light=False):
    specs, args = zip(*ins)
    moved = sum(a.size * a.dtype.itemsize for a in args)
    moved += sum(o.size * o.dtype.itemsize for o in outs)
    return pl.pallas_call(
        kernel,
        name=name,
        out_shape=tuple(outs),
        in_specs=list(specs),
        out_specs=tuple(ANY if i in apart else V for i in range(len(outs))),
        scratch_shapes=list(scratch),
        cost_estimate=pl.CostEstimate(
            flops=flops, bytes_accessed=0 if light else moved, transcendentals=0
        ),
        compiler_params=pltpu.CompilerParams(vmem_limit_bytes=limit),
    )(*args)


def vm(*dims, dtype=F32):
    return pltpu.VMEM(dims, dtype)


def shift_y(k):
    return [(2 * y + c, 2 * ((y + k) % 4) + c) for y in range(4) for c in range(2)]


SWAP = [(i, i ^ 1) for i in range(DP)]
NEXT_Z = [(i, i ^ 1) for i in range(SEQ)]


def exchange(value):
    return lax.all_to_all(value, "seq", 0, 0, tiled=True)


def together(*values):
    return lax.optimization_barrier(values)


def local(
    tokens, starts, g_in, w_in, w_dt, conv_w, conv_b, dt_bias, a_log, dskip, g_out, w_out, d_out
):
    dp = lax.axis_index("dp")
    y, core = dp // 2, dp % 2
    tok, dout = tokens[0], d_out[0]
    cont = (1 - starts[0]).astype(F32)

    row = lambda v: v.reshape(1, -1)
    pad = lambda v: jnp.pad(v, (0, 128 - v.shape[0])).reshape(1, 128)
    alog = pad(jnp.concatenate([a_log, a_log]))
    dsk = row(jnp.repeat(dskip, N))
    gin, gout, cb, dtb = row(g_in), row(g_out), row(conv_b), pad(dt_bias)
    to_y = [(y + k) % 4 for k in range(4)]
    from_y = [(y - k) % 4 for k in range(4)]
    ids = [2 * t + core for t in from_y] + [2 * t + 1 - core for t in from_y]
    ids += [2 * t + core for t in to_y] + [2 * t + 1 - core for t in to_y]
    parity = lax.axis_index("seq") % 2
    ids = jnp.stack(ids + [(t - y) % 4 for t in range(4)] + [core, parity])

    own = jnp.concatenate([w_in[:, E:], jnp.pad(w_dt, ((0, 0), (0, 128 - 2 * H)))], axis=1)
    column = [lax.ppermute(own, "dp", shift_y(k)) for k in (1, 2, 3)]
    halo = lax.ppermute(tok[-HALO:], "seq", [(i, i + 1) for i in range(SEQ - 1)])
    beside = lax.ppermute(own, "dp", SWAP)
    rest_own = jnp.concatenate([w_in[:, :D], w_in[:, D:E], w_out], axis=0)
    hc, hr = marks()
    *column, halo, beside, rest_own, alog, dsk, gin, gout, cb, dtb, ids, hc, hr = together(
        *column, halo, beside, rest_own, alog, dsk, gin, gout, cb, dtb, ids, hc, hr
    )
    parts = [own, *column, beside] + [lax.ppermute(part, "dp", SWAP) for part in column]
    rest = lax.all_gather(rest_own, "dp", axis=0, tiled=True)

    part_ins = [(ANY, part) for part in parts]
    w_scratch = vm(D, CD, dtype=BF)
    dma = pltpu.SemaphoreType.DMA
    full, half, state = vm(T, E), vm(T, E, dtype=BF), vm(N, E, dtype=BF)

    u, ci, cs, sraw, dt, cum, pay = call(
        front,
        "front",
        [(S, ids), (S, cont), (V, tok), (V, halo), (V, gin), (V, conv_w), (V, cb)]
        + [(V, dtb), (V, alog), (V, hc)]
        + part_ins,
        [shape(HALO + T, D, dtype=BF), shape(HALO + T, C, dtype=BF), shape(T, C)]
        + [shape(T, 128)] * 3
        + [shape(SEQ, 48, 384, dtype=BF)],
        [w_scratch, vm(2, HALO + T, 128), vm(T, C), vm(HALO + T, C, dtype=BF)]
        + [vm(HALO + T, D, dtype=BF), dma((8,)), dma((2, WIDE + 1)), dma(())],
        flops=2 * T * D * CD,
        apart=(0, 1, 2),
    )

    def scan(got, name):
        out = shape(SEQ, 32, 384, dtype=BF)
        return call(scan_blocks, name, [(V, got)], [out], limit=SMALL)[0]

    got = exchange(pay)
    ylf, ylr, base = call(
        local_mix,
        "local_mix",
        [(V, dt), (V, cum), (V, dsk), (V, hc), (ANY, cs)],
        [shape(T, E)] * 3,
        [vm(T, C), full, full, full, vm(2 * H, T, 128), vm(128, T), vm(T, T), vm(T, T)]
        + [dma(()), dma((1, WIDE)), dma((3, WIDE))],
        flops=4 * 24 * T * T * 256,
        apart=(0, 1, 2),
    )
    got, ylr, base = together(got, ylr, base)
    fore = exchange(scan(got, "scan_states"))
    gate, dn = call(
        gate_products,
        "gate_products",
        [(V, u), (V, dout), (ANY, rest)],
        [shape(T, E, dtype=BF)] * 2,
        [vm(2, D, D, dtype=BF), vm(E, D, dtype=BF), half, half, dma((24,)), dma((4,))],
        flops=4 * T * D * E,
        apart=(0, 1),
    )
    n16, dg16, dm16, dgout, pay_back = call(
        gated_norm,
        "gated_norm",
        [(S, cont), (V, cum), (V, fore), (V, gout), (V, hc)]
        + [(ANY, a) for a in (cs, base, gate, dn)],
        [shape(T, E, dtype=BF)] * 3 + [shape(1, E), shape(SEQ, 48, 384, dtype=BF)],
        [vm(T, 256), full, half, half] + [full] * 4 + [half] * 3 + [state] * 2
        + [dma(()), dma((3, WIDE)), dma((3, WIDE))],
        flops=12 * T * N * E,
        apart=(0, 1, 2),
    )
    got = exchange(pay_back)
    rows, dc, rest_grads = call(
        grads_and_rows,
        "grads_and_rows",
        [(S, cont)]
        + [(V, a) for a in (cum, fore, hc, hr)]
        + [(ANY, a) for a in (dout, n16, u, dg16, dm16, cs, ylf, ylr)],
        [shape(T, 128), shape(T, 128), shape(DP * 384, D, dtype=BF)],
        [vm(E, T, dtype=BF), vm(D, T, dtype=BF), vm(E, D, dtype=BF), vm(D, E, dtype=BF)]
        + [vm(T, 256), full, full, state, state, vm(T, D, dtype=BF), half]
        + [vm(HALO + T, D, dtype=BF), half, half]
        + [dma((5,)), dma((3, WIDE)), dma((24,))],
        flops=8 * T * D * E,
        apart=(2,),
    )
    got, rows, rest_grads = together(got, rows, rest_grads)
    rest_sum = lax.psum_scatter(rest_grads, "dp", scatter_dimension=0, tiled=True)
    back = exchange(scan(got, "scan_adjoints"))
    zf, zr, dgf, dgr, inner = call(
        local_back,
        "local_back",
        [(V, dt), (V, cum), (V, dm16), (V, hc), (V, hr), (ANY, cs)],
        [shape(T, E, dtype=BF)] * 2 + [shape(T, T)] * 2 + [shape(T, 128)],
        [vm(T, C), half, half, vm(2 * H, T, 128), vm(128, T), vm(T, T), vm(T, T)]
        + [vm(E, T, dtype=BF), dma((1, WIDE + 1)), dma((2, WIDE))],
        flops=4 * 48 * T * T * 256,
        apart=(0, 1),
    )
    dtok, dhalo, dall, small = call(
        inner_back,
        "inner_back",
        [(S, ids), (S, cont)]
        + [(V, a) for a in (halo, gin, conv_w, alog, dsk, sraw, dt, cum, back, fore, rows)]
        + [(V, a) for a in (inner, dc, dgout, hc, hr)]
        + [(ANY, a) for a in (dgf, dgr, tok, dout, cs, zf, zr, dm16, ci, dg16, rest)]
        + part_ins,
        [shape(T, D), shape(HALO, D), shape(HALO + T, CD, dtype=BF), shape(96, 128, dtype=BF)],
        [vm(T, C), half, half, half, vm(HALO + T, C, dtype=BF), half, w_scratch]
        + [vm(2, D, D, dtype=BF)]
        + [state] * 4
        + [vm(C // 128, HALO + T + 16, 128), vm(HALO + T, 128), vm(HALO + T, D), vm(96, 128)]
        + [vm(8, E), vm(HALO + T, CD, dtype=BF), vm(T, T), vm(T, T)]
        + [vm(T, D, dtype=BF), vm(T, D, dtype=BF)]
        + [dma((4, WIDE)), dma((7,)), dma((8,)), dma((16,)), dma((CD // 128,))],
        flops=2 * T * D * (CD + E),
        apart=(2,),
    )
    keep, send = call(
        weight_back,
        "weight_back",
        [(S, ids), (V, u), (V, dall), (V, small)],
        [shape(4, 96, 2048, dtype=BF)] * 2,
        [vm(D, HALO + T, dtype=BF), vm(D, CD, dtype=BF), dma((8,)), dma((8,))],
        flops=2 * T * D * CD,
        apart=(0, 1),
        limit=16 * 1024 * 1024,
    )
    recv = lax.ppermute(send, "dp", SWAP)
    whole, one, three, mine, other = call(
        add_pairs,
        "add_tail_cores",
        [(S, ids), (V, keep), (V, recv)],
        [shape(96, 2048, dtype=BF)] * 3 + [shape(96, 1024, dtype=BF)] * 2,
        limit=SMALL,
    )
    other = lax.ppermute(other, "seq", NEXT_Z)
    one, three = lax.ppermute(one, "dp", shift_y(1)), lax.ppermute(three, "dp", shift_y(3))
    sides = [(V, mine), (V, other)]
    half = call(add_two, "add_tail_z", sides, [shape(96, 1024, dtype=BF)], limit=SMALL)[0]
    half, n16, dhalo = together(half, n16, dhalo)
    half = lax.ppermute(half, "dp", shift_y(2))
    dback = lax.ppermute(dhalo, "seq", [(i + 1, i) for i in range(SEQ - 1)])
    out = call(
        project_out,
        "project_out",
        [(V, tok), (V, n16), (ANY, rest)],
        [shape(T, D, dtype=BF)],
        [vm(E, D, dtype=BF), dma((8,))],
        flops=2 * T * D * E,
    )[0]
    dtok = dtok.at[-HALO:].add(dback)
    one, three, half, out, dtok = together(one, three, half, out, dtok)
    slices = shape(SEQ, 240, 128, dtype=BF)
    sums = [(S, ids)] + [(V, part) for part in (rest_sum, whole, one, three, half)]
    sums = call(add_y, "add_y", sums, [slices], limit=SMALL)[0]
    sums = call(add_blocks, "add_seq", [(V, exchange(sums))], [slices], limit=SMALL)[0]
    dwin, dwdt, dwout, dcw, dcb, dgo, dgi, ddtb, dal, dds = call(
        finish,
        "finish",
        [(V, exchange(sums))],
        [shape(96, E + C), shape(2 * H, 96), shape(192, D), shape(4, C), shape(C)]
        + [shape(E), shape(D), shape(2 * H), shape(H), shape(H)],
        limit=SMALL,
    )
    return (
        out[None], dtok[None], dgi, dwin, dwdt.T, dcw, dcb, ddtb, dal, dds, dgo, dwout,
    )


def solution(mesh):
    split = P("dp", "seq", None)
    rows = P("dp", None)
    return jax.shard_map(
        local,
        mesh=mesh,
        in_specs=(split, P("dp", "seq"), P(), rows, rows, P(), P(), P(), P(), P(), P(), rows, split),
        out_specs=(split, split, P(), rows, rows, P(), P(), P(), P(), P(), P(), rows),
        check_vma=False,
    )
```

```python
from functools import partial

import jax
import jax.numpy as jnp
from jax import lax
from jax.experimental import pallas as pl
from jax.experimental.pallas import tpu as pltpu
from jax.sharding import PartitionSpec as P

F32, BF = jnp.float32, jnp.bfloat16
EPS = 1e-05
LOG2E = 1.4426950408889634
D, H, E, N, T = 768, 24, 1536, 64, 256
C = E + 4 * N
CD = C + 128
HALO = 16
WIDE = E // 256
DP, SEQ = 8, 16
VMEM = 56 * 1024 * 1024
SMALL = 12 * 1024 * 1024


def iota(shape, dim):
    return lax.broadcasted_iota(jnp.int32, shape, dim)


def mm(a, b):
    return jnp.dot(a, b, preferred_element_type=F32)


def mm_nt(a, b):
    return lax.dot_general(a, b, (((1,), (1,)), ((), ())), preferred_element_type=F32)


def mm_rows(parts, right):
    total = mm(jnp.concatenate(parts, axis=0), right)
    ends = [sum(p.shape[0] for p in parts[: k + 1]) for k in range(len(parts))]
    return [total[end - p.shape[0] : end] for end, p in zip(ends, parts)]


def flip(v):
    return v.astype(F32).T.astype(v.dtype)


def sigmoid(v):
    return 1.0 / (1.0 + jnp.exp(-v))


def silu(v):
    return v * sigmoid(v)


def split2(v):
    hi = v.astype(BF)
    return hi, (v - hi.astype(F32)).astype(BF)


def onehot(cond):
    return jnp.where(cond, 1.0, 0.0).astype(BF)


def marks():
    row, head = iota((64, E), 0), iota((64, E), 1) >> 6
    columns = onehot((row == head) | (row == head + H))
    return columns, onehot((iota((E, 128), 0) >> 6) == iota((E, 128), 1))


def to_front(v):
    return pltpu.roll(v, 128 - H, 1)


def to_back(v):
    return pltpu.roll(v, H, 1)


def pairs_of(v):
    def terms(v):
        hi = v.astype(BF).astype(F32)
        lane = lanes(v.shape[0])
        both = jnp.where(lane < H, hi, jnp.where(lane < 2 * H, to_back(v - hi), 0.0))
        return both[:, :64].astype(BF)

    return terms(v), terms(to_front(v))


def tri_sum(mask, v):
    hi = v.astype(BF)
    rest = v - hi.astype(F32)
    mid = rest.astype(BF)
    low = (rest - mid.astype(F32)).astype(BF)
    return mm(mask, hi) + mm(mask, mid) + mm(mask, low)


def tri(cond):
    return onehot(cond(iota((T, T), 0), iota((T, T), 1)))


def lanes(rows=T):
    return iota((rows, 128), 1)


def wide(i):
    return pl.ds(256 * i, 256)


def each(count, body, carry):
    for i in range(count):
        carry = body(i, carry)
    return carry


def fetch(sources, sems):
    def copies(k):
        at = (pl.ds(0, 256), pl.ds(256, E - 256))[k]
        return [
            pltpu.make_async_copy(src.at[:, at], dst.at[:, at], sems.at[n, k])
            for n, (src, dst) in enumerate(sources)
        ]

    for k in range(2):
        for copy in copies(k):
            copy.start()

    def wait(i):
        if i < 2:
            finish_all(copies(i))

    return wait


def deliver(targets, sems, tiles=WIDE):
    def copies(k):
        at = (pl.ds(0, 256 * (tiles - 1)), pl.ds(256 * (tiles - 1), 256))[k]
        return [
            pltpu.make_async_copy(src.at[:, at], dst.at[:, at], sems.at[n, k])
            for n, (src, dst) in enumerate(targets)
        ]

    def done(i):
        if i == tiles - 2:
            for copy in copies(0):
                copy.start()

    def end():
        for copy in copies(1):
            copy.start()
        finish_all(copies(0))
        finish_all(copies(1))

    return done, end


def parts_of_bc(act):
    return [act[:, N * k : N * k + N].astype(BF) for k in range(4)]


def ends(cum):
    return jnp.where(lanes(1) < H, cum[T - 1 : T], cum[0:1])


def put_slices(pay, i, first, second, dec_first, dec_second):
    row = iota((16, 128), 0)
    for e in range(2):
        at = slice(128 * e, 128 * e + 128)
        tile = 2 * i + e
        group, into = tile // 3, pl.ds(tile % 3 * 128, 128)
        a, b = dec_first[:, at], dec_second[:, at]
        ah, bh = a.astype(BF).astype(F32), b.astype(BF).astype(F32)
        dec = jnp.where(
            row == 0, ah, jnp.where(row == 1, a - ah, jnp.where(row == 2, bh, b - bh))
        )
        dec = jnp.where(row < 4, dec, 0.0).astype(BF)
        for q in range(4):
            j = 4 * group + q
            pay[j, 0:16, into] = first[16 * q : 16 * q + 16, at].astype(BF)
            pay[j, 16:32, into] = second[16 * q : 16 * q + 16, at].astype(BF)
            pay[j, 32:48, into] = dec


def take_slices(recv, first, second, first_scale):
    for j in range(SEQ):
        rows, at = pl.ds(16 * (j % 4), 16), pl.ds(384 * (j // 4), 384)
        first[rows, at] = (recv[j, 0:16].astype(F32) * first_scale).astype(BF)
        second[rows, at] = recv[j, 16:32]


def place():
    dp, seq = lax.axis_index("dp"), lax.axis_index("seq")
    return lax.div(dp, 2), lax.rem(dp, 2), lax.rem(seq, 2)


def load_weights(parts, w, sem, start=True):
    y, core, _ = place()
    copies = []
    for k in range(8):
        shard = 2 * lax.rem(y + 4 - k % 4, 4) + (core if k < 4 else 1 - core)
        at = pl.ds(pl.multiple_of(shard * 96, 32), 96)
        copies.append(pltpu.make_async_copy(parts[k], w.at[at], sem.at[k]))
    if start:
        for copy in copies:
            copy.start()
    return copies


def load_rest(rest, wg, wo, sem, start=True):
    shards = rest.reshape(DP, 384, D)
    gates, outs = [], []
    if wg is not None:
        for h in range(2):
            into = wg.at[h].reshape(DP, 96, D)
            part = shards.at[:, pl.ds(96 * h, 96)]
            gates.append(pltpu.make_async_copy(part, into, sem.at[h]))
    if wo is not None:
        part = shards.at[:, pl.ds(192, 192)]
        outs.append(pltpu.make_async_copy(part, wo.reshape(DP, 192, D), sem.at[2]))
    if start:
        for copy in gates + outs:
            copy.start()
    return gates, outs


def finish_all(copies):
    for copy in copies:
        copy.wait()


def front(ready, cont, tok, halo, gin, cw, cb, dtb, alog, hc, *refs):
    parts, outs, (w, cif, csv, civ, uv, sem, osem, usem) = refs[:8], refs[8:15], refs[15:]
    u_out, ci_out, cs_out, sraw_out, dt_out, cum_out, pay = outs
    copies = load_weights(parts, w, sem)
    ready()
    x = jnp.concatenate([halo[...], tok[...]], axis=0).astype(F32)
    u = x * lax.rsqrt(jnp.mean(x * x, axis=1, keepdims=True) + EPS) * gin[...]
    uv[...] = u.astype(BF)
    u_copy = pltpu.make_async_copy(uv, u_out, usem)
    u_copy.start()
    keep = cont[0:1, 0:1]
    mask = jnp.where(iota((HALO + T, 1), 0) < HALO, keep, 1.0)
    finish_all(copies)
    sraw = mm(uv[HALO:, :], w[:, C:]) + dtb[...]
    sraw_out[...] = sraw
    dt = jnp.maximum(sraw, 0.0) + jnp.log1p(jnp.exp(-jnp.abs(sraw)))
    dt = jnp.where(lanes() < 2 * H, dt, 0.0)
    dt_out[...] = dt
    rate = jnp.where(lanes(1) < 2 * H, jnp.exp(alog[...]), 0.0)
    la = -dt * rate
    cum = jnp.where(
        lanes() < H,
        tri_sum(tri(lambda r, c: r >= c), la),
        tri_sum(tri(lambda r, c: r <= c), la),
    )
    cum_out[...] = cum
    last = ends(cum)
    tail_f, tail_r = pairs_of(jnp.exp(last - cum) * dt)
    dec_f, dec_r = pairs_of(jnp.broadcast_to(jnp.exp(last) * keep, (16, 128)))

    done, end = deliver([(csv, cs_out), (civ, ci_out)], osem)
    bc_out = [(csv, cs_out), (civ, ci_out)]
    bc_out = [
        pltpu.make_async_copy(a.at[:, E:], b.at[:, E:], osem.at[k, 2])
        for k, (a, b) in enumerate(bc_out)
    ]

    def convolve(i):
        at = wide(i)
        ci = (mm(uv[...], w[:, at]) * mask).astype(BF)
        civ[:, at] = ci
        for e in range(2):
            here = pl.ds(256 * i + 128 * e, 128)
            cif[e] = ci[:, 128 * e : 128 * e + 128].astype(F32)
            total = cb[:, here]
            for k in range(4):
                total = total + cw[k : k + 1, here] * cif[e, HALO - 3 + k : HALO - 3 + k + T]
            csv[:, here] = total
        return silu(csv[:, at])

    bf, _, br, _ = parts_of_bc(convolve(WIDE))
    for copy in bc_out:
        copy.start()
    bf_t, br_t = flip(bf), flip(br)

    def tile(i, _):
        at = wide(i)
        x_act = convolve(i)
        tf, tr, df, dr = mm_rows([tail_f, tail_r, dec_f, dec_r], hc[:, at])
        sf = mm(bf_t, (tf * x_act).astype(BF))
        sr = mm(br_t, (tr * x_act).astype(BF)) * keep
        done(i)
        put_slices(pay, i, sf, sr, df, dr)
        return 0

    each(WIDE, tile, 0)
    end()
    u_copy.wait()
    finish_all(bc_out)


def scan_blocks(recv, out):
    carry = jnp.zeros((16, 384), F32)
    back = jnp.zeros((16, 384), F32)
    for i in range(SEQ):
        k = SEQ - 1 - i
        out[i, 0:16] = carry.astype(BF)
        out[k, 16:32] = back.astype(BF)
        dec = recv[i, 32:48].astype(F32)
        carry = (dec[0:1] + dec[1:2]) * carry + recv[i, 0:16].astype(F32)
        dec = recv[k, 32:48].astype(F32)
        back = (dec[2:3] + dec[3:4]) * back + recv[k, 16:32].astype(F32)


def columns_of(cum2, col, base=0):
    for h in range(col.shape[0]):
        col[h] = jnp.broadcast_to(cum2[:, base + h : base + h + 1], (T, 128))


def by_head(v):
    head = iota((T, 256), 1) >> 6
    return [jnp.where(head == e, v, 0.0).astype(BF) for e in range(4)]


def low_full(left, right):
    right = jnp.concatenate([jnp.zeros((128, 128), right.dtype), right], axis=0)
    return jnp.concatenate([left, right], axis=1)


def up_full(left, right):
    left = jnp.concatenate([left, jnp.zeros((128, 128), left.dtype)], axis=0)
    return jnp.concatenate([left, right], axis=1)


def local_mix(dt, cum, dsk, hc, cs, ylf, ylr, base, *scratch):
    csv, yfv, yrv, bsv, col, row, gf, gr, bsem, sem, osem = scratch
    bc = pltpu.make_async_copy(cs.at[:, E:], csv.at[:, E:], bsem)
    bc.start()
    wait = fetch([(cs, csv)], sem)
    cum2 = cum[...] * LOG2E
    row[...] = cum2.T
    columns_of(cum2, col)
    dt_f, dt_r = pairs_of(dt[...])
    bc.wait()
    bf, cf, br, cr = parts_of_bc(silu(csv[:, E:]))
    r, c = iota((T, T), 0), iota((T, T), 1)
    gf[...] = jnp.where(r > c, mm_nt(cf, bf), 0.0)
    gr[...] = jnp.where(r < c, mm_nt(cr, br), 0.0)

    def weights(h, forward):
        at, along = col[h], row[h : h + 1, :]
        if forward:
            left = jnp.exp2(jnp.minimum(at - along[:, :128], 0.0)) * gf[:, :128]
            right = jnp.exp2(jnp.minimum(at[128:] - along[:, 128:], 0.0)) * gf[128:, 128:]
            return low_full(left.astype(BF), right.astype(BF))
        left = jnp.exp2(jnp.minimum(at[:128] - along[:, :128], 0.0)) * gr[:128, :128]
        right = jnp.exp2(jnp.minimum(at - along[:, 128:], 0.0)) * gr[:, 128:]
        return up_full(left.astype(BF), right.astype(BF))

    done, end = deliver([(yfv, ylf), (yrv, ylr), (bsv, base)], osem)

    def tile(i, _):
        at = wide(i)
        wait(i)
        x = silu(csv[:, at])
        total = dsk[:, at] * x
        dts = mm_rows([dt_f, dt_r], hc[:, at])
        for forward, first, spread, y in ((True, 0, dts[0], yfv), (False, H, dts[1], yrv)):
            xs = by_head(x * spread)
            left = jnp.concatenate([weights(first + 4 * i + e, forward) for e in range(4)], axis=1)
            own = mm(left, jnp.concatenate(xs, axis=0))
            y[:, at] = own
            total = total + own
        bsv[:, at] = total
        done(i)
        return 0

    each(WIDE, tile, 0)
    end()


def gate_products(u, dout, rest, gate, dn, wg, wo, gv, dv, sem, osem):
    gates, outs = load_rest(rest, wg, wo, sem)
    copies = []

    def put(k, value, src, dst, at):
        src[:, at] = value.astype(BF)
        copies.append(pltpu.make_async_copy(src.at[:, at], dst.at[:, at], osem.at[k]))
        copies[-1].start()

    finish_all(gates)
    put(0, mm(u[HALO:, :], wg[0]), gv, gate, slice(0, D))
    put(1, mm(u[HALO:, :], wg[1]), gv, gate, slice(D, E))
    finish_all(outs)
    put(2, mm_nt(dout[...], wo[:D]), dv, dn, slice(0, D))
    put(3, mm_nt(dout[...], wo[D:]), dv, dn, slice(D, E))
    finish_all(copies)


def gated_norm(ready, cont, cum, recv, gout, hc, cs, base, gate, dn, *refs):
    (n16, dg16, dm16, dgout, pay), scratch = refs[:5], refs[5:]
    bcv, yv, gv, dv, gds, sls, eff, efr, decs, nv, dgv, dmv, sf, sr, bsem, sem, osem = scratch
    bc = pltpu.make_async_copy(cs.at[:, E:], bcv, bsem)
    bc.start()
    wait = fetch([(base, yv), (gate, gv), (dn, dv)], sem)
    ready()
    keep = cont[0:1, 0:1]
    take_slices(recv, sf, sr, keep)
    cumv = cum[...]
    ef_f, ef_r = pairs_of(jnp.exp(cumv))
    dec_f, dec_r = pairs_of(jnp.broadcast_to(jnp.exp(ends(cumv)) * keep, (16, 128)))
    bc.wait()
    _, cf, _, cr = parts_of_bc(silu(bcv[...]))
    zero = jnp.zeros((T, 128), F32)

    def first(i, sums):
        at = wide(i)
        wait(i)
        ef, er, decs[0, :, at], decs[1, :, at] = mm_rows([ef_f, ef_r, dec_f, dec_r], hc[:, at])
        eff[:, at] = ef
        efr[:, at] = er
        m = yv[:, at] + ef * mm(cf, sf[:, at]) + er * mm(cr, sr[:, at])
        g = gv[:, at].astype(F32)
        sg = sigmoid(g)
        sl = g * sg
        gd = m * sl
        gds[:, at] = gd
        sls[:, at] = sl
        yv[:, at] = m * sg * (1.0 + g * (1.0 - sg))
        squares, crossed = gd * gd, dv[:, at].astype(F32) * gout[:, at] * gd
        return (
            sums[0] + squares[:, :128] + squares[:, 128:],
            sums[1] + crossed[:, :128] + crossed[:, 128:],
        )

    squares, crossed = each(WIDE, first, (zero, zero))
    rs = lax.rsqrt(jnp.sum(squares, axis=1, keepdims=True) / E + EPS)
    pull = jnp.sum(crossed, axis=1, keepdims=True) / E * (rs * rs * rs)
    cf_t, cr_t = flip(cf), flip(cr)

    done, end = deliver([(nv, n16), (dgv, dg16), (dmv, dm16)], osem)

    def second(i, _):
        at = wide(i)
        gd = gds[:, at]
        gdr = gd * rs
        go = gout[:, at]
        nv[:, at] = (gdr * go).astype(BF)
        d = dv[:, at].astype(F32)
        dgout[:, at] = jnp.sum(d * gdr, axis=0, keepdims=True)
        dgd = rs * (d * go) - gd * pull
        dgv[:, at] = (dgd * yv[:, at]).astype(BF)
        dm = dgd * sls[:, at]
        dmv[:, at] = dm.astype(BF)
        done(i)
        lf = mm(cf_t, (eff[:, at] * dm).astype(BF)) * keep
        lr = mm(cr_t, (efr[:, at] * dm).astype(BF))
        put_slices(pay, i, lr, lf, decs[1, :, at], decs[0, :, at])
        return 0

    each(WIDE, second, 0)
    end()


def grads_and_rows(
    ready, cont, cum, recv, hc, hr, dout, n16, u, dg16, dm16, cs, ylf, ylr, rows, dc, grads,
    *scratch
):
    n_t, u_t, dwo, dwg, bcv, yfv, yrv, sf, sr, doutv, nv, uv, dgv, dmv = scratch[:14]
    lsem, sem, osem = scratch[14:]
    loads = [(dout, doutv), (n16, nv), (u, uv), (dg16, dgv), (cs.at[:, E:], bcv)]
    loads = [pltpu.make_async_copy(a, b, lsem.at[k]) for k, (a, b) in enumerate(loads)]
    for copy in loads:
        copy.start()
    finish_all(loads[:2])
    wait = fetch([(ylf, yfv), (ylr, yrv), (dm16, dmv)], sem)
    n_t[...] = flip(nv[...])

    def columns_out(i, _):
        at = wide(i)
        dwo[:, at] = mm(n_t[...], doutv[:, at]).astype(BF)
        return 0

    def columns_gate(i, _):
        at = wide(i)
        dwg[:, at] = mm(u_t[...], dgv[:, at]).astype(BF)
        return 0

    each(D // 256, columns_out, 0)
    finish_all(loads[2:4])
    u_t[...] = flip(uv[HALO:, :])
    each(WIDE, columns_gate, 0)
    shards = grads.reshape(DP, 384, D)
    gate_rows = dwg.reshape(DP, 96, E)
    outward = [
        (gate_rows.at[:, :, pl.ds(0, D)], shards.at[:, pl.ds(0, 96)]),
        (gate_rows.at[:, :, pl.ds(D, D)], shards.at[:, pl.ds(96, 96)]),
        (dwo.reshape(DP, 192, D), shards.at[:, pl.ds(192, 192)]),
    ]
    outward = [pltpu.make_async_copy(a, b, osem.at[k]) for k, (a, b) in enumerate(outward)]
    for copy in outward:
        copy.start()
    ready()
    take_slices(recv, sf, sr, cont[0:1, 0:1])
    ef_f, ef_r = pairs_of(jnp.exp(cum[...]))
    finish_all(loads[4:])
    _, cf, _, cr = parts_of_bc(silu(bcv[...]))

    def tile(i, sums):
        at = wide(i)
        wait(i)
        dm = dmv[:, at].astype(F32)
        new, halves = [], []
        efs = mm_rows([ef_f, ef_r], hc[:, at])
        for ef, c, s, yl in ((efs[0], cf, sf, yfv), (efs[1], cr, sr, yrv)):
            y = yl[:, at] + ef * mm(c, s[:, at])
            halves += split2(dm * y)
            new.append(mm_nt((ef * dm).astype(BF), s[:, at]))
        a, b, c, d = mm_rows(halves, hr[at, :])
        return sums[0] + a + b, sums[1] + new[0], sums[2] + c + d, sums[3] + new[1]

    zero, zn = jnp.zeros((T, 128), F32), jnp.zeros((T, N), F32)
    rf, dcf, rr, dcr = each(WIDE, tile, (zero, zn, zero, zn))
    rows[...] = rf + to_back(rr)
    dc[...] = jnp.concatenate([dcf, dcr], axis=1)
    finish_all(outward)


def project_out(tok, n16, rest, out, wo, sem):
    finish_all(load_rest(rest, None, wo, sem)[1])
    out[...] = (tok[...].astype(F32) + mm(n16[...], wo[...])).astype(BF)


def local_back(ready, dt, cum, dm16, hc, hr, cs, zf, zr, dgf, dgr, inner, *scratch):
    csv, zfv, zrv, col, row, gf, gr, dm_t, sem, osem = scratch
    bc = pltpu.make_async_copy(cs.at[:, E:], csv.at[:, E:], sem.at[0, 2])
    bc.start()
    wait = fetch([(cs, csv)], sem)
    ready()
    cum2 = cum[...] * LOG2E
    row[...] = cum2.T
    columns_of(cum2, col)
    dm_t[...] = flip(dm16[...])
    dt_f, dt_r = pairs_of(dt[...])
    bc.wait()
    bf, cf, br, cr = parts_of_bc(silu(csv[:, E:]))
    s, t = iota((T, T), 0), iota((T, T), 1)
    gf[...] = jnp.where(t > s, mm_nt(bf, cf), 0.0)
    gr[...] = jnp.where(t < s, mm_nt(br, cr), 0.0)
    dgf[...] = jnp.zeros((T, T), F32)
    dgr[...] = jnp.zeros((T, T), F32)

    done, end = deliver([(zfv, zf), (zrv, zr)], osem)

    def tile(i, sums):
        at = wide(i)
        wait(i)
        x = silu(csv[:, at])
        xd = [x * spread for spread in mm_rows([dt_f, dt_r], hc[:, at])]
        dws = mm_rows(by_head(xd[0]) + by_head(xd[1]), dm_t[at, :])
        all_w = []
        for forward, first, g, dg in ((True, 0, gf, dgf), (False, H, gr, dgr)):
            ws = []
            small = jnp.zeros((128, 128), F32)
            large = jnp.zeros((T, 128), F32)
            for e in range(4):
                h = first + 4 * i + e
                at_s, along = col[h], row[h : h + 1, :]
                dw = dws[e if forward else 4 + e]
                if forward:
                    ea = jnp.exp2(jnp.minimum(along[:, :128] - at_s[:128], 0.0))
                    eb = jnp.exp2(jnp.minimum(along[:, 128:] - at_s, 0.0))
                    ws.append(
                        up_full((ea * g[:128, :128]).astype(BF), (eb * g[:, 128:]).astype(BF))
                    )
                    small = small + ea * dw[:128, :128]
                    large = large + eb * dw[:, 128:]
                else:
                    ea = jnp.exp2(jnp.minimum(along[:, :128] - at_s, 0.0))
                    eb = jnp.exp2(jnp.minimum(along[:, 128:] - at_s[128:], 0.0))
                    ws.append(
                        low_full((ea * g[:, :128]).astype(BF), (eb * g[128:, 128:]).astype(BF))
                    )
                    large = large + ea * dw[:, :128]
                    small = small + eb * dw[128:, 128:]
            all_w.append(jnp.concatenate(ws, axis=1))
            if forward:
                dg[:128, :128] += small
                dg[:, 128:] += large
            else:
                dg[:, :128] += large
                dg[128:, 128:] += small
        totals = mm_rows(all_w, jnp.concatenate(by_head(dm16[:, at].astype(F32)), axis=0))
        zfv[:, at], zrv[:, at] = totals[0].astype(BF), totals[1].astype(BF)
        halves = [t for k in range(2) for t in split2(xd[k].astype(BF).astype(F32) * totals[k])]
        done(i)
        a, b, c, d = mm_rows(halves, hr[at, :])
        return sums[0] + a + b, sums[1] + c + d

    zero = jnp.zeros((T, 128), F32)
    sums = each(WIDE, tile, (zero, zero))
    inner[...] = sums[0] + to_back(sums[1])
    dgf[...] = jnp.where(t > s, dgf[...], 0.0)
    dgr[...] = jnp.where(t < s, dgr[...], 0.0)
    end()


def inner_back(
    ready, cont, halo, gin, cw, alog, dsk, sraw, dt, cum, back, fore, rows, inner, dc, dgout, hc, hr,
    dgf, dgr, tok, dout, cs, zf, zr, dm16, ci, dg16, rest, *refs
):
    parts, (dtok, dhalo, dall_out, small_out), scratch = refs[:8], refs[8:12], refs[12:]
    csv, zfv, zrv, dmv, civ, dgv, w, wg, sf, sr, kf, kr, dcs, cif, du, small = scratch[:16]
    line, dall, gfv, grv, tokv, doutv, sem, csem, wsem, gsem, osem = scratch[16:]
    first = [(cs.at[:, E:], csv.at[:, E:])]
    bcc = pltpu.make_async_copy(*first[0], csem.at[0])
    bcc.start()
    wait = fetch([(cs, csv), (zf, zfv), (zr, zrv), (dm16, dmv)], sem)
    later = [(dgf, gfv), (dgr, grv), (ci, civ), (dg16, dgv), (tok, tokv), (dout, doutv)]
    later = [pltpu.make_async_copy(a, b, csem.at[1 + k]) for k, (a, b) in enumerate(later)]
    ready()
    keep = cont[0:1, 0:1]
    take_slices(back, kr, kf, keep)
    take_slices(fore, sf, sr, keep)
    cumv, dtv = cum[...], dt[...]
    last = ends(cumv)
    te_f, te_r = pairs_of(jnp.exp(last - cumv))
    dt_f, dt_r = pairs_of(dtv)
    line[...] = jnp.zeros((8, E), F32)
    dcs[:, 0:HALO] = jnp.zeros((C // 128, HALO, 128), F32)
    dcs[:, HALO + T :] = jnp.zeros((C // 128, 16, 128), F32)
    bcc.wait()
    bc = csv[:, E:]
    bf, cf, br, cr = parts_of_bc(silu(bc))

    def weights():
        gates = load_rest(rest, wg, None, gsem, False)[0]
        return load_weights(parts, w, wsem, False) + gates

    def slope(v, sg):
        return sg * (1.0 + v * (1.0 - sg))

    def tile(i, sums):
        at = wide(i)

        if i in (1, 3):
            for copy in later if i == 1 else weights():
                copy.start()

        wait(i)
        v = csv[:, at]
        sg = sigmoid(v)
        x = v * sg
        dm = dmv[:, at].astype(F32)
        line[2:3, at] = jnp.sum(dm * x, axis=0, keepdims=True)
        dx = dsk[:, at] * dm
        new, ends_of = [], []
        for d, dt2, te2, z, k, s, b in (
            (0, dt_f, te_f, zfv, kf, sf, bf),
            (1, dt_r, te_r, zrv, kr, sr, br),
        ):
            dts, te = mm(dt2, hc[:, at]), mm(te2, hc[:, at])
            xd = (x * dts).astype(BF).astype(F32)
            zt = te * mm(b, k[:, at])
            dx = dx + dts * (z[:, at].astype(F32) + zt)
            ends_of.append((xd * zt).astype(BF))
            new.append(mm_nt((te * xd).astype(BF), k[:, at]))
            both = s[:, at].astype(F32) * k[:, at].astype(F32)
            line[d : d + 1, at] = jnp.sum(both, axis=0, keepdims=True)
        dx = dx * slope(v, sg)
        for e in range(2):
            dcs[2 * i + e, HALO : HALO + T] = dx[:, 128 * e : 128 * e + 128]
        tf, tr = mm_rows(ends_of, hr[at, :])
        return sums[0] + tf, sums[1] + new[0], sums[2] + tr, sums[3] + new[1]

    zero, zn = jnp.zeros((T, 128), F32), jnp.zeros((T, N), F32)
    sums = each(WIDE, tile, (zero, zn, zero, zn))
    tails = sums[0] + to_back(sums[2])
    finish_all(later)
    gf16, gr16 = gfv[...].astype(BF), grv[...].astype(BF)
    dbf = sums[1] + mm(gf16, cf)
    dbr = sums[3] + mm(gr16, cr)
    dcf = dc[:, :N] + mm(flip(gf16), bf)
    dcr = dc[:, N:] + mm(flip(gr16), br)
    dbc = jnp.concatenate([dbf, dcf, dbr, dcr], axis=1) * slope(bc, sigmoid(bc))
    for e in range(2):
        dcs[2 * WIDE + e, HALO : HALO + T] = dbc[:, 128 * e : 128 * e + 128]
    hi, lo = split2(line[...])
    heads = mm(hi, hr[...]) + mm(lo, hr[...])
    dots = heads[0:1] + to_back(heads)[1:2]
    rate = jnp.where(lanes(1) < 2 * H, jnp.exp(alog[...]), 0.0)
    v = rows[...] - inner[...]
    dla = jnp.where(
        lanes() < H,
        tri_sum(tri(lambda r, c: r <= c), v) + tri_sum(tri(lambda r, c: r > c), tails),
        tri_sum(tri(lambda r, c: r >= c), v) + tri_sum(tri(lambda r, c: r < c), tails),
    ) + jnp.exp(last) * dots
    sg = sigmoid(sraw[...])
    ratio = jnp.where(dtv > 1e-20, sg / jnp.maximum(dtv, 1e-20), 1.0)
    dstep = (inner[...] + tails) * ratio - dla * rate * sg
    dstep = jnp.where(lanes() < 2 * H, dstep, 0.0)
    dall[0:HALO, C:] = jnp.zeros((HALO, 128), BF)
    dall[HALO:, C:] = dstep.astype(BF)
    dal = jnp.broadcast_to(jnp.sum(dla * (-dtv * rate), axis=0, keepdims=True), (8, 128))
    small[...] = jnp.zeros((96, 128), F32)
    small[88:89] = jnp.sum(dstep, axis=0, keepdims=True)
    small[89:90] = jnp.where(lanes(1) < H, dal[0:1] + to_front(dal)[0:1], 0.0)
    small[90:91] = jnp.where(lanes(1) < H, heads[2:3], 0.0)
    mask = jnp.where(iota((HALO + T, 1), 0) < HALO, keep, 1.0)

    half_out = [
        pltpu.make_async_copy(dall.at[:, at], dall_out.at[:, at], osem.at[k])
        for k, at in enumerate((pl.ds(0, 1024), pl.ds(1024, CD - 1024)))
    ]

    def convolution(i, _):
        at = pl.ds(128 * i, 128)
        g = dcs[i, HALO : HALO + T]
        cif[...] = civ[:, at].astype(F32)
        small[56 + i : 57 + i] = jnp.sum(g, axis=0, keepdims=True)
        total = jnp.zeros((HALO + T, 128), F32)
        for k in range(4):
            shifted = cif[HALO - 3 + k : HALO - 3 + k + T]
            small[14 * k + i : 14 * k + i + 1] = jnp.sum(g * shifted, axis=0, keepdims=True)
            total = total + cw[k : k + 1, at] * dcs[i, 3 - k : 3 - k + HALO + T]
        dall[:, at] = (total * mask).astype(BF)
        if i == 7:
            half_out[0].start()
        return 0

    each(C // 128, convolution, 0)
    half_out[1].start()
    for j in range(E // 128):
        small[70 + j : 71 + j] = dgout[:, 128 * j : 128 * j + 128]
    finish_all(weights())

    def input_grad(i, _):
        at = wide(i)
        du[:, at] = mm_nt(dall[...], w[at, :])
        du[HALO:, at] += mm_nt(dgv[:, :D], wg[0, at, :]) + mm_nt(dgv[:, D:], wg[1, at, :])
        return 0

    each(D // 256, input_grad, 0)
    x = jnp.concatenate([halo[...], tokv[...]], axis=0).astype(F32)
    r = lax.rsqrt(jnp.mean(x * x, axis=1, keepdims=True) + EPS)
    duxr = jnp.sum(du[...] * x * r, axis=0, keepdims=True)
    for j in range(6):
        small[82 + j : 83 + j] = duxr[:, 128 * j : 128 * j + 128]
    small_out[...] = small[...].astype(BF)
    dxh = du[...] * gin[...]
    dx = r * dxh - x * (r * r * r * jnp.mean(dxh * x, axis=1, keepdims=True))
    dhalo[...] = dx[:HALO]
    dtok[...] = doutv[...].astype(F32) + dx[HALO:]
    finish_all(half_out)


def weight_back(ready, u, dall, small, keep, send, u_t, dw, osem):
    ready()
    y, core, _ = place()
    u_t[...] = flip(u[...])
    for d in range(DP):
        dw[96 * d : 96 * d + 96, CD:] = small[...]

    def piece(d, ref):
        where = lax.rem(d // 2 + 4 - y, 4)
        return pltpu.make_async_copy(dw.at[pl.ds(96 * d, 96)], ref.at[where], osem.at[d])

    def for_piece(d, act):
        mine = core == d % 2

        @pl.when(mine)
        def _():
            act(piece(d, keep))

        @pl.when(jnp.logical_not(mine))
        def _():
            act(piece(d, send))

    done = 0
    for c in range(D // 256):
        at = slice(256 * c, 256 * c + 256)
        dw[at, :CD] = mm(u_t[at, :], dall[...]).astype(BF)
        while 96 * (done + 1) <= 256 * (c + 1):
            for_piece(done, lambda copy: copy.start())
            done += 1
    for d in range(DP):
        for_piece(d, lambda copy: copy.wait())


def add_pairs(a, b, whole, one, three, mine, other):
    for k, out in ((0, whole), (1, one), (3, three)):

        def rows(i, _, k=k, out=out):
            at = pl.ds(pl.multiple_of(i * 48, 16), 48)
            out[at] = (a[k, at].astype(F32) + b[k, at].astype(F32)).astype(BF)
            return 0

        lax.fori_loop(0, 2, rows, 0)
    _, _, parity = place()
    for out, half in ((mine, parity), (other, 1 - parity)):
        at = pl.ds(pl.multiple_of(half * 1024, 1024), 1024)
        out[...] = (a[2, :, at].astype(F32) + b[2, :, at].astype(F32)).astype(BF)


def add_two(a, b, out):
    out[...] = (a[...].astype(F32) + b[...].astype(F32)).astype(BF)


def add_y(rest, whole, one, three, half, out):
    _, _, parity = place()
    for j in range(6):
        for r in range(0, 384, 48):
            row = 384 * j + r
            out[row // 144, row % 144 : row % 144 + 48] = rest[
                r : r + 48, 128 * j : 128 * j + 128
            ]
    for j in range(SEQ):
        at, in_half = slice(128 * j, 128 * j + 128), slice(128 * (j % 8), 128 * (j % 8) + 128)
        mine = jnp.where(parity == j // 8, 1.0, 0.0)
        total = sum(part[:, at].astype(F32) for part in (whole, one, three))
        out[j, 144:] = (total + half[:, in_half].astype(F32) * mine).astype(BF)


def add_blocks(recv, out):
    total = recv[0].astype(F32)
    for i in range(1, SEQ):
        total = total + recv[i].astype(F32)
    low = total.astype(BF)
    for i in range(SEQ):
        out[i] = low


def finish(sums, dwin, dwdt, dwout, dcw, dcb, dgout, dgin, ddtb, dal, ddsk):
    def put(ref, at, start, rows):
        for r in range(0, rows, 48):
            j, k = (start + r) // 144, (start + r) % 144
            ref[r : r + 48, at] = sums[j, k : k + 48].astype(F32)

    for j in range(6):
        at = slice(128 * j, 128 * j + 128)
        put(dwin, at, 384 * j, 96)
        put(dwin, slice(D + 128 * j, D + 128 * j + 128), 384 * j + 96, 96)
        put(dwout, at, 384 * j + 192, 192)
    for j in range(14):
        dwin[:, E + 128 * j : E + 128 * j + 128] = sums[j, 144:].astype(F32)
    dwdt[...] = sums[14, 144:].astype(F32).T[: 2 * H]
    small = sums[15, 144:].astype(F32)
    for j in range(14):
        at = slice(128 * j, 128 * j + 128)
        for k in range(4):
            dcw[k : k + 1, at] = small[14 * k + j : 14 * k + j + 1]
        dcb[at] = small[56 + j]
    for j in range(E // 128):
        dgout[128 * j : 128 * j + 128] = small[70 + j]
    for j in range(6):
        dgin[128 * j : 128 * j + 128] = small[82 + j]
    ddtb[...] = small[88, 0 : 2 * H]
    dal[...] = small[89, 0:H]
    ddsk[...] = small[90, 0:H]


V = pl.BlockSpec(memory_space=pltpu.VMEM)
ANY = pl.BlockSpec(memory_space=pl.ANY)


def shape(*dims, dtype=F32):
    return jax.ShapeDtypeStruct(dims, dtype)


def nothing():
    pass


def staged(kernel, ins, outs, scratch):
    held = [i for i, (spec, _) in enumerate(ins) if spec is V]
    more = [pltpu.VMEM(ins[i][1].shape, ins[i][1].dtype) for i in held]
    more.append(pltpu.SemaphoreType.DMA((len(held),)))

    def run(*refs):
        refs = list(refs)
        buffers, sem = refs[len(refs) - len(more) : -1], refs[-1]
        copies = []
        for k, i in enumerate(held):
            copies.append(pltpu.make_async_copy(refs[i], buffers[k], sem.at[k]))
            copies[-1].start()
            refs[i] = buffers[k]
        kernel(lambda: finish_all(copies), *refs[: len(refs) - len(more)])

    return run, [(ANY, a) for _, a in ins], list(scratch) + more


def call(kernel, name, ins, outs, scratch=(), flops=0, apart=(), limit=VMEM, stage=False):
    if stage:
        kernel, ins, scratch = staged(kernel, ins, outs, scratch)
    specs, args = zip(*ins)
    moved = sum(a.size * a.dtype.itemsize for a in args)
    moved += sum(o.size * o.dtype.itemsize for o in outs)
    return pl.pallas_call(
        kernel,
        name=name,
        out_shape=tuple(outs),
        in_specs=list(specs),
        out_specs=tuple(ANY if i in apart else V for i in range(len(outs))),
        scratch_shapes=list(scratch),
        cost_estimate=pl.CostEstimate(flops=flops, bytes_accessed=moved, transcendentals=0),
        compiler_params=pltpu.CompilerParams(vmem_limit_bytes=limit),
    )(*args)


def vm(*dims, dtype=F32):
    return pltpu.VMEM(dims, dtype)


def shift_y(k):
    return [(2 * y + c, 2 * ((y + k) % 4) + c) for y in range(4) for c in range(2)]


SWAP = [(i, i ^ 1) for i in range(DP)]
NEXT_Z = [(i, i ^ 1) for i in range(SEQ)]


def exchange(value):
    return lax.all_to_all(value, "seq", 0, 0, tiled=True)


def together(*values):
    return lax.optimization_barrier(values)


def local(
    tokens, starts, g_in, w_in, w_dt, conv_w, conv_b, dt_bias, a_log, dskip, g_out, w_out, d_out
):
    tok, dout = tokens[0], d_out[0]
    cont = jnp.broadcast_to((1 - starts).astype(F32), (1, 128))

    row = lambda v: v.reshape(1, -1)
    pad = lambda v: jnp.pad(v, (0, 128 - v.shape[0])).reshape(1, 128)
    alog = pad(jnp.concatenate([a_log, a_log]))
    dsk = row(jnp.repeat(dskip, N))
    gin, gout, cb, dtb = row(g_in), row(g_out), row(conv_b), pad(dt_bias)
    own = jnp.concatenate([w_in[:, E:], jnp.pad(w_dt, ((0, 0), (0, 128 - 2 * H)))], axis=1)
    column = [lax.ppermute(own, "dp", shift_y(k)) for k in (1, 2, 3)]
    halo = lax.ppermute(tok[-HALO:], "seq", [(i, i + 1) for i in range(SEQ - 1)])
    beside = lax.ppermute(own, "dp", SWAP)
    rest_own = jnp.concatenate([w_in[:, :D], w_in[:, D:E], w_out], axis=0)
    hc, hr = marks()
    *column, halo, beside, rest_own, alog, dsk, gin, gout, cb, dtb, cont, hc, hr = together(
        *column, halo, beside, rest_own, alog, dsk, gin, gout, cb, dtb, cont, hc, hr
    )
    parts = [own, *column, beside] + [lax.ppermute(part, "dp", SWAP) for part in column]
    rest = lax.all_gather(rest_own, "dp", axis=0, tiled=True)

    part_ins = [(ANY, part) for part in parts]
    w_scratch = vm(D, CD, dtype=BF)
    dma = pltpu.SemaphoreType.DMA
    full, half, state = vm(T, E), vm(T, E, dtype=BF), vm(N, E, dtype=BF)

    u, ci, cs, sraw, dt, cum, pay = call(
        front,
        "front",
        [(V, cont), (V, tok), (V, halo), (V, gin), (V, conv_w), (V, cb)]
        + [(V, dtb), (V, alog), (V, hc)]
        + part_ins,
        [shape(HALO + T, D, dtype=BF), shape(HALO + T, C, dtype=BF), shape(T, C)]
        + [shape(T, 128)] * 3
        + [shape(SEQ, 48, 384, dtype=BF)],
        [w_scratch, vm(2, HALO + T, 128), vm(T, C), vm(HALO + T, C, dtype=BF)]
        + [vm(HALO + T, D, dtype=BF), dma((8,)), dma((2, 3)), dma(())],
        flops=2 * T * D * CD,
        apart=(0, 1, 2),
        stage=True,
    )

    def scan(got, name):
        out = shape(SEQ, 32, 384, dtype=BF)
        return call(scan_blocks, name, [(V, got)], [out], limit=SMALL)[0]

    got = exchange(pay)
    ylf, ylr, base = call(
        local_mix,
        "local_mix",
        [(V, dt), (V, cum), (V, dsk), (V, hc), (ANY, cs)],
        [shape(T, E)] * 3,
        [vm(T, C), full, full, full, vm(2 * H, T, 128), vm(128, T), vm(T, T), vm(T, T)]
        + [dma(()), dma((1, 2)), dma((3, 2))],
        flops=4 * 24 * T * T * 256,
        apart=(0, 1, 2),
    )
    got, ylr, base = together(got, ylr, base)
    fore = exchange(scan(got, "scan_states"))
    gate, dn = call(
        gate_products,
        "gate_products",
        [(V, u), (V, dout), (ANY, rest)],
        [shape(T, E, dtype=BF)] * 2,
        [vm(2, D, D, dtype=BF), vm(E, D, dtype=BF), half, half, dma((3,)), dma((4,))],
        flops=4 * T * D * E,
        apart=(0, 1),
    )
    n16, dg16, dm16, dgout, pay_back = call(
        gated_norm,
        "gated_norm",
        [(V, cont), (V, cum), (V, fore), (V, gout), (V, hc)]
        + [(ANY, a) for a in (cs, base, gate, dn)],
        [shape(T, E, dtype=BF)] * 3 + [shape(1, E), shape(SEQ, 48, 384, dtype=BF)],
        [vm(T, 256), full, half, half] + [full] * 4 + [vm(2, 16, E)] + [half] * 3 + [state] * 2
        + [dma(()), dma((3, 2)), dma((3, 2))],
        flops=12 * T * N * E,
        apart=(0, 1, 2),
        stage=True,
    )
    got = exchange(pay_back)
    rows, dc, rest_grads = call(
        grads_and_rows,
        "grads_and_rows",
        [(V, cont)]
        + [(V, a) for a in (cum, fore, hc, hr)]
        + [(ANY, a) for a in (dout, n16, u, dg16, dm16, cs, ylf, ylr)],
        [shape(T, 128), shape(T, 128), shape(DP * 384, D, dtype=BF)],
        [vm(E, T, dtype=BF), vm(D, T, dtype=BF), vm(E, D, dtype=BF), vm(D, E, dtype=BF)]
        + [vm(T, 256), full, full, state, state, vm(T, D, dtype=BF), half]
        + [vm(HALO + T, D, dtype=BF), half, half]
        + [dma((5,)), dma((3, 2)), dma((3,))],
        flops=8 * T * D * E,
        apart=(2,),
        stage=True,
    )
    got, rows, rest_grads = together(got, rows, rest_grads)
    rest_sum = lax.psum_scatter(rest_grads, "dp", scatter_dimension=0, tiled=True)
    back = exchange(scan(got, "scan_adjoints"))
    zf, zr, dgf, dgr, inner = call(
        partial(local_back, nothing),
        "local_back",
        [(V, dt), (V, cum), (V, dm16), (V, hc), (V, hr), (ANY, cs)],
        [shape(T, E, dtype=BF)] * 2 + [shape(T, T)] * 2 + [shape(T, 128)],
        [vm(T, C), half, half, vm(2 * H, T, 128), vm(128, T), vm(T, T), vm(T, T)]
        + [vm(E, T, dtype=BF), dma((1, 3)), dma((2, 2))],
        flops=4 * 48 * T * T * 256,
        apart=(0, 1),
    )
    dtok, dhalo, dall, small = call(
        partial(inner_back, nothing),
        "inner_back",
        [(V, cont)]
        + [(V, a) for a in (halo, gin, conv_w, alog, dsk, sraw, dt, cum, back, fore, rows)]
        + [(V, a) for a in (inner, dc, dgout, hc, hr)]
        + [(ANY, a) for a in (dgf, dgr, tok, dout, cs, zf, zr, dm16, ci, dg16, rest)]
        + part_ins,
        [shape(T, D), shape(HALO, D), shape(HALO + T, CD, dtype=BF), shape(96, 128, dtype=BF)],
        [vm(T, C), half, half, half, vm(HALO + T, C, dtype=BF), half, w_scratch]
        + [vm(2, D, D, dtype=BF)]
        + [state] * 4
        + [vm(C // 128, HALO + T + 16, 128), vm(HALO + T, 128), vm(HALO + T, D), vm(96, 128)]
        + [vm(8, E), vm(HALO + T, CD, dtype=BF), vm(T, T), vm(T, T)]
        + [vm(T, D, dtype=BF), vm(T, D, dtype=BF)]
        + [dma((4, 2)), dma((7,)), dma((8,)), dma((3,)), dma((2,))],
        flops=2 * T * D * (CD + E),
        apart=(2,),
    )
    keep, send = call(
        partial(weight_back, nothing),
        "weight_back",
        [(V, u), (V, dall), (V, small)],
        [shape(4, 96, 2048, dtype=BF)] * 2,
        [vm(D, HALO + T, dtype=BF), vm(D, 2048, dtype=BF), dma((8,))],
        flops=2 * T * D * CD,
        apart=(0, 1),
        limit=16 * 1024 * 1024,
    )
    recv = lax.ppermute(send, "dp", SWAP)
    whole, one, three, mine, other = call(
        add_pairs,
        "add_tail_cores",
        [(V, keep), (V, recv)],
        [shape(96, 2048, dtype=BF)] * 3 + [shape(96, 1024, dtype=BF)] * 2,
        limit=SMALL,
    )
    other = lax.ppermute(other, "seq", NEXT_Z)
    one, three = lax.ppermute(one, "dp", shift_y(1)), lax.ppermute(three, "dp", shift_y(3))
    sides = [(V, mine), (V, other)]
    half = call(add_two, "add_tail_z", sides, [shape(96, 1024, dtype=BF)], limit=SMALL)[0]
    half, n16, dhalo = together(half, n16, dhalo)
    half = lax.ppermute(half, "dp", shift_y(2))
    dback = lax.ppermute(dhalo, "seq", [(i + 1, i) for i in range(SEQ - 1)])
    out = call(
        project_out,
        "project_out",
        [(V, tok), (V, n16), (ANY, rest)],
        [shape(T, D, dtype=BF)],
        [vm(E, D, dtype=BF), dma((3,))],
        flops=2 * T * D * E,
    )[0]
    dtok = dtok.at[-HALO:].add(dback)
    one, three, half, out, dtok = together(one, three, half, out, dtok)
    slices = shape(SEQ, 240, 128, dtype=BF)
    sums = [(V, part) for part in (rest_sum, whole, one, three, half)]
    sums = call(add_y, "add_y", sums, [slices], limit=SMALL)[0]
    sums = call(add_blocks, "add_seq", [(V, exchange(sums))], [slices], limit=SMALL)[0]
    dwin, dwdt, dwout, dcw, dcb, dgo, dgi, ddtb, dal, dds = call(
        finish,
        "finish",
        [(V, exchange(sums))],
        [shape(96, E + C), shape(2 * H, 96), shape(192, D), shape(4, C), shape(C)]
        + [shape(E), shape(D), shape(2 * H), shape(H), shape(H)],
        limit=SMALL,
    )
    return (
        out[None], dtok[None], dgi, dwin, dwdt.T, dcw, dcb, ddtb, dal, dds, dgo, dwout,
    )


def solution(mesh):
    split = P("dp", "seq", None)
    rows = P("dp", None)
    return jax.shard_map(
        local,
        mesh=mesh,
        in_specs=(split, P("dp", "seq"), P(), rows, rows, P(), P(), P(), P(), P(), P(), rows, split),
        out_specs=(split, split, P(), rows, rows, P(), P(), P(), P(), P(), P(), rows),
        check_vma=False,
    )
```

```python
from functools import partial

import jax
import jax.numpy as jnp
from jax import lax
from jax.experimental import pallas as pl
from jax.experimental.pallas import tpu as pltpu
from jax.sharding import PartitionSpec as P

F32, BF = jnp.float32, jnp.bfloat16
EPS = 1e-05
LOG2E = 1.4426950408889634
D, H, E, N, T = 768, 24, 1536, 64, 256
C = E + 4 * N
CD = C + 128
HALO = 16
WIDE = E // 256
DP, SEQ = 8, 16
VMEM = 56 * 1024 * 1024
SMALL = 12 * 1024 * 1024


def iota(shape, dim):
    return lax.broadcasted_iota(jnp.int32, shape, dim)


def mm(a, b):
    return jnp.dot(a, b, preferred_element_type=F32)


def mm_nt(a, b):
    return lax.dot_general(a, b, (((1,), (1,)), ((), ())), preferred_element_type=F32)


def mm_rows(parts, right):
    total = mm(jnp.concatenate(parts, axis=0), right)
    ends = [sum(p.shape[0] for p in parts[: k + 1]) for k in range(len(parts))]
    return [total[end - p.shape[0] : end] for end, p in zip(ends, parts)]


def flip(v):
    return v.astype(F32).T.astype(v.dtype)


def sigmoid(v):
    return 1.0 / (1.0 + jnp.exp(-v))


def silu(v):
    return v * sigmoid(v)


def split2(v):
    hi = v.astype(BF)
    return hi, (v - hi.astype(F32)).astype(BF)


def onehot(cond):
    return jnp.where(cond, 1.0, 0.0).astype(BF)


def marks():
    row, head = iota((64, E), 0), iota((64, E), 1) >> 6
    columns = onehot((row == head) | (row == head + H))
    return columns, onehot((iota((E, 128), 0) >> 6) == iota((E, 128), 1))


def to_front(v):
    return pltpu.roll(v, 128 - H, 1)


def to_back(v):
    return pltpu.roll(v, H, 1)


def pairs_of(v):
    def terms(v):
        hi = v.astype(BF).astype(F32)
        lane = lanes(v.shape[0])
        both = jnp.where(lane < H, hi, jnp.where(lane < 2 * H, to_back(v - hi), 0.0))
        return both[:, :64].astype(BF)

    return terms(v), terms(to_front(v))


def tri_sum(mask, v):
    hi = v.astype(BF)
    rest = v - hi.astype(F32)
    mid = rest.astype(BF)
    low = (rest - mid.astype(F32)).astype(BF)
    return mm(mask, hi) + mm(mask, mid) + mm(mask, low)


def tri(cond):
    return onehot(cond(iota((T, T), 0), iota((T, T), 1)))


def lanes(rows=T):
    return iota((rows, 128), 1)


def wide(i):
    return pl.ds(256 * i, 256)


def each(count, body, carry):
    for i in range(count):
        carry = body(i, carry)
    return carry


def fetch(sources, sems):
    def copies(k):
        at = (pl.ds(0, 256), pl.ds(256, E - 256))[k]
        return [
            pltpu.make_async_copy(src.at[:, at], dst.at[:, at], sems.at[n, k])
            for n, (src, dst) in enumerate(sources)
        ]

    for k in range(2):
        for copy in copies(k):
            copy.start()

    def wait(i):
        if i < 2:
            finish_all(copies(i))

    return wait


def deliver(targets, sems, tiles=WIDE):
    def copies(k):
        at = (pl.ds(0, 256 * (tiles - 1)), pl.ds(256 * (tiles - 1), 256))[k]
        return [
            pltpu.make_async_copy(src.at[:, at], dst.at[:, at], sems.at[n, k])
            for n, (src, dst) in enumerate(targets)
        ]

    def done(i):
        if i == tiles - 2:
            for copy in copies(0):
                copy.start()

    def end():
        for copy in copies(1):
            copy.start()
        finish_all(copies(0))
        finish_all(copies(1))

    return done, end


def parts_of_bc(act):
    return [act[:, N * k : N * k + N].astype(BF) for k in range(4)]


def ends(cum):
    return jnp.where(lanes(1) < H, cum[T - 1 : T], cum[0:1])


def put_slices(pay, i, first, second, dec_first, dec_second):
    row = iota((16, 128), 0)
    for e in range(2):
        at = slice(128 * e, 128 * e + 128)
        tile = 2 * i + e
        group, into = tile // 3, pl.ds(tile % 3 * 128, 128)
        a, b = dec_first[:, at], dec_second[:, at]
        ah, bh = a.astype(BF).astype(F32), b.astype(BF).astype(F32)
        dec = jnp.where(
            row == 0, ah, jnp.where(row == 1, a - ah, jnp.where(row == 2, bh, b - bh))
        )
        dec = jnp.where(row < 4, dec, 0.0).astype(BF)
        for q in range(4):
            j = 4 * group + q
            pay[j, 0:16, into] = first[16 * q : 16 * q + 16, at].astype(BF)
            pay[j, 16:32, into] = second[16 * q : 16 * q + 16, at].astype(BF)
            pay[j, 32:48, into] = dec


def take_slices(recv, first, second, first_scale):
    for j in range(SEQ):
        rows, at = pl.ds(16 * (j % 4), 16), pl.ds(384 * (j // 4), 384)
        first[rows, at] = (recv[j, 0:16].astype(F32) * first_scale).astype(BF)
        second[rows, at] = recv[j, 16:32]


def place():
    dp, seq = lax.axis_index("dp"), lax.axis_index("seq")
    return lax.div(dp, 2), lax.rem(dp, 2), lax.rem(seq, 2)


def load_weights(parts, w, sem, start=True):
    y, core, _ = place()
    copies = []
    for k in range(8):
        shard = 2 * lax.rem(y + 4 - k % 4, 4) + (core if k < 4 else 1 - core)
        at = pl.ds(pl.multiple_of(shard * 96, 32), 96)
        copies.append(pltpu.make_async_copy(parts[k], w.at[at], sem.at[k]))
    if start:
        for copy in copies:
            copy.start()
    return copies


def load_rest(rest, wg, wo, sem, start=True):
    shards = rest.reshape(DP, 384, D)
    gates, outs = [], []
    if wg is not None:
        for h in range(2):
            into = wg.at[h].reshape(DP, 96, D)
            part = shards.at[:, pl.ds(96 * h, 96)]
            gates.append(pltpu.make_async_copy(part, into, sem.at[h]))
    if wo is not None:
        part = shards.at[:, pl.ds(192, 192)]
        outs.append(pltpu.make_async_copy(part, wo.reshape(DP, 192, D), sem.at[2]))
    if start:
        for copy in gates + outs:
            copy.start()
    return gates, outs


def finish_all(copies):
    for copy in copies:
        copy.wait()


def front(ready, cont, tok, halo, gin, cw, cb, dtb, alog, hc, *refs):
    parts, outs, (w, cif, csv, civ, uv, sem, osem, usem) = refs[:8], refs[8:15], refs[15:]
    u_out, ci_out, cs_out, sraw_out, dt_out, cum_out, pay = outs
    copies = load_weights(parts, w, sem)
    ready()
    x = jnp.concatenate([halo[...], tok[...]], axis=0).astype(F32)
    u = x * lax.rsqrt(jnp.mean(x * x, axis=1, keepdims=True) + EPS) * gin[...]
    uv[...] = u.astype(BF)
    u_copy = pltpu.make_async_copy(uv, u_out, usem)
    u_copy.start()
    keep = cont[0:1, 0:1]
    mask = jnp.where(iota((HALO + T, 1), 0) < HALO, keep, 1.0)
    finish_all(copies)
    sraw = mm(uv[HALO:, :], w[:, C:]) + dtb[...]
    sraw_out[...] = sraw
    dt = jnp.maximum(sraw, 0.0) + jnp.log1p(jnp.exp(-jnp.abs(sraw)))
    dt = jnp.where(lanes() < 2 * H, dt, 0.0)
    dt_out[...] = dt
    rate = jnp.where(lanes(1) < 2 * H, jnp.exp(alog[...]), 0.0)
    la = -dt * rate
    cum = jnp.where(
        lanes() < H,
        tri_sum(tri(lambda r, c: r >= c), la),
        tri_sum(tri(lambda r, c: r <= c), la),
    )
    cum_out[...] = cum
    last = ends(cum)
    tail_f, tail_r = pairs_of(jnp.exp(last - cum) * dt)
    dec_f, dec_r = pairs_of(jnp.broadcast_to(jnp.exp(last) * keep, (16, 128)))

    done, end = deliver([(csv, cs_out), (civ, ci_out)], osem)
    bc_out = [(csv, cs_out), (civ, ci_out)]
    bc_out = [
        pltpu.make_async_copy(a.at[:, E:], b.at[:, E:], osem.at[k, 2])
        for k, (a, b) in enumerate(bc_out)
    ]

    def convolve(i):
        at = wide(i)
        ci = (mm(uv[...], w[:, at]) * mask).astype(BF)
        civ[:, at] = ci
        for e in range(2):
            here = pl.ds(256 * i + 128 * e, 128)
            cif[e] = ci[:, 128 * e : 128 * e + 128].astype(F32)
            total = cb[:, here]
            for k in range(4):
                total = total + cw[k : k + 1, here] * cif[e, HALO - 3 + k : HALO - 3 + k + T]
            csv[:, here] = total
        return silu(csv[:, at])

    bf, _, br, _ = parts_of_bc(convolve(WIDE))
    for copy in bc_out:
        copy.start()
    bf_t, br_t = flip(bf), flip(br)

    def tile(i, _):
        at = wide(i)
        x_act = convolve(i)
        tf, tr, df, dr = mm_rows([tail_f, tail_r, dec_f, dec_r], hc[:, at])
        sf = mm(bf_t, (tf * x_act).astype(BF))
        sr = mm(br_t, (tr * x_act).astype(BF)) * keep
        done(i)
        put_slices(pay, i, sf, sr, df, dr)
        return 0

    each(WIDE, tile, 0)
    end()
    u_copy.wait()
    finish_all(bc_out)


def scan_blocks(recv, out):
    carry = jnp.zeros((16, 384), F32)
    back = jnp.zeros((16, 384), F32)
    for i in range(SEQ):
        k = SEQ - 1 - i
        out[i, 0:16] = carry.astype(BF)
        out[k, 16:32] = back.astype(BF)
        dec = recv[i, 32:48].astype(F32)
        carry = (dec[0:1] + dec[1:2]) * carry + recv[i, 0:16].astype(F32)
        dec = recv[k, 32:48].astype(F32)
        back = (dec[2:3] + dec[3:4]) * back + recv[k, 16:32].astype(F32)


def columns_of(cum2, col, base=0):
    for h in range(col.shape[0]):
        col[h] = jnp.broadcast_to(cum2[:, base + h : base + h + 1], (T, 128))


def by_head(v):
    head = iota((T, 256), 1) >> 6
    return [jnp.where(head == e, v, 0.0).astype(BF) for e in range(4)]


def low_full(left, right):
    right = jnp.concatenate([jnp.zeros((128, 128), right.dtype), right], axis=0)
    return jnp.concatenate([left, right], axis=1)


def up_full(left, right):
    left = jnp.concatenate([left, jnp.zeros((128, 128), left.dtype)], axis=0)
    return jnp.concatenate([left, right], axis=1)


def local_mix(dt, cum, dsk, hc, cs, ylf, ylr, base, *scratch):
    csv, yfv, yrv, bsv, col, row, gf, gr, bsem, sem, osem = scratch
    bc = pltpu.make_async_copy(cs.at[:, E:], csv.at[:, E:], bsem)
    bc.start()
    wait = fetch([(cs, csv)], sem)
    cum2 = cum[...] * LOG2E
    row[...] = cum2.T
    columns_of(cum2, col)
    dt_f, dt_r = pairs_of(dt[...])
    bc.wait()
    bf, cf, br, cr = parts_of_bc(silu(csv[:, E:]))
    r, c = iota((T, T), 0), iota((T, T), 1)
    gf[...] = jnp.where(r > c, mm_nt(cf, bf), 0.0)
    gr[...] = jnp.where(r < c, mm_nt(cr, br), 0.0)

    def weights(h, forward):
        at, along = col[h], row[h : h + 1, :]
        if forward:
            left = jnp.exp2(jnp.minimum(at - along[:, :128], 0.0)) * gf[:, :128]
            right = jnp.exp2(jnp.minimum(at[128:] - along[:, 128:], 0.0)) * gf[128:, 128:]
            return low_full(left.astype(BF), right.astype(BF))
        left = jnp.exp2(jnp.minimum(at[:128] - along[:, :128], 0.0)) * gr[:128, :128]
        right = jnp.exp2(jnp.minimum(at - along[:, 128:], 0.0)) * gr[:, 128:]
        return up_full(left.astype(BF), right.astype(BF))

    done, end = deliver([(yfv, ylf), (yrv, ylr), (bsv, base)], osem)

    def tile(i, _):
        at = wide(i)
        wait(i)
        x = silu(csv[:, at])
        total = dsk[:, at] * x
        dts = mm_rows([dt_f, dt_r], hc[:, at])
        for forward, first, spread, y in ((True, 0, dts[0], yfv), (False, H, dts[1], yrv)):
            xs = by_head(x * spread)
            left = jnp.concatenate([weights(first + 4 * i + e, forward) for e in range(4)], axis=1)
            own = mm(left, jnp.concatenate(xs, axis=0))
            y[:, at] = own
            total = total + own
        bsv[:, at] = total
        done(i)
        return 0

    each(WIDE, tile, 0)
    end()


def gate_products(u, dout, rest, gate, dn, wg, wo, gv, dv, sem, osem):
    gates, outs = load_rest(rest, wg, wo, sem)
    copies = []

    def put(k, value, src, dst, at):
        src[:, at] = value.astype(BF)
        copies.append(pltpu.make_async_copy(src.at[:, at], dst.at[:, at], osem.at[k]))
        copies[-1].start()

    finish_all(gates)
    put(0, mm(u[HALO:, :], wg[0]), gv, gate, slice(0, D))
    put(1, mm(u[HALO:, :], wg[1]), gv, gate, slice(D, E))
    finish_all(outs)
    put(2, mm_nt(dout[...], wo[:D]), dv, dn, slice(0, D))
    put(3, mm_nt(dout[...], wo[D:]), dv, dn, slice(D, E))
    finish_all(copies)


def gated_norm(ready, cont, cum, recv, gout, hc, cs, base, gate, dn, *refs):
    (n16, dg16, dm16, dgout, pay), scratch = refs[:5], refs[5:]
    bcv, yv, gv, dv, gds, sls, eff, efr, decs, nv, dgv, dmv, sf, sr, bsem, sem, osem = scratch
    bc = pltpu.make_async_copy(cs.at[:, E:], bcv, bsem)
    bc.start()
    wait = fetch([(base, yv), (gate, gv), (dn, dv)], sem)
    ready()
    keep = cont[0:1, 0:1]
    take_slices(recv, sf, sr, keep)
    cumv = cum[...]
    ef_f, ef_r = pairs_of(jnp.exp(cumv))
    dec_f, dec_r = pairs_of(jnp.broadcast_to(jnp.exp(ends(cumv)) * keep, (16, 128)))
    bc.wait()
    _, cf, _, cr = parts_of_bc(silu(bcv[...]))
    zero = jnp.zeros((T, 128), F32)

    def first(i, sums):
        at = wide(i)
        wait(i)
        ef, er, decs[0, :, at], decs[1, :, at] = mm_rows([ef_f, ef_r, dec_f, dec_r], hc[:, at])
        eff[:, at] = ef
        efr[:, at] = er
        m = yv[:, at] + ef * mm(cf, sf[:, at]) + er * mm(cr, sr[:, at])
        g = gv[:, at].astype(F32)
        sg = sigmoid(g)
        sl = g * sg
        gd = m * sl
        gds[:, at] = gd
        sls[:, at] = sl
        yv[:, at] = m * sg * (1.0 + g * (1.0 - sg))
        squares, crossed = gd * gd, dv[:, at].astype(F32) * gout[:, at] * gd
        return (
            sums[0] + squares[:, :128] + squares[:, 128:],
            sums[1] + crossed[:, :128] + crossed[:, 128:],
        )

    squares, crossed = each(WIDE, first, (zero, zero))
    rs = lax.rsqrt(jnp.sum(squares, axis=1, keepdims=True) / E + EPS)
    pull = jnp.sum(crossed, axis=1, keepdims=True) / E * (rs * rs * rs)
    cf_t, cr_t = flip(cf), flip(cr)

    done, end = deliver([(nv, n16), (dgv, dg16), (dmv, dm16)], osem)

    def second(i, _):
        at = wide(i)
        gd = gds[:, at]
        gdr = gd * rs
        go = gout[:, at]
        nv[:, at] = (gdr * go).astype(BF)
        d = dv[:, at].astype(F32)
        dgout[:, at] = jnp.sum(d * gdr, axis=0, keepdims=True)
        dgd = rs * (d * go) - gd * pull
        dgv[:, at] = (dgd * yv[:, at]).astype(BF)
        dm = dgd * sls[:, at]
        dmv[:, at] = dm.astype(BF)
        done(i)
        lf = mm(cf_t, (eff[:, at] * dm).astype(BF)) * keep
        lr = mm(cr_t, (efr[:, at] * dm).astype(BF))
        put_slices(pay, i, lr, lf, decs[1, :, at], decs[0, :, at])
        return 0

    each(WIDE, second, 0)
    end()


def grads_and_rows(
    ready, cont, cum, recv, hc, hr, dout, n16, u, dg16, dm16, cs, ylf, ylr, rows, dc, grads,
    *scratch
):
    n_t, u_t, dwo, dwg, bcv, yfv, yrv, sf, sr, doutv, nv, uv, dgv, dmv = scratch[:14]
    lsem, sem, osem = scratch[14:]
    loads = [(dout, doutv), (n16, nv), (u, uv), (dg16, dgv), (cs.at[:, E:], bcv)]
    loads = [pltpu.make_async_copy(a, b, lsem.at[k]) for k, (a, b) in enumerate(loads)]
    for copy in loads:
        copy.start()
    finish_all(loads[:2])
    wait = fetch([(ylf, yfv), (ylr, yrv), (dm16, dmv)], sem)
    n_t[...] = flip(nv[...])

    def columns_out(i, _):
        at = wide(i)
        dwo[:, at] = mm(n_t[...], doutv[:, at]).astype(BF)
        return 0

    def columns_gate(i, _):
        at = wide(i)
        dwg[:, at] = mm(u_t[...], dgv[:, at]).astype(BF)
        return 0

    each(D // 256, columns_out, 0)
    finish_all(loads[2:4])
    u_t[...] = flip(uv[HALO:, :])
    each(WIDE, columns_gate, 0)
    shards = grads.reshape(DP, 384, D)
    gate_rows = dwg.reshape(DP, 96, E)
    outward = [
        (gate_rows.at[:, :, pl.ds(0, D)], shards.at[:, pl.ds(0, 96)]),
        (gate_rows.at[:, :, pl.ds(D, D)], shards.at[:, pl.ds(96, 96)]),
        (dwo.reshape(DP, 192, D), shards.at[:, pl.ds(192, 192)]),
    ]
    outward = [pltpu.make_async_copy(a, b, osem.at[k]) for k, (a, b) in enumerate(outward)]
    for copy in outward:
        copy.start()
    ready()
    take_slices(recv, sf, sr, cont[0:1, 0:1])
    ef_f, ef_r = pairs_of(jnp.exp(cum[...]))
    finish_all(loads[4:])
    _, cf, _, cr = parts_of_bc(silu(bcv[...]))

    def tile(i, sums):
        at = wide(i)
        wait(i)
        dm = dmv[:, at].astype(F32)
        new, halves = [], []
        efs = mm_rows([ef_f, ef_r], hc[:, at])
        for ef, c, s, yl in ((efs[0], cf, sf, yfv), (efs[1], cr, sr, yrv)):
            y = yl[:, at] + ef * mm(c, s[:, at])
            halves += split2(dm * y)
            new.append(mm_nt((ef * dm).astype(BF), s[:, at]))
        a, b, c, d = mm_rows(halves, hr[at, :])
        return sums[0] + a + b, sums[1] + new[0], sums[2] + c + d, sums[3] + new[1]

    zero, zn = jnp.zeros((T, 128), F32), jnp.zeros((T, N), F32)
    rf, dcf, rr, dcr = each(WIDE, tile, (zero, zn, zero, zn))
    rows[...] = rf + to_back(rr)
    dc[...] = jnp.concatenate([dcf, dcr], axis=1)
    finish_all(outward)


def project_out(ready, tok, n16, rest, out, wo, sem):
    finish_all(load_rest(rest, None, wo, sem)[1])
    ready()
    out[...] = (tok[...].astype(F32) + mm(n16[...], wo[...])).astype(BF)


def local_back(ready, dt, cum, dm16, hc, hr, cs, zf, zr, dgf, dgr, inner, *scratch):
    csv, zfv, zrv, col, row, gf, gr, dm_t, sem, osem = scratch
    bc = pltpu.make_async_copy(cs.at[:, E:], csv.at[:, E:], sem.at[0, 2])
    bc.start()
    wait = fetch([(cs, csv)], sem)
    ready()
    cum2 = cum[...] * LOG2E
    row[...] = cum2.T
    columns_of(cum2, col)
    dm_t[...] = flip(dm16[...])
    dt_f, dt_r = pairs_of(dt[...])
    bc.wait()
    bf, cf, br, cr = parts_of_bc(silu(csv[:, E:]))
    s, t = iota((T, T), 0), iota((T, T), 1)
    gf[...] = jnp.where(t > s, mm_nt(bf, cf), 0.0)
    gr[...] = jnp.where(t < s, mm_nt(br, cr), 0.0)
    dgf[...] = jnp.zeros((T, T), F32)
    dgr[...] = jnp.zeros((T, T), F32)

    done, end = deliver([(zfv, zf), (zrv, zr)], osem)

    def tile(i, sums):
        at = wide(i)
        wait(i)
        x = silu(csv[:, at])
        xd = [x * spread for spread in mm_rows([dt_f, dt_r], hc[:, at])]
        dws = mm_rows(by_head(xd[0]) + by_head(xd[1]), dm_t[at, :])
        all_w = []
        for forward, first, g, dg in ((True, 0, gf, dgf), (False, H, gr, dgr)):
            ws = []
            small = jnp.zeros((128, 128), F32)
            large = jnp.zeros((T, 128), F32)
            for e in range(4):
                h = first + 4 * i + e
                at_s, along = col[h], row[h : h + 1, :]
                dw = dws[e if forward else 4 + e]
                if forward:
                    ea = jnp.exp2(jnp.minimum(along[:, :128] - at_s[:128], 0.0))
                    eb = jnp.exp2(jnp.minimum(along[:, 128:] - at_s, 0.0))
                    ws.append(
                        up_full((ea * g[:128, :128]).astype(BF), (eb * g[:, 128:]).astype(BF))
                    )
                    small = small + ea * dw[:128, :128]
                    large = large + eb * dw[:, 128:]
                else:
                    ea = jnp.exp2(jnp.minimum(along[:, :128] - at_s, 0.0))
                    eb = jnp.exp2(jnp.minimum(along[:, 128:] - at_s[128:], 0.0))
                    ws.append(
                        low_full((ea * g[:, :128]).astype(BF), (eb * g[128:, 128:]).astype(BF))
                    )
                    large = large + ea * dw[:, :128]
                    small = small + eb * dw[128:, 128:]
            all_w.append(jnp.concatenate(ws, axis=1))
            if forward:
                dg[:128, :128] += small
                dg[:, 128:] += large
            else:
                dg[:, :128] += large
                dg[128:, 128:] += small
        totals = mm_rows(all_w, jnp.concatenate(by_head(dm16[:, at].astype(F32)), axis=0))
        zfv[:, at], zrv[:, at] = totals[0].astype(BF), totals[1].astype(BF)
        halves = [t for k in range(2) for t in split2(xd[k].astype(BF).astype(F32) * totals[k])]
        done(i)
        a, b, c, d = mm_rows(halves, hr[at, :])
        return sums[0] + a + b, sums[1] + c + d

    zero = jnp.zeros((T, 128), F32)
    sums = each(WIDE, tile, (zero, zero))
    inner[...] = sums[0] + to_back(sums[1])
    dgf[...] = jnp.where(t > s, dgf[...], 0.0)
    dgr[...] = jnp.where(t < s, dgr[...], 0.0)
    end()


def inner_back(
    ready, cont, halo, gin, cw, alog, dsk, sraw, dt, cum, back, fore, rows, inner, dc, dgout, hc, hr,
    dgf, dgr, tok, dout, cs, zf, zr, dm16, ci, dg16, rest, *refs
):
    parts, (dtok, dhalo, dall_out, small_out), scratch = refs[:8], refs[8:12], refs[12:]
    csv, zfv, zrv, dmv, civ, dgv, w, wg, sf, sr, kf, kr, dcs, cif, du, small = scratch[:16]
    line, dall, gfv, grv, tokv, doutv, sem, csem, wsem, gsem, osem = scratch[16:]
    first = [(cs.at[:, E:], csv.at[:, E:])]
    bcc = pltpu.make_async_copy(*first[0], csem.at[0])
    bcc.start()
    wait = fetch([(cs, csv), (zf, zfv), (zr, zrv), (dm16, dmv)], sem)
    later = [(dgf, gfv), (dgr, grv), (ci, civ), (dg16, dgv), (tok, tokv), (dout, doutv)]
    later = [pltpu.make_async_copy(a, b, csem.at[1 + k]) for k, (a, b) in enumerate(later)]
    ready()
    keep = cont[0:1, 0:1]
    take_slices(back, kr, kf, keep)
    take_slices(fore, sf, sr, keep)
    cumv, dtv = cum[...], dt[...]
    last = ends(cumv)
    te_f, te_r = pairs_of(jnp.exp(last - cumv))
    dt_f, dt_r = pairs_of(dtv)
    line[...] = jnp.zeros((8, E), F32)
    dcs[:, 0:HALO] = jnp.zeros((C // 128, HALO, 128), F32)
    dcs[:, HALO + T :] = jnp.zeros((C // 128, 16, 128), F32)
    bcc.wait()
    bc = csv[:, E:]
    bf, cf, br, cr = parts_of_bc(silu(bc))

    def weights():
        gates = load_rest(rest, wg, None, gsem, False)[0]
        return load_weights(parts, w, wsem, False) + gates

    def slope(v, sg):
        return sg * (1.0 + v * (1.0 - sg))

    def tile(i, sums):
        at = wide(i)

        if i in (1, 3):
            for copy in later if i == 1 else weights():
                copy.start()

        wait(i)
        v = csv[:, at]
        sg = sigmoid(v)
        x = v * sg
        dm = dmv[:, at].astype(F32)
        line[2:3, at] = jnp.sum(dm * x, axis=0, keepdims=True)
        dx = dsk[:, at] * dm
        new, ends_of = [], []
        for d, dt2, te2, z, k, s, b in (
            (0, dt_f, te_f, zfv, kf, sf, bf),
            (1, dt_r, te_r, zrv, kr, sr, br),
        ):
            dts, te = mm(dt2, hc[:, at]), mm(te2, hc[:, at])
            xd = (x * dts).astype(BF).astype(F32)
            zt = te * mm(b, k[:, at])
            dx = dx + dts * (z[:, at].astype(F32) + zt)
            ends_of.append((xd * zt).astype(BF))
            new.append(mm_nt((te * xd).astype(BF), k[:, at]))
            both = s[:, at].astype(F32) * k[:, at].astype(F32)
            line[d : d + 1, at] = jnp.sum(both, axis=0, keepdims=True)
        dx = dx * slope(v, sg)
        for e in range(2):
            dcs[2 * i + e, HALO : HALO + T] = dx[:, 128 * e : 128 * e + 128]
        tf, tr = mm_rows(ends_of, hr[at, :])
        return sums[0] + tf, sums[1] + new[0], sums[2] + tr, sums[3] + new[1]

    zero, zn = jnp.zeros((T, 128), F32), jnp.zeros((T, N), F32)
    sums = each(WIDE, tile, (zero, zn, zero, zn))
    tails = sums[0] + to_back(sums[2])
    finish_all(later)
    gf16, gr16 = gfv[...].astype(BF), grv[...].astype(BF)
    dbf = sums[1] + mm(gf16, cf)
    dbr = sums[3] + mm(gr16, cr)
    dcf = dc[:, :N] + mm(flip(gf16), bf)
    dcr = dc[:, N:] + mm(flip(gr16), br)
    dbc = jnp.concatenate([dbf, dcf, dbr, dcr], axis=1) * slope(bc, sigmoid(bc))
    for e in range(2):
        dcs[2 * WIDE + e, HALO : HALO + T] = dbc[:, 128 * e : 128 * e + 128]
    hi, lo = split2(line[...])
    heads = mm(hi, hr[...]) + mm(lo, hr[...])
    dots = heads[0:1] + to_back(heads)[1:2]
    rate = jnp.where(lanes(1) < 2 * H, jnp.exp(alog[...]), 0.0)
    v = rows[...] - inner[...]
    dla = jnp.where(
        lanes() < H,
        tri_sum(tri(lambda r, c: r <= c), v) + tri_sum(tri(lambda r, c: r > c), tails),
        tri_sum(tri(lambda r, c: r >= c), v) + tri_sum(tri(lambda r, c: r < c), tails),
    ) + jnp.exp(last) * dots
    sg = sigmoid(sraw[...])
    ratio = jnp.where(dtv > 1e-20, sg / jnp.maximum(dtv, 1e-20), 1.0)
    dstep = (inner[...] + tails) * ratio - dla * rate * sg
    dstep = jnp.where(lanes() < 2 * H, dstep, 0.0)
    dall[0:HALO, C:] = jnp.zeros((HALO, 128), BF)
    dall[HALO:, C:] = dstep.astype(BF)
    dal = jnp.broadcast_to(jnp.sum(dla * (-dtv * rate), axis=0, keepdims=True), (8, 128))
    small[...] = jnp.zeros((96, 128), F32)
    small[88:89] = jnp.sum(dstep, axis=0, keepdims=True)
    small[89:90] = jnp.where(lanes(1) < H, dal[0:1] + to_front(dal)[0:1], 0.0)
    small[90:91] = jnp.where(lanes(1) < H, heads[2:3], 0.0)
    mask = jnp.where(iota((HALO + T, 1), 0) < HALO, keep, 1.0)

    half_out = [
        pltpu.make_async_copy(dall.at[:, at], dall_out.at[:, at], osem.at[k])
        for k, at in enumerate((pl.ds(0, 1024), pl.ds(1024, CD - 1024)))
    ]

    def convolution(i, _):
        at = pl.ds(128 * i, 128)
        g = dcs[i, HALO : HALO + T]
        cif[...] = civ[:, at].astype(F32)
        small[56 + i : 57 + i] = jnp.sum(g, axis=0, keepdims=True)
        total = jnp.zeros((HALO + T, 128), F32)
        for k in range(4):
            shifted = cif[HALO - 3 + k : HALO - 3 + k + T]
            small[14 * k + i : 14 * k + i + 1] = jnp.sum(g * shifted, axis=0, keepdims=True)
            total = total + cw[k : k + 1, at] * dcs[i, 3 - k : 3 - k + HALO + T]
        dall[:, at] = (total * mask).astype(BF)
        if i == 7:
            half_out[0].start()
        return 0

    each(C // 128, convolution, 0)
    half_out[1].start()
    for j in range(E // 128):
        small[70 + j : 71 + j] = dgout[:, 128 * j : 128 * j + 128]
    finish_all(weights())

    def input_grad(i, _):
        at = wide(i)
        du[:, at] = mm_nt(dall[...], w[at, :])
        du[HALO:, at] += mm_nt(dgv[:, :D], wg[0, at, :]) + mm_nt(dgv[:, D:], wg[1, at, :])
        return 0

    each(D // 256, input_grad, 0)
    x = jnp.concatenate([halo[...], tokv[...]], axis=0).astype(F32)
    r = lax.rsqrt(jnp.mean(x * x, axis=1, keepdims=True) + EPS)
    duxr = jnp.sum(du[...] * x * r, axis=0, keepdims=True)
    for j in range(6):
        small[82 + j : 83 + j] = duxr[:, 128 * j : 128 * j + 128]
    small_out[...] = small[...].astype(BF)
    dxh = du[...] * gin[...]
    dx = r * dxh - x * (r * r * r * jnp.mean(dxh * x, axis=1, keepdims=True))
    dhalo[...] = dx[:HALO]
    dtok[...] = doutv[...].astype(F32) + dx[HALO:]
    finish_all(half_out)


def weight_back(to_other, u, dall, small, out, u_t):
    y, core, _ = place()
    u_t[...] = flip(u[...])
    core = 1 - core if to_other else core
    shards = [2 * lax.rem(y + k, 4) + core for k in range(4)]
    rows = [u_t[pl.ds(pl.multiple_of(shard * 96, 32), 96), :] for shard in shards]
    parts = mm_rows(rows, dall[...])
    for k in range(4):
        out[k, :, :CD] = parts[k].astype(BF)
        out[k, :, CD:] = small[...]


def add_pairs(a, b, whole, one, three, mine, other):
    for k, out in ((0, whole), (1, one), (3, three)):

        def rows(i, _, k=k, out=out):
            at = pl.ds(pl.multiple_of(i * 48, 16), 48)
            out[at] = (a[k, at].astype(F32) + b[k, at].astype(F32)).astype(BF)
            return 0

        lax.fori_loop(0, 2, rows, 0)
    _, _, parity = place()
    for out, half in ((mine, parity), (other, 1 - parity)):
        at = pl.ds(pl.multiple_of(half * 1024, 1024), 1024)
        out[...] = (a[2, :, at].astype(F32) + b[2, :, at].astype(F32)).astype(BF)


def add_two(a, b, out):
    out[...] = (a[...].astype(F32) + b[...].astype(F32)).astype(BF)


def add_y(rest, whole, one, three, half, out):
    _, _, parity = place()
    for j in range(6):
        for r in range(0, 384, 48):
            row = 384 * j + r
            out[row // 144, row % 144 : row % 144 + 48] = rest[
                r : r + 48, 128 * j : 128 * j + 128
            ]
    for j in range(SEQ):
        at, in_half = slice(128 * j, 128 * j + 128), slice(128 * (j % 8), 128 * (j % 8) + 128)
        mine = jnp.where(parity == j // 8, 1.0, 0.0)
        total = sum(part[:, at].astype(F32) for part in (whole, one, three))
        out[j, 144:] = (total + half[:, in_half].astype(F32) * mine).astype(BF)


def add_blocks(recv, out):
    total = recv[0].astype(F32)
    for i in range(1, SEQ):
        total = total + recv[i].astype(F32)
    low = total.astype(BF)
    for i in range(SEQ):
        out[i] = low


def finish(sums, dwin, dwdt, dwout, dcw, dcb, dgout, dgin, ddtb, dal, ddsk):
    def put(ref, at, start, rows):
        for r in range(0, rows, 48):
            j, k = (start + r) // 144, (start + r) % 144
            ref[r : r + 48, at] = sums[j, k : k + 48].astype(F32)

    for j in range(6):
        at = slice(128 * j, 128 * j + 128)
        put(dwin, at, 384 * j, 96)
        put(dwin, slice(D + 128 * j, D + 128 * j + 128), 384 * j + 96, 96)
        put(dwout, at, 384 * j + 192, 192)
    for j in range(14):
        dwin[:, E + 128 * j : E + 128 * j + 128] = sums[j, 144:].astype(F32)
    dwdt[...] = sums[14, 144:].astype(F32).T[: 2 * H]
    small = sums[15, 144:].astype(F32)
    for j in range(14):
        at = slice(128 * j, 128 * j + 128)
        for k in range(4):
            dcw[k : k + 1, at] = small[14 * k + j : 14 * k + j + 1]
        dcb[at] = small[56 + j]
    for j in range(E // 128):
        dgout[128 * j : 128 * j + 128] = small[70 + j]
    for j in range(6):
        dgin[128 * j : 128 * j + 128] = small[82 + j]
    ddtb[...] = small[88, 0 : 2 * H]
    dal[...] = small[89, 0:H]
    ddsk[...] = small[90, 0:H]


V = pl.BlockSpec(memory_space=pltpu.VMEM)
ANY = pl.BlockSpec(memory_space=pl.ANY)


def shape(*dims, dtype=F32):
    return jax.ShapeDtypeStruct(dims, dtype)


def nothing():
    pass


def staged(kernel, ins, outs, scratch):
    held = [i for i, (spec, _) in enumerate(ins) if spec is V]
    more = [pltpu.VMEM(ins[i][1].shape, ins[i][1].dtype) for i in held]
    more.append(pltpu.SemaphoreType.DMA((len(held),)))

    def run(*refs):
        refs = list(refs)
        buffers, sem = refs[len(refs) - len(more) : -1], refs[-1]
        copies = []
        for k, i in enumerate(held):
            copies.append(pltpu.make_async_copy(refs[i], buffers[k], sem.at[k]))
            copies[-1].start()
            refs[i] = buffers[k]
        kernel(lambda: finish_all(copies), *refs[: len(refs) - len(more)])

    return run, [(ANY, a) for _, a in ins], list(scratch) + more


def call(kernel, name, ins, outs, scratch=(), flops=0, apart=(), limit=VMEM, stage=False):
    if stage:
        kernel, ins, scratch = staged(kernel, ins, outs, scratch)
    specs, args = zip(*ins)
    moved = sum(a.size * a.dtype.itemsize for a in args)
    moved += sum(o.size * o.dtype.itemsize for o in outs)
    return pl.pallas_call(
        kernel,
        name=name,
        out_shape=tuple(outs),
        in_specs=list(specs),
        out_specs=tuple(ANY if i in apart else V for i in range(len(outs))),
        scratch_shapes=list(scratch),
        cost_estimate=pl.CostEstimate(flops=flops, bytes_accessed=moved, transcendentals=0),
        compiler_params=pltpu.CompilerParams(vmem_limit_bytes=limit),
    )(*args)


def vm(*dims, dtype=F32):
    return pltpu.VMEM(dims, dtype)


def shift_y(k):
    return [(2 * y + c, 2 * ((y + k) % 4) + c) for y in range(4) for c in range(2)]


SWAP = [(i, i ^ 1) for i in range(DP)]
NEXT_Z = [(i, i ^ 1) for i in range(SEQ)]


def exchange(value):
    return lax.all_to_all(value, "seq", 0, 0, tiled=True)


def together(*values):
    return lax.optimization_barrier(values)


def local(
    tokens, starts, g_in, w_in, w_dt, conv_w, conv_b, dt_bias, a_log, dskip, g_out, w_out, d_out
):
    tok, dout = tokens[0], d_out[0]
    cont = jnp.broadcast_to((1 - starts).astype(F32), (1, 128))

    row = lambda v: v.reshape(1, -1)
    pad = lambda v: jnp.pad(v, (0, 128 - v.shape[0])).reshape(1, 128)
    alog = pad(jnp.concatenate([a_log, a_log]))
    dsk = row(jnp.repeat(dskip, N))
    gin, gout, cb, dtb = row(g_in), row(g_out), row(conv_b), pad(dt_bias)
    own = jnp.concatenate([w_in[:, E:], jnp.pad(w_dt, ((0, 0), (0, 128 - 2 * H)))], axis=1)
    column = [lax.ppermute(own, "dp", shift_y(k)) for k in (1, 2, 3)]
    halo = lax.ppermute(tok[-HALO:], "seq", [(i, i + 1) for i in range(SEQ - 1)])
    beside = lax.ppermute(own, "dp", SWAP)
    rest_own = jnp.concatenate([w_in[:, :D], w_in[:, D:E], w_out], axis=0)
    hc, hr = marks()
    column[0], halo, beside, alog, dsk, gin, gout, cb, dtb, cont, hc, hr = together(
        column[0], halo, beside, alog, dsk, gin, gout, cb, dtb, cont, hc, hr
    )
    parts = [own, *column, beside] + [lax.ppermute(part, "dp", SWAP) for part in column]
    rest_own = together(rest_own, *column)[0]
    rest = lax.all_gather(rest_own, "dp", axis=0, tiled=True)

    part_ins = [(ANY, part) for part in parts]
    w_scratch = vm(D, CD, dtype=BF)
    dma = pltpu.SemaphoreType.DMA
    full, half, state = vm(T, E), vm(T, E, dtype=BF), vm(N, E, dtype=BF)

    u, ci, cs, sraw, dt, cum, pay = call(
        front,
        "front",
        [(V, cont), (V, tok), (V, halo), (V, gin), (V, conv_w), (V, cb)]
        + [(V, dtb), (V, alog), (V, hc)]
        + part_ins,
        [shape(HALO + T, D, dtype=BF), shape(HALO + T, C, dtype=BF), shape(T, C)]
        + [shape(T, 128)] * 3
        + [shape(SEQ, 48, 384, dtype=BF)],
        [w_scratch, vm(2, HALO + T, 128), vm(T, C), vm(HALO + T, C, dtype=BF)]
        + [vm(HALO + T, D, dtype=BF), dma((8,)), dma((2, 3)), dma(())],
        flops=2 * T * D * CD,
        apart=(0, 1, 2),
        stage=True,
    )

    def scan(got, name):
        out = shape(SEQ, 32, 384, dtype=BF)
        return call(scan_blocks, name, [(V, got)], [out], limit=SMALL)[0]

    got = exchange(pay)
    ylf, ylr, base = call(
        local_mix,
        "local_mix",
        [(V, dt), (V, cum), (V, dsk), (V, hc), (ANY, cs)],
        [shape(T, E)] * 3,
        [vm(T, C), full, full, full, vm(2 * H, T, 128), vm(128, T), vm(T, T), vm(T, T)]
        + [dma(()), dma((1, 2)), dma((3, 2))],
        flops=4 * 24 * T * T * 256,
        apart=(0, 1, 2),
    )
    got, ylr, base = together(got, ylr, base)
    fore = exchange(scan(got, "scan_states"))
    gate, dn = call(
        gate_products,
        "gate_products",
        [(V, u), (V, dout), (ANY, rest)],
        [shape(T, E, dtype=BF)] * 2,
        [vm(2, D, D, dtype=BF), vm(E, D, dtype=BF), half, half, dma((3,)), dma((4,))],
        flops=4 * T * D * E,
        apart=(0, 1),
    )
    n16, dg16, dm16, dgout, pay_back = call(
        gated_norm,
        "gated_norm",
        [(V, cont), (V, cum), (V, fore), (V, gout), (V, hc)]
        + [(ANY, a) for a in (cs, base, gate, dn)],
        [shape(T, E, dtype=BF)] * 3 + [shape(1, E), shape(SEQ, 48, 384, dtype=BF)],
        [vm(T, 256), full, half, half] + [full] * 4 + [vm(2, 16, E)] + [half] * 3 + [state] * 2
        + [dma(()), dma((3, 2)), dma((3, 2))],
        flops=12 * T * N * E,
        apart=(0, 1, 2),
        stage=True,
    )
    got = exchange(pay_back)
    rows, dc, rest_grads = call(
        grads_and_rows,
        "grads_and_rows",
        [(V, cont)]
        + [(V, a) for a in (cum, fore, hc, hr)]
        + [(ANY, a) for a in (dout, n16, u, dg16, dm16, cs, ylf, ylr)],
        [shape(T, 128), shape(T, 128), shape(DP * 384, D, dtype=BF)],
        [vm(E, T, dtype=BF), vm(D, T, dtype=BF), vm(E, D, dtype=BF), vm(D, E, dtype=BF)]
        + [vm(T, 256), full, full, state, state, vm(T, D, dtype=BF), half]
        + [vm(HALO + T, D, dtype=BF), half, half]
        + [dma((5,)), dma((3, 2)), dma((3,))],
        flops=8 * T * D * E,
        apart=(2,),
        stage=True,
    )
    got, rows, rest_grads = together(got, rows, rest_grads)
    rest_sum = lax.psum_scatter(rest_grads, "dp", scatter_dimension=0, tiled=True)
    back = exchange(scan(got, "scan_adjoints"))
    zf, zr, dgf, dgr, inner = call(
        partial(local_back, nothing),
        "local_back",
        [(V, dt), (V, cum), (V, dm16), (V, hc), (V, hr), (ANY, cs)],
        [shape(T, E, dtype=BF)] * 2 + [shape(T, T)] * 2 + [shape(T, 128)],
        [vm(T, C), half, half, vm(2 * H, T, 128), vm(128, T), vm(T, T), vm(T, T)]
        + [vm(E, T, dtype=BF), dma((1, 3)), dma((2, 2))],
        flops=4 * 48 * T * T * 256,
        apart=(0, 1),
    )
    dtok, dhalo, dall, small = call(
        partial(inner_back, nothing),
        "inner_back",
        [(V, cont)]
        + [(V, a) for a in (halo, gin, conv_w, alog, dsk, sraw, dt, cum, back, fore, rows)]
        + [(V, a) for a in (inner, dc, dgout, hc, hr)]
        + [(ANY, a) for a in (dgf, dgr, tok, dout, cs, zf, zr, dm16, ci, dg16, rest)]
        + part_ins,
        [shape(T, D), shape(HALO, D), shape(HALO + T, CD, dtype=BF), shape(96, 128, dtype=BF)],
        [vm(T, C), half, half, half, vm(HALO + T, C, dtype=BF), half, w_scratch]
        + [vm(2, D, D, dtype=BF)]
        + [state] * 4
        + [vm(C // 128, HALO + T + 16, 128), vm(HALO + T, 128), vm(HALO + T, D), vm(96, 128)]
        + [vm(8, E), vm(HALO + T, CD, dtype=BF), vm(T, T), vm(T, T)]
        + [vm(T, D, dtype=BF), vm(T, D, dtype=BF)]
        + [dma((4, 2)), dma((7,)), dma((8,)), dma((3,)), dma((2,))],
        flops=2 * T * D * (CD + E),
        apart=(2,),
    )
    def grads_for(to_other, name):
        return call(
            partial(weight_back, to_other),
            name,
            [(V, u), (V, dall), (V, small)],
            [shape(4, 96, 2048, dtype=BF)],
            [vm(D, HALO + T, dtype=BF)],
            flops=T * D * CD,
            limit=16 * 1024 * 1024,
        )[0]

    send = grads_for(True, "grads_to_other_core")
    send, u, dall, small = together(send, u, dall, small)
    recv = lax.ppermute(send, "dp", SWAP)
    keep = grads_for(False, "grads_to_this_core")
    whole, one, three, mine, other = call(
        add_pairs,
        "add_tail_cores",
        [(V, keep), (V, recv)],
        [shape(96, 2048, dtype=BF)] * 3 + [shape(96, 1024, dtype=BF)] * 2,
        limit=SMALL,
    )
    other = lax.ppermute(other, "seq", NEXT_Z)
    one, three = lax.ppermute(one, "dp", shift_y(1)), lax.ppermute(three, "dp", shift_y(3))
    sides = [(V, mine), (V, other)]
    half = call(add_two, "add_tail_z", sides, [shape(96, 1024, dtype=BF)], limit=SMALL)[0]
    half, n16, dhalo = together(half, n16, dhalo)
    half = lax.ppermute(half, "dp", shift_y(2))
    dback = lax.ppermute(dhalo, "seq", [(i + 1, i) for i in range(SEQ - 1)])
    out = call(
        project_out,
        "project_out",
        [(V, tok), (V, n16), (ANY, rest)],
        [shape(T, D, dtype=BF)],
        [vm(E, D, dtype=BF), dma((3,))],
        flops=2 * T * D * E,
        stage=True,
    )[0]
    dtok = dtok.at[-HALO:].add(dback)
    one, three, half, out, dtok = together(one, three, half, out, dtok)
    slices = shape(SEQ, 240, 128, dtype=BF)
    sums = [(V, part) for part in (rest_sum, whole, one, three, half)]
    sums = call(add_y, "add_y", sums, [slices], limit=SMALL)[0]
    sums = call(add_blocks, "add_seq", [(V, exchange(sums))], [slices], limit=SMALL)[0]
    dwin, dwdt, dwout, dcw, dcb, dgo, dgi, ddtb, dal, dds = call(
        finish,
        "finish",
        [(V, exchange(sums))],
        [shape(96, E + C), shape(2 * H, 96), shape(192, D), shape(4, C), shape(C)]
        + [shape(E), shape(D), shape(2 * H), shape(H), shape(H)],
        limit=SMALL,
    )
    return (
        out[None], dtok[None], dgi, dwin, dwdt.T, dcw, dcb, ddtb, dal, dds, dgo, dwout,
    )


def solution(mesh):
    split = P("dp", "seq", None)
    rows = P("dp", None)
    return jax.shard_map(
        local,
        mesh=mesh,
        in_specs=(split, P("dp", "seq"), P(), rows, rows, P(), P(), P(), P(), P(), P(), rows, split),
        out_specs=(split, split, P(), rows, rows, P(), P(), P(), P(), P(), P(), rows),
        check_vma=False,
    )
```

```python
from functools import partial

import jax
import jax.numpy as jnp
from jax import lax
from jax.experimental import pallas as pl
from jax.experimental.pallas import tpu as pltpu
from jax.sharding import PartitionSpec as P

F32, BF = jnp.float32, jnp.bfloat16
EPS = 1e-05
LOG2E = 1.4426950408889634
D, H, E, N, T = 768, 24, 1536, 64, 256
C = E + 4 * N
CD = C + 128
HALO = 16
WIDE = E // 256
DP, SEQ = 8, 16
VMEM = 56 * 1024 * 1024
SMALL = 12 * 1024 * 1024


def iota(shape, dim):
    return lax.broadcasted_iota(jnp.int32, shape, dim)


def mm(a, b):
    return jnp.dot(a, b, preferred_element_type=F32)


def mm_nt(a, b):
    return lax.dot_general(a, b, (((1,), (1,)), ((), ())), preferred_element_type=F32)


def mm_rows(parts, right):
    total = mm(jnp.concatenate(parts, axis=0), right)
    ends = [sum(p.shape[0] for p in parts[: k + 1]) for k in range(len(parts))]
    return [total[end - p.shape[0] : end] for end, p in zip(ends, parts)]


def flip(v):
    return v.astype(F32).T.astype(v.dtype)


def sigmoid(v):
    return 1.0 / (1.0 + jnp.exp(-v))


def silu(v):
    return v * sigmoid(v)


def split2(v):
    hi = v.astype(BF)
    return hi, (v - hi.astype(F32)).astype(BF)


def onehot(cond):
    return jnp.where(cond, 1.0, 0.0).astype(BF)


def marks():
    row, head = iota((64, E), 0), iota((64, E), 1) >> 6
    columns = onehot((row == head) | (row == head + H))
    return columns, onehot((iota((E, 128), 0) >> 6) == iota((E, 128), 1))


def to_front(v):
    return pltpu.roll(v, 128 - H, 1)


def to_back(v):
    return pltpu.roll(v, H, 1)


def pairs_of(v):
    def terms(v):
        hi = v.astype(BF).astype(F32)
        lane = lanes(v.shape[0])
        both = jnp.where(lane < H, hi, jnp.where(lane < 2 * H, to_back(v - hi), 0.0))
        return both[:, :64].astype(BF)

    return terms(v), terms(to_front(v))


def tri_sum(mask, v):
    hi = v.astype(BF)
    rest = v - hi.astype(F32)
    mid = rest.astype(BF)
    low = (rest - mid.astype(F32)).astype(BF)
    return mm(mask, hi) + mm(mask, mid) + mm(mask, low)


def tri(cond):
    return onehot(cond(iota((T, T), 0), iota((T, T), 1)))


def lanes(rows=T):
    return iota((rows, 128), 1)


def wide(i):
    return pl.ds(256 * i, 256)


def each(count, body, carry):
    for i in range(count):
        carry = body(i, carry)
    return carry


def fetch(sources, sems):
    def copies(k):
        at = (pl.ds(0, 256), pl.ds(256, E - 256))[k]
        return [
            pltpu.make_async_copy(src.at[:, at], dst.at[:, at], sems.at[n, k])
            for n, (src, dst) in enumerate(sources)
        ]

    for k in range(2):
        for copy in copies(k):
            copy.start()

    def wait(i):
        if i < 2:
            finish_all(copies(i))

    return wait


def deliver(targets, sems, tiles=WIDE):
    def copies(k):
        at = (pl.ds(0, 256 * (tiles - 1)), pl.ds(256 * (tiles - 1), 256))[k]
        return [
            pltpu.make_async_copy(src.at[:, at], dst.at[:, at], sems.at[n, k])
            for n, (src, dst) in enumerate(targets)
        ]

    def done(i):
        if i == tiles - 2:
            for copy in copies(0):
                copy.start()

    def end():
        for copy in copies(1):
            copy.start()
        finish_all(copies(0))
        finish_all(copies(1))

    return done, end


def parts_of_bc(act):
    return [act[:, N * k : N * k + N].astype(BF) for k in range(4)]


def ends(cum):
    return jnp.where(lanes(1) < H, cum[T - 1 : T], cum[0:1])


def put_slices(pay, i, first, second, dec_first, dec_second):
    row = iota((16, 128), 0)
    for e in range(2):
        at = slice(128 * e, 128 * e + 128)
        tile = 2 * i + e
        group, into = tile // 3, pl.ds(tile % 3 * 128, 128)
        a, b = dec_first[:, at], dec_second[:, at]
        ah, bh = a.astype(BF).astype(F32), b.astype(BF).astype(F32)
        dec = jnp.where(
            row == 0, ah, jnp.where(row == 1, a - ah, jnp.where(row == 2, bh, b - bh))
        )
        dec = jnp.where(row < 4, dec, 0.0).astype(BF)
        for q in range(4):
            j = 4 * group + q
            pay[j, 0:16, into] = first[16 * q : 16 * q + 16, at].astype(BF)
            pay[j, 16:32, into] = second[16 * q : 16 * q + 16, at].astype(BF)
            pay[j, 32:48, into] = dec


def take_slices(recv, first, second, first_scale):
    for j in range(SEQ):
        rows, at = pl.ds(16 * (j % 4), 16), pl.ds(384 * (j // 4), 384)
        first[rows, at] = (recv[j, 0:16].astype(F32) * first_scale).astype(BF)
        second[rows, at] = recv[j, 16:32]


def place():
    dp, seq = lax.axis_index("dp"), lax.axis_index("seq")
    return lax.div(dp, 2), lax.rem(dp, 2), lax.rem(seq, 2)


def load_weights(parts, w, sem, start=True):
    y, core, _ = place()
    copies = []
    for k in range(8):
        shard = 2 * lax.rem(y + 4 - k % 4, 4) + (core if k < 4 else 1 - core)
        at = pl.ds(pl.multiple_of(shard * 96, 32), 96)
        copies.append(pltpu.make_async_copy(parts[k], w.at[at], sem.at[k]))
    if start:
        for copy in copies:
            copy.start()
    return copies


def load_rest(rest, wg, wo, sem, start=True):
    shards = rest.reshape(DP, 384, D)
    gates, outs = [], []
    if wg is not None:
        for h in range(2):
            into = wg.at[h].reshape(DP, 96, D)
            part = shards.at[:, pl.ds(96 * h, 96)]
            gates.append(pltpu.make_async_copy(part, into, sem.at[h]))
    if wo is not None:
        part = shards.at[:, pl.ds(192, 192)]
        outs.append(pltpu.make_async_copy(part, wo.reshape(DP, 192, D), sem.at[2]))
    if start:
        for copy in gates + outs:
            copy.start()
    return gates, outs


def finish_all(copies):
    for copy in copies:
        copy.wait()


def front(ready, cont, tok, halo, gin, cw, cb, dtb, alog, hc, *refs):
    parts, outs, (w, cif, csv, civ, uv, sem, osem, usem) = refs[:8], refs[8:15], refs[15:]
    u_out, ci_out, cs_out, sraw_out, dt_out, cum_out, pay = outs
    copies = load_weights(parts, w, sem)
    ready()
    x = jnp.concatenate([halo[...], tok[...]], axis=0).astype(F32)
    u = x * lax.rsqrt(jnp.mean(x * x, axis=1, keepdims=True) + EPS) * gin[...]
    uv[...] = u.astype(BF)
    u_copy = pltpu.make_async_copy(uv, u_out, usem)
    u_copy.start()
    keep = cont[0:1, 0:1]
    mask = jnp.where(iota((HALO + T, 1), 0) < HALO, keep, 1.0)
    finish_all(copies)
    sraw = mm(uv[HALO:, :], w[:, C:]) + dtb[...]
    sraw_out[...] = sraw
    dt = jnp.maximum(sraw, 0.0) + jnp.log1p(jnp.exp(-jnp.abs(sraw)))
    dt = jnp.where(lanes() < 2 * H, dt, 0.0)
    dt_out[...] = dt
    rate = jnp.where(lanes(1) < 2 * H, jnp.exp(alog[...]), 0.0)
    la = -dt * rate
    cum = jnp.where(
        lanes() < H,
        tri_sum(tri(lambda r, c: r >= c), la),
        tri_sum(tri(lambda r, c: r <= c), la),
    )
    cum_out[...] = cum
    last = ends(cum)
    tail_f, tail_r = pairs_of(jnp.exp(last - cum) * dt)
    dec_f, dec_r = pairs_of(jnp.broadcast_to(jnp.exp(last) * keep, (16, 128)))

    done, end = deliver([(csv, cs_out), (civ, ci_out)], osem)
    bc_out = [(csv, cs_out), (civ, ci_out)]
    bc_out = [
        pltpu.make_async_copy(a.at[:, E:], b.at[:, E:], osem.at[k, 2])
        for k, (a, b) in enumerate(bc_out)
    ]

    def convolve(i):
        at = wide(i)
        ci = (mm(uv[...], w[:, at]) * mask).astype(BF)
        civ[:, at] = ci
        for e in range(2):
            here = pl.ds(256 * i + 128 * e, 128)
            cif[e] = ci[:, 128 * e : 128 * e + 128].astype(F32)
            total = cb[:, here]
            for k in range(4):
                total = total + cw[k : k + 1, here] * cif[e, HALO - 3 + k : HALO - 3 + k + T]
            csv[:, here] = total
        return silu(csv[:, at])

    bf, _, br, _ = parts_of_bc(convolve(WIDE))
    for copy in bc_out:
        copy.start()
    bf_t, br_t = flip(bf), flip(br)

    def tile(i, _):
        at = wide(i)
        x_act = convolve(i)
        tf, tr, df, dr = mm_rows([tail_f, tail_r, dec_f, dec_r], hc[:, at])
        sf = mm(bf_t, (tf * x_act).astype(BF))
        sr = mm(br_t, (tr * x_act).astype(BF)) * keep
        done(i)
        put_slices(pay, i, sf, sr, df, dr)
        return 0

    each(WIDE, tile, 0)
    end()
    u_copy.wait()
    finish_all(bc_out)


def scan_blocks(recv, out):
    carry = jnp.zeros((16, 384), F32)
    back = jnp.zeros((16, 384), F32)
    for i in range(SEQ):
        k = SEQ - 1 - i
        out[i, 0:16] = carry.astype(BF)
        out[k, 16:32] = back.astype(BF)
        dec = recv[i, 32:48].astype(F32)
        carry = (dec[0:1] + dec[1:2]) * carry + recv[i, 0:16].astype(F32)
        dec = recv[k, 32:48].astype(F32)
        back = (dec[2:3] + dec[3:4]) * back + recv[k, 16:32].astype(F32)


def columns_of(cum2, col, base=0):
    for h in range(col.shape[0]):
        col[h] = jnp.broadcast_to(cum2[:, base + h : base + h + 1], (T, 128))


def by_head(v):
    head = iota((T, 256), 1) >> 6
    return [jnp.where(head == e, v, 0.0).astype(BF) for e in range(4)]


def low_full(left, right):
    right = jnp.concatenate([jnp.zeros((128, 128), right.dtype), right], axis=0)
    return jnp.concatenate([left, right], axis=1)


def up_full(left, right):
    left = jnp.concatenate([left, jnp.zeros((128, 128), left.dtype)], axis=0)
    return jnp.concatenate([left, right], axis=1)


def local_mix(dt, cum, dsk, hc, cs, ylf, ylr, base, *scratch):
    csv, yfv, yrv, bsv, col, row, gf, gr, bsem, sem, osem = scratch
    bc = pltpu.make_async_copy(cs.at[:, E:], csv.at[:, E:], bsem)
    bc.start()
    wait = fetch([(cs, csv)], sem)
    cum2 = cum[...] * LOG2E
    row[...] = cum2.T
    columns_of(cum2, col)
    dt_f, dt_r = pairs_of(dt[...])
    bc.wait()
    bf, cf, br, cr = parts_of_bc(silu(csv[:, E:]))
    r, c = iota((T, T), 0), iota((T, T), 1)
    gf[...] = jnp.where(r > c, mm_nt(cf, bf), 0.0)
    gr[...] = jnp.where(r < c, mm_nt(cr, br), 0.0)

    def weights(h, forward):
        at, along = col[h], row[h : h + 1, :]
        if forward:
            left = jnp.exp2(jnp.minimum(at - along[:, :128], 0.0)) * gf[:, :128]
            right = jnp.exp2(jnp.minimum(at[128:] - along[:, 128:], 0.0)) * gf[128:, 128:]
            return low_full(left.astype(BF), right.astype(BF))
        left = jnp.exp2(jnp.minimum(at[:128] - along[:, :128], 0.0)) * gr[:128, :128]
        right = jnp.exp2(jnp.minimum(at - along[:, 128:], 0.0)) * gr[:, 128:]
        return up_full(left.astype(BF), right.astype(BF))

    done, end = deliver([(yfv, ylf), (yrv, ylr), (bsv, base)], osem)

    def tile(i, _):
        at = wide(i)
        wait(i)
        x = silu(csv[:, at])
        total = dsk[:, at] * x
        dts = mm_rows([dt_f, dt_r], hc[:, at])
        for forward, first, spread, y in ((True, 0, dts[0], yfv), (False, H, dts[1], yrv)):
            xs = by_head(x * spread)
            left = jnp.concatenate([weights(first + 4 * i + e, forward) for e in range(4)], axis=1)
            own = mm(left, jnp.concatenate(xs, axis=0))
            y[:, at] = own
            total = total + own
        bsv[:, at] = total
        done(i)
        return 0

    each(WIDE, tile, 0)
    end()


def gate_products(u, dout, rest, gate, dn, wg, wo, gv, dv, sem, osem):
    gates, outs = load_rest(rest, wg, wo, sem)
    copies = []

    def put(k, value, src, dst, at):
        src[:, at] = value.astype(BF)
        copies.append(pltpu.make_async_copy(src.at[:, at], dst.at[:, at], osem.at[k]))
        copies[-1].start()

    finish_all(gates)
    put(0, mm(u[HALO:, :], wg[0]), gv, gate, slice(0, D))
    put(1, mm(u[HALO:, :], wg[1]), gv, gate, slice(D, E))
    finish_all(outs)
    put(2, mm_nt(dout[...], wo[:D]), dv, dn, slice(0, D))
    put(3, mm_nt(dout[...], wo[D:]), dv, dn, slice(D, E))
    finish_all(copies)


def gated_norm(ready, cont, cum, recv, gout, hc, cs, base, gate, dn, *refs):
    (n16, dg16, dm16, dgout, pay), scratch = refs[:5], refs[5:]
    bcv, yv, gv, dv, gds, sls, eff, efr, decs, nv, dgv, dmv, sf, sr, bsem, sem, osem = scratch
    bc = pltpu.make_async_copy(cs.at[:, E:], bcv, bsem)
    bc.start()
    wait = fetch([(base, yv), (gate, gv), (dn, dv)], sem)
    ready()
    keep = cont[0:1, 0:1]
    take_slices(recv, sf, sr, keep)
    cumv = cum[...]
    ef_f, ef_r = pairs_of(jnp.exp(cumv))
    dec_f, dec_r = pairs_of(jnp.broadcast_to(jnp.exp(ends(cumv)) * keep, (16, 128)))
    bc.wait()
    _, cf, _, cr = parts_of_bc(silu(bcv[...]))
    zero = jnp.zeros((T, 128), F32)

    def first(i, sums):
        at = wide(i)
        wait(i)
        ef, er, decs[0, :, at], decs[1, :, at] = mm_rows([ef_f, ef_r, dec_f, dec_r], hc[:, at])
        eff[:, at] = ef
        efr[:, at] = er
        m = yv[:, at] + ef * mm(cf, sf[:, at]) + er * mm(cr, sr[:, at])
        g = gv[:, at].astype(F32)
        sg = sigmoid(g)
        sl = g * sg
        gd = m * sl
        gds[:, at] = gd
        sls[:, at] = sl
        yv[:, at] = m * sg * (1.0 + g * (1.0 - sg))
        squares, crossed = gd * gd, dv[:, at].astype(F32) * gout[:, at] * gd
        return (
            sums[0] + squares[:, :128] + squares[:, 128:],
            sums[1] + crossed[:, :128] + crossed[:, 128:],
        )

    squares, crossed = each(WIDE, first, (zero, zero))
    rs = lax.rsqrt(jnp.sum(squares, axis=1, keepdims=True) / E + EPS)
    pull = jnp.sum(crossed, axis=1, keepdims=True) / E * (rs * rs * rs)
    cf_t, cr_t = flip(cf), flip(cr)

    done, end = deliver([(nv, n16), (dgv, dg16), (dmv, dm16)], osem)

    def second(i, _):
        at = wide(i)
        gd = gds[:, at]
        gdr = gd * rs
        go = gout[:, at]
        nv[:, at] = (gdr * go).astype(BF)
        d = dv[:, at].astype(F32)
        dgout[:, at] = jnp.sum(d * gdr, axis=0, keepdims=True)
        dgd = rs * (d * go) - gd * pull
        dgv[:, at] = (dgd * yv[:, at]).astype(BF)
        dm = dgd * sls[:, at]
        dmv[:, at] = dm.astype(BF)
        done(i)
        lf = mm(cf_t, (eff[:, at] * dm).astype(BF)) * keep
        lr = mm(cr_t, (efr[:, at] * dm).astype(BF))
        put_slices(pay, i, lr, lf, decs[1, :, at], decs[0, :, at])
        return 0

    each(WIDE, second, 0)
    end()


def grads_and_rows(
    ready, cont, cum, recv, hc, hr, dout, n16, u, dg16, dm16, cs, ylf, ylr, rows, dc, grads,
    *scratch
):
    n_t, u_t, dwo, dwg, bcv, yfv, yrv, sf, sr, doutv, nv, uv, dgv, dmv = scratch[:14]
    lsem, sem, osem = scratch[14:]
    loads = [(dout, doutv), (n16, nv), (u, uv), (dg16, dgv), (cs.at[:, E:], bcv)]
    loads = [pltpu.make_async_copy(a, b, lsem.at[k]) for k, (a, b) in enumerate(loads)]
    for copy in loads:
        copy.start()
    finish_all(loads[:2])
    wait = fetch([(ylf, yfv), (ylr, yrv), (dm16, dmv)], sem)
    n_t[...] = flip(nv[...])

    def columns_out(i, _):
        at = wide(i)
        dwo[:, at] = mm(n_t[...], doutv[:, at]).astype(BF)
        return 0

    def columns_gate(i, _):
        at = wide(i)
        dwg[:, at] = mm(u_t[...], dgv[:, at]).astype(BF)
        return 0

    each(D // 256, columns_out, 0)
    finish_all(loads[2:4])
    u_t[...] = flip(uv[HALO:, :])
    each(WIDE, columns_gate, 0)
    shards = grads.reshape(DP, 384, D)
    gate_rows = dwg.reshape(DP, 96, E)
    outward = [
        (gate_rows.at[:, :, pl.ds(0, D)], shards.at[:, pl.ds(0, 96)]),
        (gate_rows.at[:, :, pl.ds(D, D)], shards.at[:, pl.ds(96, 96)]),
        (dwo.reshape(DP, 192, D), shards.at[:, pl.ds(192, 192)]),
    ]
    outward = [pltpu.make_async_copy(a, b, osem.at[k]) for k, (a, b) in enumerate(outward)]
    for copy in outward:
        copy.start()
    ready()
    take_slices(recv, sf, sr, cont[0:1, 0:1])
    ef_f, ef_r = pairs_of(jnp.exp(cum[...]))
    finish_all(loads[4:])
    _, cf, _, cr = parts_of_bc(silu(bcv[...]))

    def tile(i, sums):
        at = wide(i)
        wait(i)
        dm = dmv[:, at].astype(F32)
        new, halves = [], []
        efs = mm_rows([ef_f, ef_r], hc[:, at])
        for ef, c, s, yl in ((efs[0], cf, sf, yfv), (efs[1], cr, sr, yrv)):
            y = yl[:, at] + ef * mm(c, s[:, at])
            halves += split2(dm * y)
            new.append(mm_nt((ef * dm).astype(BF), s[:, at]))
        a, b, c, d = mm_rows(halves, hr[at, :])
        return sums[0] + a + b, sums[1] + new[0], sums[2] + c + d, sums[3] + new[1]

    zero, zn = jnp.zeros((T, 128), F32), jnp.zeros((T, N), F32)
    rf, dcf, rr, dcr = each(WIDE, tile, (zero, zn, zero, zn))
    rows[...] = rf + to_back(rr)
    dc[...] = jnp.concatenate([dcf, dcr], axis=1)
    finish_all(outward)


def project_out(ready, tok, n16, dback, dtok, rest, out, dtok_out, wo, last, sem, dsem):
    at = pl.ds(T - HALO, HALO)
    rows_in = pltpu.make_async_copy(dtok.at[at], last, dsem.at[0])
    rows_out = pltpu.make_async_copy(last, dtok_out.at[at], dsem.at[1])
    rows_in.start()
    copies = load_rest(rest, None, wo, sem)[1]
    ready()
    rows_in.wait()
    last[...] += dback[...]
    rows_out.start()
    finish_all(copies)
    out[...] = (tok[...].astype(F32) + mm(n16[...], wo[...])).astype(BF)
    rows_out.wait()


def local_back(ready, dt, cum, dm16, hc, hr, cs, zf, zr, dgf, dgr, inner, *scratch):
    csv, zfv, zrv, col, row, gf, gr, dm_t, sem, osem = scratch
    bc = pltpu.make_async_copy(cs.at[:, E:], csv.at[:, E:], sem.at[0, 2])
    bc.start()
    wait = fetch([(cs, csv)], sem)
    ready()
    cum2 = cum[...] * LOG2E
    row[...] = cum2.T
    columns_of(cum2, col)
    dm_t[...] = flip(dm16[...])
    dt_f, dt_r = pairs_of(dt[...])
    bc.wait()
    bf, cf, br, cr = parts_of_bc(silu(csv[:, E:]))
    s, t = iota((T, T), 0), iota((T, T), 1)
    gf[...] = jnp.where(t > s, mm_nt(bf, cf), 0.0)
    gr[...] = jnp.where(t < s, mm_nt(br, cr), 0.0)
    dgf[...] = jnp.zeros((T, T), F32)
    dgr[...] = jnp.zeros((T, T), F32)

    done, end = deliver([(zfv, zf), (zrv, zr)], osem)

    def tile(i, sums):
        at = wide(i)
        wait(i)
        x = silu(csv[:, at])
        xd = [x * spread for spread in mm_rows([dt_f, dt_r], hc[:, at])]
        dws = mm_rows(by_head(xd[0]) + by_head(xd[1]), dm_t[at, :])
        all_w = []
        for forward, first, g, dg in ((True, 0, gf, dgf), (False, H, gr, dgr)):
            ws = []
            small = jnp.zeros((128, 128), F32)
            large = jnp.zeros((T, 128), F32)
            for e in range(4):
                h = first + 4 * i + e
                at_s, along = col[h], row[h : h + 1, :]
                dw = dws[e if forward else 4 + e]
                if forward:
                    ea = jnp.exp2(jnp.minimum(along[:, :128] - at_s[:128], 0.0))
                    eb = jnp.exp2(jnp.minimum(along[:, 128:] - at_s, 0.0))
                    ws.append(
                        up_full((ea * g[:128, :128]).astype(BF), (eb * g[:, 128:]).astype(BF))
                    )
                    small = small + ea * dw[:128, :128]
                    large = large + eb * dw[:, 128:]
                else:
                    ea = jnp.exp2(jnp.minimum(along[:, :128] - at_s, 0.0))
                    eb = jnp.exp2(jnp.minimum(along[:, 128:] - at_s[128:], 0.0))
                    ws.append(
                        low_full((ea * g[:, :128]).astype(BF), (eb * g[128:, 128:]).astype(BF))
                    )
                    large = large + ea * dw[:, :128]
                    small = small + eb * dw[128:, 128:]
            all_w.append(jnp.concatenate(ws, axis=1))
            if forward:
                dg[:128, :128] += small
                dg[:, 128:] += large
            else:
                dg[:, :128] += large
                dg[128:, 128:] += small
        totals = mm_rows(all_w, jnp.concatenate(by_head(dm16[:, at].astype(F32)), axis=0))
        zfv[:, at], zrv[:, at] = totals[0].astype(BF), totals[1].astype(BF)
        halves = [t for k in range(2) for t in split2(xd[k].astype(BF).astype(F32) * totals[k])]
        done(i)
        a, b, c, d = mm_rows(halves, hr[at, :])
        return sums[0] + a + b, sums[1] + c + d

    zero = jnp.zeros((T, 128), F32)
    sums = each(WIDE, tile, (zero, zero))
    inner[...] = sums[0] + to_back(sums[1])
    dgf[...] = jnp.where(t > s, dgf[...], 0.0)
    dgr[...] = jnp.where(t < s, dgr[...], 0.0)
    end()


def inner_back(
    ready, cont, halo, gin, cw, alog, dsk, sraw, dt, cum, back, fore, rows, inner, dc, dgout, hc, hr,
    dgf, dgr, tok, dout, cs, zf, zr, dm16, ci, dg16, rest, *refs
):
    parts, (dtok, dhalo, dall_out, small_out), scratch = refs[:8], refs[8:12], refs[12:]
    csv, zfv, zrv, dmv, civ, dgv, w, wg, sf, sr, kf, kr, dcs, cif, du, small = scratch[:16]
    line, dall, gfv, grv, tokv, doutv, sem, csem, wsem, gsem, osem = scratch[16:]
    first = [(cs.at[:, E:], csv.at[:, E:])]
    bcc = pltpu.make_async_copy(*first[0], csem.at[0])
    bcc.start()
    wait = fetch([(cs, csv), (zf, zfv), (zr, zrv), (dm16, dmv)], sem)
    later = [(dgf, gfv), (dgr, grv), (ci, civ), (dg16, dgv), (tok, tokv), (dout, doutv)]
    later = [pltpu.make_async_copy(a, b, csem.at[1 + k]) for k, (a, b) in enumerate(later)]
    ready()
    keep = cont[0:1, 0:1]
    take_slices(back, kr, kf, keep)
    take_slices(fore, sf, sr, keep)
    cumv, dtv = cum[...], dt[...]
    last = ends(cumv)
    te_f, te_r = pairs_of(jnp.exp(last - cumv))
    dt_f, dt_r = pairs_of(dtv)
    line[...] = jnp.zeros((8, E), F32)
    dcs[:, 0:HALO] = jnp.zeros((C // 128, HALO, 128), F32)
    dcs[:, HALO + T :] = jnp.zeros((C // 128, 16, 128), F32)
    bcc.wait()
    bc = csv[:, E:]
    bf, cf, br, cr = parts_of_bc(silu(bc))

    def weights():
        gates = load_rest(rest, wg, None, gsem, False)[0]
        return load_weights(parts, w, wsem, False) + gates

    def slope(v, sg):
        return sg * (1.0 + v * (1.0 - sg))

    def tile(i, sums):
        at = wide(i)

        if i in (1, 3):
            for copy in later if i == 1 else weights():
                copy.start()

        wait(i)
        v = csv[:, at]
        sg = sigmoid(v)
        x = v * sg
        dm = dmv[:, at].astype(F32)
        line[2:3, at] = jnp.sum(dm * x, axis=0, keepdims=True)
        dx = dsk[:, at] * dm
        new, ends_of = [], []
        for d, dt2, te2, z, k, s, b in (
            (0, dt_f, te_f, zfv, kf, sf, bf),
            (1, dt_r, te_r, zrv, kr, sr, br),
        ):
            dts, te = mm(dt2, hc[:, at]), mm(te2, hc[:, at])
            xd = (x * dts).astype(BF).astype(F32)
            zt = te * mm(b, k[:, at])
            dx = dx + dts * (z[:, at].astype(F32) + zt)
            ends_of.append((xd * zt).astype(BF))
            new.append(mm_nt((te * xd).astype(BF), k[:, at]))
            both = s[:, at].astype(F32) * k[:, at].astype(F32)
            line[d : d + 1, at] = jnp.sum(both, axis=0, keepdims=True)
        dx = dx * slope(v, sg)
        for e in range(2):
            dcs[2 * i + e, HALO : HALO + T] = dx[:, 128 * e : 128 * e + 128]
        tf, tr = mm_rows(ends_of, hr[at, :])
        return sums[0] + tf, sums[1] + new[0], sums[2] + tr, sums[3] + new[1]

    zero, zn = jnp.zeros((T, 128), F32), jnp.zeros((T, N), F32)
    sums = each(WIDE, tile, (zero, zn, zero, zn))
    tails = sums[0] + to_back(sums[2])
    finish_all(later)
    gf16, gr16 = gfv[...].astype(BF), grv[...].astype(BF)
    dbf = sums[1] + mm(gf16, cf)
    dbr = sums[3] + mm(gr16, cr)
    dcf = dc[:, :N] + mm(flip(gf16), bf)
    dcr = dc[:, N:] + mm(flip(gr16), br)
    dbc = jnp.concatenate([dbf, dcf, dbr, dcr], axis=1) * slope(bc, sigmoid(bc))
    for e in range(2):
        dcs[2 * WIDE + e, HALO : HALO + T] = dbc[:, 128 * e : 128 * e + 128]
    hi, lo = split2(line[...])
    heads = mm(hi, hr[...]) + mm(lo, hr[...])
    dots = heads[0:1] + to_back(heads)[1:2]
    rate = jnp.where(lanes(1) < 2 * H, jnp.exp(alog[...]), 0.0)
    v = rows[...] - inner[...]
    dla = jnp.where(
        lanes() < H,
        tri_sum(tri(lambda r, c: r <= c), v) + tri_sum(tri(lambda r, c: r > c), tails),
        tri_sum(tri(lambda r, c: r >= c), v) + tri_sum(tri(lambda r, c: r < c), tails),
    ) + jnp.exp(last) * dots
    sg = sigmoid(sraw[...])
    ratio = jnp.where(dtv > 1e-20, sg / jnp.maximum(dtv, 1e-20), 1.0)
    dstep = (inner[...] + tails) * ratio - dla * rate * sg
    dstep = jnp.where(lanes() < 2 * H, dstep, 0.0)
    dall[0:HALO, C:] = jnp.zeros((HALO, 128), BF)
    dall[HALO:, C:] = dstep.astype(BF)
    dal = jnp.broadcast_to(jnp.sum(dla * (-dtv * rate), axis=0, keepdims=True), (8, 128))
    small[...] = jnp.zeros((96, 128), F32)
    small[88:89] = jnp.sum(dstep, axis=0, keepdims=True)
    small[89:90] = jnp.where(lanes(1) < H, dal[0:1] + to_front(dal)[0:1], 0.0)
    small[90:91] = jnp.where(lanes(1) < H, heads[2:3], 0.0)
    mask = jnp.where(iota((HALO + T, 1), 0) < HALO, keep, 1.0)

    half_out = [
        pltpu.make_async_copy(dall.at[:, at], dall_out.at[:, at], osem.at[k])
        for k, at in enumerate((pl.ds(0, 1024), pl.ds(1024, CD - 1024)))
    ]

    def convolution(i, _):
        at = pl.ds(128 * i, 128)
        g = dcs[i, HALO : HALO + T]
        cif[...] = civ[:, at].astype(F32)
        small[56 + i : 57 + i] = jnp.sum(g, axis=0, keepdims=True)
        total = jnp.zeros((HALO + T, 128), F32)
        for k in range(4):
            shifted = cif[HALO - 3 + k : HALO - 3 + k + T]
            small[14 * k + i : 14 * k + i + 1] = jnp.sum(g * shifted, axis=0, keepdims=True)
            total = total + cw[k : k + 1, at] * dcs[i, 3 - k : 3 - k + HALO + T]
        dall[:, at] = (total * mask).astype(BF)
        if i == 7:
            half_out[0].start()
        return 0

    each(C // 128, convolution, 0)
    half_out[1].start()
    for j in range(E // 128):
        small[70 + j : 71 + j] = dgout[:, 128 * j : 128 * j + 128]
    finish_all(weights())

    def input_grad(i, _):
        at = wide(i)
        du[:, at] = mm_nt(dall[...], w[at, :])
        du[HALO:, at] += mm_nt(dgv[:, :D], wg[0, at, :]) + mm_nt(dgv[:, D:], wg[1, at, :])
        return 0

    each(D // 256, input_grad, 0)
    x = jnp.concatenate([halo[...], tokv[...]], axis=0).astype(F32)
    r = lax.rsqrt(jnp.mean(x * x, axis=1, keepdims=True) + EPS)
    duxr = jnp.sum(du[...] * x * r, axis=0, keepdims=True)
    for j in range(6):
        small[82 + j : 83 + j] = duxr[:, 128 * j : 128 * j + 128]
    small_out[...] = small[...].astype(BF)
    dxh = du[...] * gin[...]
    dx = r * dxh - x * (r * r * r * jnp.mean(dxh * x, axis=1, keepdims=True))
    dhalo[...] = dx[:HALO]
    dtok[...] = doutv[...].astype(F32) + dx[HALO:]
    finish_all(half_out)


def weight_back(to_other, u, dall, small, out, u_t):
    y, core, _ = place()
    u_t[...] = flip(u[...])
    core = 1 - core if to_other else core
    shards = [2 * lax.rem(y + k, 4) + core for k in range(4)]
    rows = [u_t[pl.ds(pl.multiple_of(shard * 96, 32), 96), :] for shard in shards]
    parts = mm_rows(rows, dall[...])
    for k in range(4):
        out[k, :, :CD] = parts[k].astype(BF)
        out[k, :, CD:] = small[...]


def add_pairs(a, b, whole, one, three, mine, other):
    for k, out in ((0, whole), (1, one), (3, three)):

        def rows(i, _, k=k, out=out):
            at = pl.ds(pl.multiple_of(i * 48, 16), 48)
            out[at] = (a[k, at].astype(F32) + b[k, at].astype(F32)).astype(BF)
            return 0

        lax.fori_loop(0, 2, rows, 0)
    _, _, parity = place()
    for out, half in ((mine, parity), (other, 1 - parity)):
        at = pl.ds(pl.multiple_of(half * 1024, 1024), 1024)
        out[...] = (a[2, :, at].astype(F32) + b[2, :, at].astype(F32)).astype(BF)


def add_two(a, b, out):
    out[...] = (a[...].astype(F32) + b[...].astype(F32)).astype(BF)


def add_y(rest, whole, one, three, half, out):
    _, _, parity = place()
    for j in range(6):
        for r in range(0, 384, 48):
            row = 384 * j + r
            out[row // 144, row % 144 : row % 144 + 48] = rest[
                r : r + 48, 128 * j : 128 * j + 128
            ]
    for j in range(SEQ):
        at, in_half = slice(128 * j, 128 * j + 128), slice(128 * (j % 8), 128 * (j % 8) + 128)
        mine = jnp.where(parity == j // 8, 1.0, 0.0)
        total = sum(part[:, at].astype(F32) for part in (whole, one, three))
        out[j, 144:] = (total + half[:, in_half].astype(F32) * mine).astype(BF)


def add_blocks(recv, out):
    total = recv[0].astype(F32)
    for i in range(1, SEQ):
        total = total + recv[i].astype(F32)
    low = total.astype(BF)
    for i in range(SEQ):
        out[i] = low


def finish(sums, dwin, dwdt, dwout, dcw, dcb, dgout, dgin, ddtb, dal, ddsk):
    def put(ref, at, start, rows):
        for r in range(0, rows, 48):
            j, k = (start + r) // 144, (start + r) % 144
            ref[r : r + 48, at] = sums[j, k : k + 48].astype(F32)

    for j in range(6):
        at = slice(128 * j, 128 * j + 128)
        put(dwin, at, 384 * j, 96)
        put(dwin, slice(D + 128 * j, D + 128 * j + 128), 384 * j + 96, 96)
        put(dwout, at, 384 * j + 192, 192)
    for j in range(14):
        dwin[:, E + 128 * j : E + 128 * j + 128] = sums[j, 144:].astype(F32)
    dwdt[...] = sums[14, 144:].astype(F32).T[: 2 * H]
    small = sums[15, 144:].astype(F32)
    for j in range(14):
        at = slice(128 * j, 128 * j + 128)
        for k in range(4):
            dcw[k : k + 1, at] = small[14 * k + j : 14 * k + j + 1]
        dcb[at] = small[56 + j]
    for j in range(E // 128):
        dgout[128 * j : 128 * j + 128] = small[70 + j]
    for j in range(6):
        dgin[128 * j : 128 * j + 128] = small[82 + j]
    ddtb[...] = small[88, 0 : 2 * H]
    dal[...] = small[89, 0:H]
    ddsk[...] = small[90, 0:H]


V = pl.BlockSpec(memory_space=pltpu.VMEM)
ANY = pl.BlockSpec(memory_space=pl.ANY)


def shape(*dims, dtype=F32):
    return jax.ShapeDtypeStruct(dims, dtype)


def nothing():
    pass


def staged(kernel, ins, outs, scratch):
    held = [i for i, (spec, _) in enumerate(ins) if spec is V]
    more = [pltpu.VMEM(ins[i][1].shape, ins[i][1].dtype) for i in held]
    more.append(pltpu.SemaphoreType.DMA((len(held),)))

    def run(*refs):
        refs = list(refs)
        buffers, sem = refs[len(refs) - len(more) : -1], refs[-1]
        copies = []
        for k, i in enumerate(held):
            copies.append(pltpu.make_async_copy(refs[i], buffers[k], sem.at[k]))
            copies[-1].start()
            refs[i] = buffers[k]
        kernel(lambda: finish_all(copies), *refs[: len(refs) - len(more)])

    return run, [(ANY, a) for _, a in ins], list(scratch) + more


def call(kernel, name, ins, outs, scratch=(), flops=0, apart=(), limit=VMEM, stage=False, alias=None):
    if stage:
        kernel, ins, scratch = staged(kernel, ins, outs, scratch)
    specs, args = zip(*ins)
    moved = sum(a.size * a.dtype.itemsize for a in args)
    moved += sum(o.size * o.dtype.itemsize for o in outs)
    return pl.pallas_call(
        kernel,
        name=name,
        out_shape=tuple(outs),
        in_specs=list(specs),
        out_specs=tuple(ANY if i in apart else V for i in range(len(outs))),
        scratch_shapes=list(scratch),
        input_output_aliases=alias or {},
        cost_estimate=pl.CostEstimate(flops=flops, bytes_accessed=moved, transcendentals=0),
        compiler_params=pltpu.CompilerParams(vmem_limit_bytes=limit),
    )(*args)


def vm(*dims, dtype=F32):
    return pltpu.VMEM(dims, dtype)


def shift_y(k):
    return [(2 * y + c, 2 * ((y + k) % 4) + c) for y in range(4) for c in range(2)]


SWAP = [(i, i ^ 1) for i in range(DP)]
NEXT_Z = [(i, i ^ 1) for i in range(SEQ)]


def exchange(value):
    return lax.all_to_all(value, "seq", 0, 0, tiled=True)


def together(*values):
    return lax.optimization_barrier(values)


def local(
    tokens, starts, g_in, w_in, w_dt, conv_w, conv_b, dt_bias, a_log, dskip, g_out, w_out, d_out
):
    tok, dout = tokens[0], d_out[0]
    cont = jnp.broadcast_to((1 - starts).astype(F32), (1, 128))

    row = lambda v: v.reshape(1, -1)
    pad = lambda v: jnp.pad(v, (0, 128 - v.shape[0])).reshape(1, 128)
    alog = pad(jnp.concatenate([a_log, a_log]))
    dsk = row(jnp.repeat(dskip, N))
    gin, gout, cb, dtb = row(g_in), row(g_out), row(conv_b), pad(dt_bias)
    own = jnp.concatenate([w_in[:, E:], jnp.pad(w_dt, ((0, 0), (0, 128 - 2 * H)))], axis=1)
    column = [lax.ppermute(own, "dp", shift_y(k)) for k in (1, 2, 3)]
    halo = lax.ppermute(tok[-HALO:], "seq", [(i, i + 1) for i in range(SEQ - 1)])
    beside = lax.ppermute(own, "dp", SWAP)
    rest_own = jnp.concatenate([w_in[:, :D], w_in[:, D:E], w_out], axis=0)
    hc, hr = marks()
    column[0], halo, beside, alog, dsk, gin, gout, cb, dtb, cont, hc, hr = together(
        column[0], halo, beside, alog, dsk, gin, gout, cb, dtb, cont, hc, hr
    )
    parts = [own, *column, beside] + [lax.ppermute(part, "dp", SWAP) for part in column]
    rest_own = together(rest_own, *column)[0]
    rest = lax.all_gather(rest_own, "dp", axis=0, tiled=True)

    part_ins = [(ANY, part) for part in parts]
    w_scratch = vm(D, CD, dtype=BF)
    dma = pltpu.SemaphoreType.DMA
    full, half, state = vm(T, E), vm(T, E, dtype=BF), vm(N, E, dtype=BF)

    u, ci, cs, sraw, dt, cum, pay = call(
        front,
        "front",
        [(V, cont), (V, tok), (V, halo), (V, gin), (V, conv_w), (V, cb)]
        + [(V, dtb), (V, alog), (V, hc)]
        + part_ins,
        [shape(HALO + T, D, dtype=BF), shape(HALO + T, C, dtype=BF), shape(T, C)]
        + [shape(T, 128)] * 3
        + [shape(SEQ, 48, 384, dtype=BF)],
        [w_scratch, vm(2, HALO + T, 128), vm(T, C), vm(HALO + T, C, dtype=BF)]
        + [vm(HALO + T, D, dtype=BF), dma((8,)), dma((2, 3)), dma(())],
        flops=2 * T * D * CD,
        apart=(0, 1, 2),
        stage=True,
    )

    def scan(got, name):
        out = shape(SEQ, 32, 384, dtype=BF)
        return call(scan_blocks, name, [(V, got)], [out], limit=SMALL)[0]

    got = exchange(pay)
    ylf, ylr, base = call(
        local_mix,
        "local_mix",
        [(V, dt), (V, cum), (V, dsk), (V, hc), (ANY, cs)],
        [shape(T, E)] * 3,
        [vm(T, C), full, full, full, vm(2 * H, T, 128), vm(128, T), vm(T, T), vm(T, T)]
        + [dma(()), dma((1, 2)), dma((3, 2))],
        flops=4 * 24 * T * T * 256,
        apart=(0, 1, 2),
    )
    got, ylr, base = together(got, ylr, base)
    fore = exchange(scan(got, "scan_states"))
    gate, dn = call(
        gate_products,
        "gate_products",
        [(V, u), (V, dout), (ANY, rest)],
        [shape(T, E, dtype=BF)] * 2,
        [vm(2, D, D, dtype=BF), vm(E, D, dtype=BF), half, half, dma((3,)), dma((4,))],
        flops=4 * T * D * E,
        apart=(0, 1),
    )
    n16, dg16, dm16, dgout, pay_back = call(
        gated_norm,
        "gated_norm",
        [(V, cont), (V, cum), (V, fore), (V, gout), (V, hc)]
        + [(ANY, a) for a in (cs, base, gate, dn)],
        [shape(T, E, dtype=BF)] * 3 + [shape(1, E), shape(SEQ, 48, 384, dtype=BF)],
        [vm(T, 256), full, half, half] + [full] * 4 + [vm(2, 16, E)] + [half] * 3 + [state] * 2
        + [dma(()), dma((3, 2)), dma((3, 2))],
        flops=12 * T * N * E,
        apart=(0, 1, 2),
        stage=True,
    )
    got = exchange(pay_back)
    rows, dc, rest_grads = call(
        grads_and_rows,
        "grads_and_rows",
        [(V, cont)]
        + [(V, a) for a in (cum, fore, hc, hr)]
        + [(ANY, a) for a in (dout, n16, u, dg16, dm16, cs, ylf, ylr)],
        [shape(T, 128), shape(T, 128), shape(DP * 384, D, dtype=BF)],
        [vm(E, T, dtype=BF), vm(D, T, dtype=BF), vm(E, D, dtype=BF), vm(D, E, dtype=BF)]
        + [vm(T, 256), full, full, state, state, vm(T, D, dtype=BF), half]
        + [vm(HALO + T, D, dtype=BF), half, half]
        + [dma((5,)), dma((3, 2)), dma((3,))],
        flops=8 * T * D * E,
        apart=(2,),
        stage=True,
    )
    got, rows, rest_grads = together(got, rows, rest_grads)
    rest_sum = lax.psum_scatter(rest_grads, "dp", scatter_dimension=0, tiled=True)
    back = exchange(scan(got, "scan_adjoints"))
    zf, zr, dgf, dgr, inner = call(
        partial(local_back, nothing),
        "local_back",
        [(V, dt), (V, cum), (V, dm16), (V, hc), (V, hr), (ANY, cs)],
        [shape(T, E, dtype=BF)] * 2 + [shape(T, T)] * 2 + [shape(T, 128)],
        [vm(T, C), half, half, vm(2 * H, T, 128), vm(128, T), vm(T, T), vm(T, T)]
        + [vm(E, T, dtype=BF), dma((1, 3)), dma((2, 2))],
        flops=4 * 48 * T * T * 256,
        apart=(0, 1),
    )
    dtok, dhalo, dall, small = call(
        partial(inner_back, nothing),
        "inner_back",
        [(V, cont)]
        + [(V, a) for a in (halo, gin, conv_w, alog, dsk, sraw, dt, cum, back, fore, rows)]
        + [(V, a) for a in (inner, dc, dgout, hc, hr)]
        + [(ANY, a) for a in (dgf, dgr, tok, dout, cs, zf, zr, dm16, ci, dg16, rest)]
        + part_ins,
        [shape(T, D), shape(HALO, D), shape(HALO + T, CD, dtype=BF), shape(96, 128, dtype=BF)],
        [vm(T, C), half, half, half, vm(HALO + T, C, dtype=BF), half, w_scratch]
        + [vm(2, D, D, dtype=BF)]
        + [state] * 4
        + [vm(C // 128, HALO + T + 16, 128), vm(HALO + T, 128), vm(HALO + T, D), vm(96, 128)]
        + [vm(8, E), vm(HALO + T, CD, dtype=BF), vm(T, T), vm(T, T)]
        + [vm(T, D, dtype=BF), vm(T, D, dtype=BF)]
        + [dma((4, 2)), dma((7,)), dma((8,)), dma((3,)), dma((2,))],
        flops=2 * T * D * (CD + E),
        apart=(2,),
    )
    def grads_for(to_other, name):
        return call(
            partial(weight_back, to_other),
            name,
            [(V, u), (V, dall), (V, small)],
            [shape(4, 96, 2048, dtype=BF)],
            [vm(D, HALO + T, dtype=BF)],
            flops=T * D * CD,
            limit=16 * 1024 * 1024,
        )[0]

    send = grads_for(True, "grads_to_other_core")
    send, u, dall, small, dhalo = together(send, u, dall, small, dhalo)
    recv = lax.ppermute(send, "dp", SWAP)
    keep = grads_for(False, "grads_to_this_core")
    whole, one, three, mine, other = call(
        add_pairs,
        "add_tail_cores",
        [(V, keep), (V, recv)],
        [shape(96, 2048, dtype=BF)] * 3 + [shape(96, 1024, dtype=BF)] * 2,
        limit=SMALL,
    )
    other = lax.ppermute(other, "seq", NEXT_Z)
    one, three = lax.ppermute(one, "dp", shift_y(1)), lax.ppermute(three, "dp", shift_y(3))
    sides = [(V, mine), (V, other)]
    half = call(add_two, "add_tail_z", sides, [shape(96, 1024, dtype=BF)], limit=SMALL)[0]
    half, n16 = together(half, n16)
    half = lax.ppermute(half, "dp", shift_y(2))
    dback = lax.ppermute(dhalo, "seq", [(i + 1, i) for i in range(SEQ - 1)])
    out, dtok = call(
        project_out,
        "project_out",
        [(V, tok), (V, n16), (V, dback), (ANY, dtok), (ANY, rest)],
        [shape(T, D, dtype=BF), shape(T, D)],
        [vm(E, D, dtype=BF), vm(HALO, D), dma((3,)), dma((2,))],
        flops=2 * T * D * E,
        apart=(1,),
        stage=True,
        alias={3: 1},
    )
    one, three, half, out, dtok = together(one, three, half, out, dtok)
    slices = shape(SEQ, 240, 128, dtype=BF)
    sums = [(V, part) for part in (rest_sum, whole, one, three, half)]
    sums = call(add_y, "add_y", sums, [slices], limit=SMALL)[0]
    sums = call(add_blocks, "add_seq", [(V, exchange(sums))], [slices], limit=SMALL)[0]
    dwin, dwdt, dwout, dcw, dcb, dgo, dgi, ddtb, dal, dds = call(
        finish,
        "finish",
        [(V, exchange(sums))],
        [shape(96, E + C), shape(2 * H, 96), shape(192, D), shape(4, C), shape(C)]
        + [shape(E), shape(D), shape(2 * H), shape(H), shape(H)],
        limit=SMALL,
    )
    return (
        out[None], dtok[None], dgi, dwin, dwdt.T, dcw, dcb, ddtb, dal, dds, dgo, dwout,
    )


def solution(mesh):
    split = P("dp", "seq", None)
    rows = P("dp", None)
    return jax.shard_map(
        local,
        mesh=mesh,
        in_specs=(split, P("dp", "seq"), P(), rows, rows, P(), P(), P(), P(), P(), P(), rows, split),
        out_specs=(split, split, P(), rows, rows, P(), P(), P(), P(), P(), P(), rows),
        check_vma=False,
    )
```
